32 devices in a mesh: dp: 8 (over y, x, core), ctx: 4 (over z).
Axes of the slice: x: 2, y: 2, z: 4, core: 2. Of those that a mesh axis runs over, the one named last changes fastest.
Arguments:
- layer_input: bfloat16 [8192, 1024], P(('dp', 'ctx')), may hold values from -6 to 6
- out_cotangent: bfloat16 [8192, 1024], P(('dp', 'ctx')), may hold values from -6 to 6
- params: float32 [2, 4, 24576, 128], P(None, 'ctx', 'dp')
- vectors: float32 [2, 12288], P(None, ('dp', 'ctx')), may hold values from -1.2 to 1.6, as said below
- param_moment: float32 [2, 4, 24576, 128], P(None, 'ctx', 'dp'), may hold values from -6 to 6
- vector_moment: float32 [2, 12288], P(None, ('dp', 'ctx')), may hold values from -6 to 6
- param_square: float32 [2, 4, 24576, 128], P(None, 'ctx', 'dp'), may hold values from 1 to 100
- vector_square: float32 [2, 12288], P(None, ('dp', 'ctx')), may hold values from 1 to 100
Outputs:
- layer_output: bfloat16 [8192, 1024], P(('dp', 'ctx'))
- input_grad: float32 [8192, 1024], P(('dp', 'ctx'))
- param_grad: float32 [2, 4, 24576, 128], P(None, 'ctx', 'dp')
- vector_grad: float32 [2, 12288], P(None, ('dp', 'ctx'))
- param_moment_next: float32 [2, 4, 24576, 128], P(None, 'ctx', 'dp')
- vector_moment_next: float32 [2, 12288], P(None, ('dp', 'ctx'))
- param_square_next: float32 [2, 4, 24576, 128], P(None, 'ctx', 'dp')
- vector_square_next: float32 [2, 12288], P(None, ('dp', 'ctx'))
- param_update: float32 [2, 4, 24576, 128], P(None, 'ctx', 'dp')
- vector_update: float32 [2, 12288], P(None, ('dp', 'ctx'))
The draws below stay inside these ranges and needn't reach their ends.
Inputs may be any that keep to these rules, and one draw needn't show every extreme that they name: Rows 0 and 5 of each block's vectors are norm gains between 0.4 and 1.6; the others are biases.
All inputs are finite; a program needn't handle non-finite values.
Results may differ from the reference program's by a relative error of at most 0.015.
Values may be sent and summed in bfloat16 or wider, within the bound.
A program may use at most 256 MiB of HBM per device.

```python
import math
import jax
import jax.numpy as jnp
from jax import lax

D = 1024
HEADS = 16
HEAD = 64
FF = 4096
LAYERS = 2
STEP = 10
SEQ_LEN = 1024
SEQS = 8
TOKENS = 8192
SLAB_ROWS = 24576
N_CTX = 4


def draw_params(key, part):
    key = jax.random.fold_in(key, 11)
    shape = (LAYERS, N_CTX, SLAB_ROWS, 128)
    base = jnp.clip(jax.random.normal(key, shape, jnp.float32), -6.0, 6.0)
    place = lax.broadcasted_iota(jnp.int32, shape, 2) * 128 + lax.broadcasted_iota(jnp.int32, shape, 3)
    first = 3 * D * D // N_CTX
    second = first + D * D // N_CTX
    third = second + D * FF // N_CTX
    scale = jnp.where(place < first, D ** (-0.5), jnp.where(place < second, (D // 8) ** (-0.5), jnp.where(place < third, D ** (-0.5), FF ** (-0.5))))
    return base * scale


def draw_vectors(key, part):
    key = jax.random.fold_in(key, 23)
    shape = (LAYERS, 12 * D)
    base = jnp.clip(jax.random.normal(key, shape, jnp.float32), -4.0, 4.0) * 0.3
    row_index = lax.broadcasted_iota(jnp.int32, shape, 1) // D
    gains = (row_index == 0) | (row_index == 5)
    return jnp.where(gains, 1.0 + 0.5 * base, base)


def block_scale(key, shape, pieces, smallest, top_value):
    def one(axis_at, blocks):
        steps = jax.random.uniform(jax.random.fold_in(jax.random.fold_in(key, 6), axis_at), (blocks,), jnp.float32, smallest / len(pieces), top_value / len(pieces))
        return jnp.repeat(jnp.exp(steps), shape[axis_at] // blocks).reshape((-1,) + (1,) * (len(shape) - axis_at - 1))

    factor_of = one(*pieces[0])
    for cut in pieces[1:]:
        factor_of = factor_of * one(*cut)
    return factor_of


def noise(stream_key, extent, width, most, cuts=(), dtype=jnp.bfloat16):
    values = jax.random.normal(stream_key, extent, jnp.float32) * width
    if len(cuts) > 0:
        values = block_scale(stream_key, extent, cuts, -0.22, 0.18) * values
    return jnp.clip(values, min=-most, max=most).astype(dtype)


def setup_inputs(seed: int = 0) -> dict:
    arg_keys = jax.random.split(jax.random.key(seed), 9)
    return {
        "layer_input": noise(arg_keys[0], (TOKENS, D), 1.0, 6.0, ((0, 32),)),
        "out_cotangent": noise(arg_keys[1], (TOKENS, D), 1.0, 6.0, ((0, 32),)),
        "params": draw_params(jax.random.fold_in(arg_keys[8], 71), 0),
        "vectors": draw_vectors(jax.random.fold_in(arg_keys[8], 71), 0),
        "param_moment": noise(arg_keys[4], (LAYERS, N_CTX, SLAB_ROWS, 128), 1.0, 6.0, ((1, 4), (2, 8)), jnp.float32),
        "vector_moment": noise(arg_keys[5], (LAYERS, 12 * D), 1.0, 6.0, ((1, 32),), jnp.float32),
        "param_square": jnp.clip(jnp.exp(math.log(100.0) - 4.6051702 * jax.random.uniform(arg_keys[6], (LAYERS, N_CTX, SLAB_ROWS, 128), jnp.float32) ** block_scale(arg_keys[6], (LAYERS, N_CTX, SLAB_ROWS, 128), ((1, 4), (2, 8)), -0.2, 0.2)), 1.0, 100.0),
        "vector_square": jnp.clip(jnp.exp(math.log(100.0) - 4.6051702 * jax.random.uniform(arg_keys[7], (LAYERS, 12 * D), jnp.float32) ** block_scale(arg_keys[7], (LAYERS, 12 * D), ((1, 32),), -0.2, 0.2)), 1.0, 100.0),
    }


@jax.custom_vjp
def low(v):
    return lax.optimization_barrier(v.astype(jnp.bfloat16)).astype(jnp.float32)

@jax.custom_vjp
def low_back(v):
    return v

def low_keep(v):
    return (low(v), None)

def low_pass(kept, grad):
    return (grad,)

def back_keep(v):
    return (v, None)

def back_low(kept, grad):
    return (low(grad),)
low.defvjp(low_keep, low_pass)
low_back.defvjp(back_keep, back_low)
HIGHEST = lax.Precision.HIGHEST
norm_eps = 1e-05
beta_one = 0.9
beta_two = 0.999
rate = 0.01
decay = 0.1
adam_eps = 1e-08

def unpack(slabs):
    count = slabs.shape[0]
    flat = slabs.reshape(count, -1)
    first = 3 * D * D // count
    second = first + D * D // count
    third = second + D * FF // count

    def join(block, rows, cols):
        return block.reshape(count, rows, cols // count).transpose(1, 0, 2).reshape(rows, cols)
    return (join(flat[:, :first], D, 3 * D), join(flat[:, first:second], D, D), join(flat[:, second:third], D, FF), join(flat[:, third:], FF, D))

def layer_norm(values, gain, shift):
    center = values - lax.optimization_barrier(jnp.mean(values, axis=-1, keepdims=True))
    spread = lax.optimization_barrier(jnp.mean(center * center, axis=-1, keepdims=True))
    return center * lax.rsqrt(spread + norm_eps) * gain + shift

def gelu_tanh(values):
    return 0.5 * values * (1.0 + jnp.tanh(0.7978845608028654 * (values + 0.044715 * values * values * values)))

def attend_block(queries, keys, values, start):
    raw = jnp.einsum('thd,shd->hts', queries, keys, precision=HIGHEST)
    scores = low_back(raw) * 0.125
    rows = queries.shape[0]
    qpos = start + lax.broadcasted_iota(jnp.int32, (rows, keys.shape[0]), 0)
    kpos = lax.broadcasted_iota(jnp.int32, (rows, keys.shape[0]), 1)
    scores = jnp.where((kpos <= qpos)[None], scores, -1000000000.0)
    top = lax.optimization_barrier(jnp.max(scores, axis=-1, keepdims=True))
    expo = jnp.exp(scores - top)
    probs = low(expo / lax.optimization_barrier(jnp.sum(expo, axis=-1, keepdims=True)))
    mixed = jnp.einsum('hts,shd->thd', probs, values, precision=HIGHEST)
    return low(low_back(mixed))

def attend_sequence(triple):
    queries, keys, values = triple
    block = min(512, SEQ_LEN)
    number = SEQ_LEN // block
    blocks = queries.reshape(number, block, HEADS, HEAD)
    starts = (jnp.arange(number) * block).astype(jnp.int32)
    runner = jax.checkpoint(attend_block)
    result = lax.map(lambda pair: runner(pair[0], keys, values, pair[1]), (blocks, starts))
    return result.reshape(SEQ_LEN, HEADS, HEAD)

def one_layer(resid, attend_w, output_w, expand_w, reduce_w, vec):
    normed1 = low(layer_norm(resid, vec[0], vec[1]))
    mixed = low_back(jnp.dot(normed1, attend_w, precision=HIGHEST))
    queries = low(mixed[:, :D] + vec[2])
    keys = low(mixed[:, D:2 * D])
    values = low(mixed[:, 2 * D:] + vec[3])
    shape4 = (SEQS, SEQ_LEN, HEADS, HEAD)
    attended = lax.map(attend_sequence, (queries.reshape(shape4), keys.reshape(shape4), values.reshape(shape4)))
    attended = attended.reshape(TOKENS, D)
    hidden = resid + low_back(jnp.dot(attended, output_w, precision=HIGHEST)) + vec[4]
    normed2 = low(layer_norm(hidden, vec[5], vec[6]))
    upper = low_back(jnp.dot(normed2, expand_w, precision=HIGHEST)) + vec[7:11].reshape(FF)
    active = low(gelu_tanh(upper))
    return hidden + low_back(jnp.dot(active, reduce_w, precision=HIGHEST)) + vec[11]

def forward(inputs, params_all, vector_all):
    resid = inputs
    for layer_id in range(LAYERS):
        attend_w, output_w, expand_w, reduce_w = unpack(low(params_all[layer_id]))
        vec = low(vector_all[layer_id]).reshape(12, D)
        resid = one_layer(resid, attend_w, output_w, expand_w, reduce_w, vec)
    return resid

def adam_step(grad, moment, square, master, weight_decay):
    moment_next = beta_one * moment + (1.0 - beta_one) * grad
    square_next = beta_two * square + (1.0 - beta_two) * grad * grad
    corrected = moment_next / (1.0 - beta_one ** STEP)
    scaled = square_next / (1.0 - beta_two ** STEP)
    update = -rate * (corrected / (jnp.sqrt(scaled) + adam_eps) + weight_decay * master)
    return (moment_next, square_next, update)

def reference(layer_input, out_cotangent, params, vectors, param_moment, vector_moment, param_square, vector_square):
    inputs = layer_input.astype(jnp.float32)
    result, pull = jax.vjp(forward, inputs, params, vectors)
    input_grad, param_grad, vector_grad = pull(out_cotangent.astype(jnp.float32))
    param_step = adam_step(param_grad, param_moment, param_square, params, decay)
    vector_step = adam_step(vector_grad, vector_moment, vector_square, vectors, 0.0)
    return (result.astype(jnp.bfloat16), input_grad, param_grad, vector_grad, param_step[0], vector_step[0], param_step[1], vector_step[1], param_step[2], vector_step[2])
```

```python
import functools

import jax
import jax.numpy as jnp
from jax import lax
from jax.experimental import pallas as pl
from jax.experimental.pallas import tpu as pltpu
from jax.sharding import PartitionSpec as P

D = 1024
HEADS = 16
HEAD = 64
FF = 4096
LAYERS = 2
STEP = 10
BF = jnp.bfloat16
F32 = jnp.float32
LANES = 128
GROUP = 4
WIDE = D // GROUP
CHUNKS = FF // WIDE

norm_eps = 1e-05
beta_one = 0.9
beta_two = 0.999
rate = 0.01
decay = 0.1
adam_eps = 1e-08
gelu_c = 0.7978845608028654
gelu_a = 0.044715

VMEM_LIMIT = 58 * 1024 * 1024

ROWS = (D, D, D, FF)
PANELS = (3 * D // 4 // LANES, D // 4 // LANES, FF // 4 // LANES, D // 4 // LANES)


def pieces_of(count):
    size = sum(r * p for r, p in zip(ROWS, PANELS)) // count
    result = []
    for d in range(count):
        low, high = d * size, (d + 1) * size
        held, start = [], 0
        for mat in range(4):
            end = start + ROWS[mat] * PANELS[mat]
            a, b = max(low, start), min(high, end)
            if a < b:
                held.append((mat, (a - start) // PANELS[mat], (b - start) // PANELS[mat], a - low))
            start = end
        result.append(held)
    return size, result


def params_of(**extra):
    return pltpu.CompilerParams(vmem_limit_bytes=VMEM_LIMIT, **extra)


ANY = pl.BlockSpec(memory_space=pl.ANY)
VM = pl.BlockSpec(memory_space=pltpu.VMEM)
SM = pl.BlockSpec(memory_space=pltpu.SMEM)


def shape(dims, dtype):
    return jax.ShapeDtypeStruct(dims, dtype)


def nt(a, b):
    return lax.dot_general(a, b, (((1,), (1,)), ((), ())), preferred_element_type=F32)


def tn(a, b):
    return lax.dot_general(a, b, (((0,), (0,)), ((), ())), preferred_element_type=F32)


def nn(a, b):
    return jnp.dot(a, b, preferred_element_type=F32)


def norm_parts(values):
    center = values - jnp.mean(values, axis=-1, keepdims=True)
    spread = jnp.mean(center * center, axis=-1, keepdims=True)
    scale = lax.rsqrt(spread + norm_eps)
    return center * scale, scale


def norm_back(values, gain, grad):
    hat, scale = norm_parts(values)
    dhat = grad * gain
    back = scale * (
        dhat
        - jnp.mean(dhat, axis=-1, keepdims=True)
        - hat * jnp.mean(dhat * hat, axis=-1, keepdims=True)
    )
    return back, jnp.sum(grad * hat, axis=0, keepdims=True), jnp.sum(grad, axis=0, keepdims=True)


def load_matrix(whole, target, mat, pieces, sem):
    for c in range(4):
        for d, held in enumerate(pieces):
            for m, k0, k1, base in held:
                if m != mat:
                    continue
                for j in range(PANELS[mat]):
                    pltpu.make_async_copy(
                        whole.at[c, d, pl.ds(base + j * (k1 - k0), k1 - k0)],
                        target.at[c * PANELS[mat] + j, pl.ds(k0, k1 - k0)],
                        sem,
                    ).start()


def wait_all(ref, sem):
    pltpu.make_async_copy(ref, ref, sem).wait()


def store_matrix(stage, whole, mat, pieces, sem):
    for c in range(4):
        for d, held in enumerate(pieces):
            for m, k0, k1, base in held:
                if m != mat:
                    continue
                for j in range(PANELS[mat]):
                    pltpu.make_async_copy(
                        stage.at[c * PANELS[mat] + j, pl.ds(k0, k1 - k0)],
                        whole.at[c, d, pl.ds(base + j * (k1 - k0), k1 - k0)],
                        sem,
                    ).start()


def prep_kernel(plan, me, slab, out):
    for d, held in enumerate(plan.pieces):

        @pl.when(me[0] == d)
        def _(held=held):
            for mat, k0, k1, base in held:
                count, step = k1 - k0, PANELS[mat]
                for j in range(step):
                    out[pl.ds(base + j * count, count), :] = slab[pl.ds(base + j, count, stride=step), :].astype(BF)


def prepare(plan, me, slab):
    return pl.pallas_call(
        functools.partial(prep_kernel, plan),
        out_shape=shape((plan.size, LANES), BF),
        in_specs=[SM, VM],
        out_specs=VM,
        compiler_params=params_of(),
        name="prep",
    )(me, slab)


def qkv_kernel(pieces, me, x, vec, whole, normed, out0, out1, out2, out3, weight, qkv, sem):
    load_matrix(whole, weight, 0, pieces, sem)
    hat, _ = norm_parts(x[...])
    normed[...] = (hat * vec[0:1, :] + vec[1:2, :]).astype(BF)
    wait_all(weight, sem)
    for b in range(3 * GROUP):
        kind, at = b // GROUP, b % GROUP
        acc = nn(normed[...], jnp.concatenate([weight[2 * b], weight[2 * b + 1]], axis=1))
        if kind != 1:
            row = 2 if kind == 0 else 3
            acc = acc + vec[row : row + 1, at * WIDE : (at + 1) * WIDE]
        qkv[b] = acc.astype(BF)
    mine = me[0] % GROUP
    for r, out in enumerate((out0, out1, out2, out3)):
        for kind in range(3):
            out[:, kind * WIDE : (kind + 1) * WIDE] = qkv[kind * GROUP + (mine ^ r)]


def qkv_call(plan, me, x, vec, whole):
    rows = x.shape[0]
    return pl.pallas_call(
        functools.partial(qkv_kernel, plan.pieces),
        out_shape=[shape((rows, D), BF)] + [shape((rows, 3 * WIDE), BF)] * GROUP,
        in_specs=[SM, VM, VM, ANY],
        out_specs=[VM] * 5,
        scratch_shapes=[
            pltpu.VMEM((3 * D // LANES, D, LANES), BF),
            pltpu.VMEM((3 * GROUP, rows, WIDE), BF),
            pltpu.SemaphoreType.DMA,
        ],
        compiler_params=params_of(),
        name="qkv",
    )(me, x, vec, whole)


def diagonal(rows):
    return lax.broadcasted_iota(jnp.int32, (rows, rows), 1) <= lax.broadcasted_iota(jnp.int32, (rows, rows), 0)


def attend_kernel(me, in0, in1, in2, in3, out0, out1, out2, out3, lse, q, k, v, o):
    mine = me[0] % GROUP
    rows = in0.shape[0]
    for r, ref in enumerate((in0, in1, in2, in3)):
        at = pl.ds(pl.multiple_of((mine ^ r) * rows, rows), rows)
        q[at, :] = ref[:, 0:WIDE]
        k[at, :] = ref[:, WIDE : 2 * WIDE]
        v[at, :] = ref[:, 2 * WIDE : 3 * WIDE]
    seen = diagonal(rows)
    for h in range(WIDE // HEAD):
        cols = slice(h * HEAD, (h + 1) * HEAD)
        for i in range(GROUP):
            here = slice(i * rows, (i + 1) * rows)
            qi = q[here, cols]
            near = jnp.where(seen, nt(qi, k[here, cols]) * 0.125, -1000000000.0)
            top = jnp.max(near, axis=1, keepdims=True)
            if i:
                far = nt(qi, k[0 : i * rows, cols]) * 0.125
                top = jnp.maximum(top, jnp.max(far, axis=1, keepdims=True))
                far = jnp.exp(far - top)
            near = jnp.exp(near - top)
            total = jnp.sum(near, axis=1, keepdims=True)
            if i:
                total = total + jnp.sum(far, axis=1, keepdims=True)
            inv = 1.0 / total
            res = nn((near * inv).astype(BF), v[here, cols])
            if i:
                res = res + nn((far * inv).astype(BF), v[0 : i * rows, cols])
            o[i, :, cols] = res.astype(BF)
            lse[here, h : h + 1] = top + jnp.log(total)
    for r, out in enumerate((out0, out1, out2, out3)):
        out[...] = o[mine ^ r]


def attend_call(me, heads):
    rows = heads[0].shape[0]
    span = GROUP * rows
    return pl.pallas_call(
        attend_kernel,
        out_shape=[shape((rows, WIDE), BF)] * GROUP + [shape((span, LANES), F32)],
        in_specs=[SM] + [VM] * GROUP,
        out_specs=[VM] * 5,
        scratch_shapes=[pltpu.VMEM((span, WIDE), BF)] * 3 + [pltpu.VMEM((GROUP, rows, WIDE), BF)],
        compiler_params=params_of(),
        name="attend",
    )(me, *heads)


def side(ref, at, count=2):
    return jnp.concatenate([ref[at + i] for i in range(count)], axis=1)


def rows_of(ref, at):
    return jnp.concatenate([ref[p, at, :] for p in range(D // LANES)], axis=1)


def ff_kernel(
    pieces, me, in0, in1, in2, in3, x, vec, bias, whole,
    attended, hidden, normed, upper, active, out,
    wo, we, wr, parts, sems,
):
    load_matrix(whole, wo, 1, pieces, sems.at[0])
    load_matrix(whole, we, 2, pieces, sems.at[1])
    load_matrix(whole, wr, 3, pieces, sems.at[2])
    mine = me[0] % GROUP
    for r, ref in enumerate((in0, in1, in2, in3)):
        parts[mine ^ r] = ref[...]
    for g in range(GROUP):
        attended[:, g * WIDE : (g + 1) * WIDE] = parts[g]
    wait_all(wo, sems.at[0])
    for g in range(GROUP):
        cols = slice(g * WIDE, (g + 1) * WIDE)
        hidden[:, cols] = x[:, cols] + nn(attended[...], side(wo, 2 * g)) + vec[4:5, cols]
    hat, _ = norm_parts(hidden[...])
    normed[...] = (hat * vec[5:6, :] + vec[6:7, :]).astype(BF)
    out[...] = hidden[...] + vec[11:12, :]
    wait_all(we, sems.at[1])
    wait_all(wr, sems.at[2])

    def body(n, _):
        u = nn(normed[...], side(we, 2 * n)) + bias[n]
        upper[n] = u
        act = (0.5 * u * (1.0 + jnp.tanh(gelu_c * (u + gelu_a * u * u * u)))).astype(BF)
        active[n] = act
        out[...] += nn(act, rows_of(wr, pl.ds(pl.multiple_of(n * WIDE, WIDE), WIDE)))
        return 0

    lax.fori_loop(0, CHUNKS, body, 0)


def ff_call(plan, me, heads, x, vec, bias, whole):
    rows = x.shape[0]
    return pl.pallas_call(
        functools.partial(ff_kernel, plan.pieces),
        out_shape=[
            shape((rows, D), BF),
            shape((rows, D), F32),
            shape((rows, D), BF),
            shape((CHUNKS, rows, WIDE), F32),
            shape((CHUNKS, rows, WIDE), BF),
            shape((rows, D), F32),
        ],
        in_specs=[SM] + [VM] * 7 + [ANY],
        out_specs=[VM] * 6,
        scratch_shapes=[
            pltpu.VMEM((D // LANES, D, LANES), BF),
            pltpu.VMEM((FF // LANES, D, LANES), BF),
            pltpu.VMEM((D // LANES, FF, LANES), BF),
            pltpu.VMEM((GROUP, rows, WIDE), BF),
            pltpu.SemaphoreType.DMA((3,)),
        ],
        compiler_params=params_of(),
        name="ff",
    )(me, *heads, x, vec, bias, whole)


def ff_back_kernel(
    pieces, me, dy, upper, hidden, vec, whole,
    dyb, dub, dh, dhb, out0, out1, out2, out3, bias_grad, vec_grad,
    wo, we, wr, acc, parts, sems,
):
    load_matrix(whole, wr, 3, pieces, sems.at[2])
    load_matrix(whole, we, 2, pieces, sems.at[1])
    load_matrix(whole, wo, 1, pieces, sems.at[0])
    dyb[...] = dy[...].astype(BF)
    vec_grad[0:1, :] = jnp.sum(dy[...], axis=0, keepdims=True)
    acc[...] = jnp.zeros_like(acc)
    wait_all(wr, sems.at[2])
    wait_all(we, sems.at[1])

    def body(n, _):
        dg = nt(dyb[...], rows_of(wr, pl.ds(pl.multiple_of(n * WIDE, WIDE), WIDE)))
        u = upper[n]
        t = jnp.tanh(gelu_c * (u + gelu_a * u * u * u))
        slope = 0.5 * (1.0 + t) + 0.5 * u * (1.0 - t * t) * (gelu_c * (1.0 + 3.0 * gelu_a * u * u))
        du = dg * slope
        bias_grad[n] = jnp.sum(du, axis=0, keepdims=True)
        low = du.astype(BF)
        dub[n] = low
        acc[...] += nt(low, side(we, 2 * n))
        return 0

    lax.fori_loop(0, CHUNKS, body, 0)
    back, gain, shift = norm_back(hidden[...], vec[5:6, :], acc[...])
    total = dy[...] + back
    vec_grad[1:2, :] = gain
    vec_grad[2:3, :] = shift
    vec_grad[3:4, :] = jnp.sum(total, axis=0, keepdims=True)
    vec_grad[4:8, :] = jnp.zeros((4, D), F32)
    dh[...] = total
    dhb[...] = total.astype(BF)
    wait_all(wo, sems.at[0])
    for g in range(GROUP):
        parts[g] = nt(dhb[...], rows_of(wo, slice(g * WIDE, (g + 1) * WIDE))).astype(BF)
    mine = me[0] % GROUP
    for r, out in enumerate((out0, out1, out2, out3)):
        out[...] = parts[mine ^ r]


def ff_back_call(plan, me, dy, upper, hidden, vec, whole):
    rows = dy.shape[0]
    return pl.pallas_call(
        functools.partial(ff_back_kernel, plan.pieces),
        out_shape=[
            shape((rows, D), BF),
            shape((CHUNKS, rows, WIDE), BF),
            shape((rows, D), F32),
            shape((rows, D), BF),
        ]
        + [shape((rows, WIDE), BF)] * GROUP
        + [shape((CHUNKS, 1, WIDE), F32), shape((8, D), F32)],
        in_specs=[SM] + [VM] * 4 + [ANY],
        out_specs=[VM] * 10,
        scratch_shapes=[
            pltpu.VMEM((D // LANES, D, LANES), BF),
            pltpu.VMEM((FF // LANES, D, LANES), BF),
            pltpu.VMEM((D // LANES, FF, LANES), BF),
            pltpu.VMEM((rows, D), F32),
            pltpu.VMEM((GROUP, rows, WIDE), BF),
            pltpu.SemaphoreType.DMA((3,)),
        ],
        compiler_params=params_of(),
        name="ff_back",
    )(me, dy, upper, hidden, vec, whole)


def attend_back_kernel(
    me, in0, in1, in2, in3, do0, do1, do2, do3, lse,
    out0, out1, out2, out3, sums,
    q, k, v, do, dq, dk, dv,
):
    mine = me[0] % GROUP
    rows = in0.shape[0]
    for r, (ref, grad) in enumerate(((in0, do0), (in1, do1), (in2, do2), (in3, do3))):
        at = pl.ds(pl.multiple_of((mine ^ r) * rows, rows), rows)
        q[at, :] = ref[:, 0:WIDE]
        k[at, :] = ref[:, WIDE : 2 * WIDE]
        v[at, :] = ref[:, 2 * WIDE : 3 * WIDE]
        do[at, :] = grad[...]
    seen = diagonal(rows)
    for h in range(WIDE // HEAD):
        cols = slice(h * HEAD, (h + 1) * HEAD)
        total = jnp.zeros((1, HEAD), F32)
        for i in reversed(range(GROUP)):
            here = slice(i * rows, (i + 1) * rows)
            past = slice(0, i * rows)
            qi, doi, ls = q[here, cols], do[here, cols], lse[here, h : h + 1]
            near = jnp.exp(jnp.where(seen, nt(qi, k[here, cols]) * 0.125, -1000000000.0) - ls)
            dnear = nt(doi, v[here, cols])
            inner = jnp.sum(near * dnear, axis=1, keepdims=True)
            if i:
                far = jnp.exp(nt(qi, k[past, cols]) * 0.125 - ls)
                dfar = nt(doi, v[past, cols])
                inner = inner + jnp.sum(far * dfar, axis=1, keepdims=True)
            snear = (near * (dnear - inner) * 0.125).astype(BF)
            res = nn(snear, k[here, cols])
            dkn = tn(snear, qi)
            dvn = tn(near.astype(BF), doi)
            last = i == GROUP - 1
            dk[here, cols] = dkn if last else dk[here, cols] + dkn
            dv[here, cols] = dvn if last else dv[here, cols] + dvn
            if i:
                sfar = (far * (dfar - inner) * 0.125).astype(BF)
                res = res + nn(sfar, k[past, cols])
                dkf = tn(sfar, qi)
                dvf = tn(far.astype(BF), doi)
                dk[past, cols] = dkf if last else dk[past, cols] + dkf
                dv[past, cols] = dvf if last else dv[past, cols] + dvf
            total = total + jnp.sum(res, axis=0, keepdims=True)
            dq[i, :, cols] = res.astype(BF)
        sums[0:1, cols] = total
    sums[1:2, :] = jnp.sum(dv[...], axis=0, keepdims=True)
    sums[2:8, :] = jnp.zeros((6, WIDE), F32)
    for r, out in enumerate((out0, out1, out2, out3)):
        at = pl.ds(pl.multiple_of((mine ^ r) * rows, rows), rows)
        out[:, 0:WIDE] = dq[mine ^ r]
        out[:, WIDE : 2 * WIDE] = dk[at, :].astype(BF)
        out[:, 2 * WIDE : 3 * WIDE] = dv[at, :].astype(BF)


def attend_back_call(me, heads, grads, lse):
    rows = heads[0].shape[0]
    span = GROUP * rows
    return pl.pallas_call(
        attend_back_kernel,
        out_shape=[shape((rows, 3 * WIDE), BF)] * GROUP + [shape((8, WIDE), F32)],
        in_specs=[SM] + [VM] * 9,
        out_specs=[VM] * 5,
        scratch_shapes=[pltpu.VMEM((span, WIDE), BF)] * 4
        + [pltpu.VMEM((GROUP, rows, WIDE), BF)]
        + [pltpu.VMEM((span, WIDE), F32)] * 2,
        compiler_params=params_of(),
        name="attend_back",
    )(me, *heads, *grads, lse)


def qkv_back_kernel(pieces, me, in0, in1, in2, in3, dh, x, vec, whole, mixed, dx, vec_grad, weight, acc, sem):
    load_matrix(whole, weight, 0, pieces, sem)
    mine = me[0] % GROUP
    for r, ref in enumerate((in0, in1, in2, in3)):
        for kind in range(3):
            mixed[kind * GROUP + (mine ^ r)] = ref[:, kind * WIDE : (kind + 1) * WIDE]
    acc[...] = jnp.zeros_like(acc)
    wait_all(weight, sem)

    def body(b, _):
        acc[...] += nt(mixed[b], side(weight, 2 * b))
        return 0

    lax.fori_loop(0, 3 * GROUP, body, 0)
    back, gain, shift = norm_back(x[...], vec[0:1, :], acc[...])
    dx[...] = dh[...] + back
    vec_grad[0:1, :] = gain
    vec_grad[1:2, :] = shift
    vec_grad[2:8, :] = jnp.zeros((6, D), F32)


def qkv_back_call(plan, me, grads, dh, x, vec, whole):
    rows = x.shape[0]
    return pl.pallas_call(
        functools.partial(qkv_back_kernel, plan.pieces),
        out_shape=[shape((3 * GROUP, rows, WIDE), BF), shape((rows, D), F32), shape((8, D), F32)],
        in_specs=[SM] + [VM] * 7 + [ANY],
        out_specs=[VM] * 3,
        scratch_shapes=[
            pltpu.VMEM((3 * D // LANES, D, LANES), BF),
            pltpu.VMEM((rows, D), F32),
            pltpu.SemaphoreType.DMA,
        ],
        compiler_params=params_of(),
        name="qkv_back",
    )(me, *grads, dh, x, vec, whole)


def ff_weight_kernel(pieces, attended, normed, active, dhb, dub, dyb, out, so, se, sr, sems):
    def reduce_body(n, _):
        res = tn(active[n], dyb[...]).astype(BF)
        at = pl.ds(pl.multiple_of(n * WIDE, WIDE), WIDE)
        for p in range(D // LANES):
            sr[p, at, :] = res[:, p * LANES : (p + 1) * LANES]
        return 0

    lax.fori_loop(0, CHUNKS, reduce_body, 0)
    store_matrix(sr, out, 3, pieces, sems.at[2])

    def expand_body(n, _):
        res = tn(normed[...], dub[n]).astype(BF)
        se[2 * n] = res[:, :LANES]
        se[2 * n + 1] = res[:, LANES:]
        return 0

    lax.fori_loop(0, CHUNKS, expand_body, 0)
    store_matrix(se, out, 2, pieces, sems.at[1])
    for g in range(GROUP):
        res = tn(attended[...], dhb[:, g * WIDE : (g + 1) * WIDE]).astype(BF)
        so[2 * g] = res[:, :LANES]
        so[2 * g + 1] = res[:, LANES:]
    store_matrix(so, out, 1, pieces, sems.at[0])
    wait_all(sr, sems.at[2])
    wait_all(se, sems.at[1])
    wait_all(so, sems.at[0])


def ff_weight_call(plan, attended, normed, active, dhb, dub, dyb):
    return pl.pallas_call(
        functools.partial(ff_weight_kernel, plan.pieces),
        out_shape=shape((4, plan.n_dp, plan.size, LANES), BF),
        in_specs=[VM] * 6,
        out_specs=ANY,
        scratch_shapes=[
            pltpu.VMEM((D // LANES, D, LANES), BF),
            pltpu.VMEM((FF // LANES, D, LANES), BF),
            pltpu.VMEM((D // LANES, FF, LANES), BF),
            pltpu.SemaphoreType.DMA((3,)),
        ],
        compiler_params=params_of(),
        name="ff_weight",
    )(attended, normed, active, dhb, dub, dyb)


def qkv_weight_kernel(pieces, normed, mixed, before, out, stage, sem):
    def body(b, _):
        res = tn(normed[...], mixed[b]).astype(BF)
        stage[2 * b] = res[:, :LANES]
        stage[2 * b + 1] = res[:, LANES:]
        return 0

    lax.fori_loop(0, 3 * GROUP, body, 0)
    store_matrix(stage, out, 0, pieces, sem)
    wait_all(stage, sem)


def qkv_weight_call(plan, normed, mixed, buffer):
    return pl.pallas_call(
        functools.partial(qkv_weight_kernel, plan.pieces),
        out_shape=shape(buffer.shape, BF),
        in_specs=[VM, VM, ANY],
        out_specs=ANY,
        input_output_aliases={2: 0},
        scratch_shapes=[pltpu.VMEM((3 * D // LANES, D, LANES), BF), pltpu.SemaphoreType.DMA],
        compiler_params=params_of(),
        name="qkv_weight",
    )(normed, mixed, buffer)


def adam_parts(grad, moment, square, master, weight_decay):
    moment_next = beta_one * moment + (1.0 - beta_one) * grad
    square_next = beta_two * square + (1.0 - beta_two) * grad * grad
    corrected = moment_next / (1.0 - beta_one**STEP)
    scaled = square_next / (1.0 - beta_two**STEP)
    update = -rate * (corrected / (jnp.sqrt(scaled) + adam_eps) + weight_decay * master)
    return moment_next, square_next, update


def adam_kernel(plan, me, owned, master, moment, square, *refs):
    grad, moment_next, square_next, update = refs[-4:]
    for d, held in enumerate(plan.pieces):

        @pl.when(me[0] == d)
        def _(held=held):
            for mat, k0, k1, base in held:
                size, step = k1 - k0, PANELS[mat]
                for j in range(step):
                    grad[0, 0, pl.ds(base + j, size, stride=step), :] = owned[pl.ds(base + j * size, size), :]

    new = adam_parts(grad[0, 0], moment[0, 0], square[0, 0], master[0, 0], decay)
    moment_next[0, 0], square_next[0, 0], update[0, 0] = new


def adam_call(plan, me, layer, grads, master, moment, square, before):
    block = pl.BlockSpec((1, 1) + master.shape[2:], lambda i: (layer, 0, 0, 0))
    whole = [pl.BlockSpec(g.shape, lambda i: (0, 0)) for g in grads]
    first = 1 + len(grads) + 3
    return pl.pallas_call(
        functools.partial(adam_kernel, plan),
        grid=(1,),
        out_shape=[shape(master.shape, F32)] * 4,
        in_specs=[SM] + whole + [block] * 3 + [ANY] * len(before),
        out_specs=[block] * 4,
        input_output_aliases={first + i: i for i in range(len(before))},
        compiler_params=params_of(),
        name="adam",
    )(me, *grads, master, moment, square, *before)


class Mover:
    def __init__(self, n_dp):
        self.n_dp = n_dp
        self.size, self.pieces = pieces_of(n_dp)

    def gather_all(self, helds):
        wholes = [lax.all_gather(held, ("ctx", "dp"), axis=0, tiled=True) for held in helds]
        return [whole.reshape(4, self.n_dp, self.size, LANES) for whole in wholes]

    def scatter(self, buffer):
        flat = buffer.reshape(-1, LANES)
        return [lax.psum_scatter(flat, ("ctx", "dp"), scatter_dimension=0, tiled=True).astype(F32)]

    def scatter_vectors(self, grads):
        return lax.psum_scatter(grads.reshape(-1), ("dp", "ctx"), scatter_dimension=0, tiled=True)


MESH = pl.DeviceIdType.MESH
CORE = 1
FLIPS = ((1, 0), (2, 0), (4, 0), (0, 1), (0, 2), (0, 3))


def exchange(values, flip_dp, flip_ctx):
    pairs = [(d * 4 + z, (d ^ flip_dp) * 4 + (z ^ flip_ctx)) for d in range(8) for z in range(4)]
    return lax.ppermute(values, ("dp", "ctx"), pairs)


def greet(d, z):
    barrier = pltpu.get_barrier_semaphore()
    for fd, fz in FLIPS:
        pl.semaphore_signal(barrier, inc=1, device_id=(d ^ fd, z ^ fz), device_id_type=MESH)
    pl.semaphore_wait(barrier, len(FLIPS))


def run_jobs(jobs, lag):
    live = list(zip(jobs, lag))
    step = 0
    while live:
        rest = []
        for job, late in live:
            if step >= late:
                try:
                    next(job)
                except StopIteration:
                    continue
            rest.append((job, late))
        live = rest
        step += 1


class BitMover(Mover):
    def __init__(self, n_dp):
        super().__init__(n_dp)
        unit = self.size // 6
        self.rows = [(0, 2 * unit), (2 * unit, 2 * unit), (4 * unit, unit), (5 * unit, unit)]
        self.orders = [(True, 2, 4), (True, 4, 2), (False, 2, 4), (False, 4, 2)]

    def gather_all(self, helds):
        layers = len(helds)
        per_job = 16

        def kernel(*refs):
            helds, wholes = refs[:layers], refs[layers : 2 * layers]
            local, send, recv = refs[2 * layers :]
            d, z = lax.axis_index("dp"), lax.axis_index("ctx")
            greet(d, z)

            def job(layer, part):
                low, size = self.rows[part]
                z_first, a, b = self.orders[part]
                rows = pl.ds(low, size)
                held, whole = helds[layer].at[rows], wholes[layer]
                slots = iter(range((layer * 4 + part) * per_job, (layer * 4 + part + 1) * per_job))
                started = []

                def push(src, dst, fd, fz):
                    slot = next(slots)
                    copy = pltpu.make_async_remote_copy(
                        src_ref=src, dst_ref=dst, send_sem=send.at[slot], recv_sem=recv.at[slot],
                        device_id=(d ^ fd, z ^ fz), device_id_type=MESH,
                    )
                    copy.start()
                    started.append(copy)
                    return copy

                def line(dd, fd):
                    ref = whole.at[:, dd, rows]
                    return push(ref, ref, fd, 0)

                own = pltpu.make_async_copy(held, whole.at[z, d, rows], local.at[layer * 4 + part])
                own.start()
                mine = [push(held, whole.at[z, d, rows], 0, k) for k in (3, 2, 1)]
                if z_first:
                    yield
                    own.wait()
                    for copy in mine:
                        copy.wait_recv()
                    first = line(d, a)
                    second = line(d, b)
                    cores = [line(d, CORE)]
                    yield
                    first.wait_recv()
                    third = line(d ^ a, b)
                    cores.append(line(d ^ a, CORE))
                    yield
                    second.wait_recv()
                    cores.append(line(d ^ b, CORE))
                    third.wait_recv()
                    cores.append(line(d ^ a ^ b, CORE))
                else:
                    first = push(held, whole.at[z, d, rows], a, 0)
                    yield
                    first.wait_recv()
                    other = whole.at[z, d ^ a, rows]
                    theirs = [push(other, other, 0, k) for k in (3, 2, 1)]
                    yield
                    own.wait()
                    for copy in mine:
                        copy.wait_recv()
                    second = line(d, b)
                    cores = [line(d, CORE)]
                    yield
                    for copy in theirs:
                        copy.wait_recv()
                    third = line(d ^ a, b)
                    cores.append(line(d ^ a, CORE))
                    yield
                    second.wait_recv()
                    cores.append(line(d ^ b, CORE))
                    third.wait_recv()
                    cores.append(line(d ^ a ^ b, CORE))
                yield
                for copy in cores:
                    copy.wait_recv()
                for copy in started:
                    copy.wait_send()

            jobs = [job(layer, part) for layer in range(layers) for part in range(4)]
            run_jobs(jobs, [2 * (i // 4) for i in range(len(jobs))])

        count = layers * 4 * per_job
        return pl.pallas_call(
            kernel,
            out_shape=[shape((4, self.n_dp, self.size, LANES), BF)] * layers,
            in_specs=[VM] * layers,
            out_specs=[ANY] * layers,
            scratch_shapes=[
                pltpu.SemaphoreType.DMA((4 * layers,)),
                pltpu.SemaphoreType.DMA((count,)),
                pltpu.SemaphoreType.DMA((count,)),
            ],
            compiler_params=params_of(collective_id=1, has_side_effects=True),
            name="gather",
        )(*helds)

    def scatter(self, buffer):
        per_job = 16

        def kernel(grads, out, *scratch):
            sums, cores, bees, ays, zees = (scratch[i : i + 4] for i in range(0, 20, 4))
            local, send, recv = scratch[20:]
            d, z = lax.axis_index("dp"), lax.axis_index("ctx")
            greet(d, z)

            def job(part):
                low, size = self.rows[part]
                z_first, a, b = self.orders[part]
                rows = pl.ds(low, size)
                acc, from_c, from_b, from_a, from_z = sums[part], cores[part], bees[part], ays[part], zees[part]
                slots = iter(range(part * per_job, (part + 1) * per_job))
                started = []

                def push(src, dst, fd, fz):
                    slot = next(slots)
                    copy = pltpu.make_async_remote_copy(
                        src_ref=src, dst_ref=dst, send_sem=send.at[slot], recv_sem=recv.at[slot],
                        device_id=(d ^ fd, z ^ fz), device_id_type=MESH,
                    )
                    copy.start()
                    started.append(copy)
                    return copy

                def add(into, more):
                    block = 256

                    def body(i, _):
                        at = pl.ds(pl.multiple_of(i * block, block), block)
                        for x, y in zip(into, more):
                            x[at, :] = x[at, :] + y[at, :]
                        return 0

                    lax.fori_loop(0, size // block, body, 0)

                places = [(1, 1), (0, 1), (1, 0), (0, 0)]
                loads, gives = [], []
                for i, (ja, jb) in enumerate(places):
                    here = d ^ (ja * a) ^ (jb * b)
                    load = pltpu.make_async_copy(grads.at[:, here, rows], acc.at[i], local.at[part * 4 + i])
                    load.start()
                    loads.append(load)
                    gives.append(push(grads.at[:, here ^ CORE, rows], from_c.at[i], CORE, 0))
                yield
                for i in (0, 1):
                    loads[i].wait()
                    gives[i].wait_recv()
                    add([acc.at[i, k] for k in range(4)], [from_c.at[i, k] for k in range(4)])
                to_b = [push(acc.at[i], from_b.at[i], b, 0) for i in (0, 1)]
                for i in (2, 3):
                    loads[i].wait()
                    gives[i].wait_recv()
                    add([acc.at[i, k] for k in range(4)], [from_c.at[i, k] for k in range(4)])
                yield
                if z_first:
                    to_b[0].wait_recv()
                    add([acc.at[2, k] for k in range(4)], [from_b.at[0, k] for k in range(4)])
                    to_a = push(acc.at[2], from_a, a, 0)
                    to_b[1].wait_recv()
                    add([acc.at[3, k] for k in range(4)], [from_b.at[1, k] for k in range(4)])
                    yield
                    to_a.wait_recv()
                    add([acc.at[3, k] for k in range(4)], [from_a.at[k] for k in range(4)])
                    to_z = [push(acc.at[3, z ^ k], from_z.at[k - 1, 0], 0, k) for k in (3, 2, 1)]
                    yield
                    for copy in to_z:
                        copy.wait_recv()

                    def total(at):
                        value = acc[3, z, at, :].astype(F32)
                        for k in range(3):
                            value = value + from_z[k, 0, at, :].astype(F32)
                        return value
                else:
                    for i in (0, 1):
                        to_b[i].wait_recv()
                        add([acc.at[2 + i, k] for k in range(4)], [from_b.at[i, k] for k in range(4)])
                    to_z = [push(acc.at[2 + i, z ^ k], from_z.at[k - 1, i], 0, k) for i in (0, 1) for k in (3, 2, 1)]
                    yield
                    for copy in to_z[:3]:
                        copy.wait_recv()
                    for k in range(3):
                        add([acc.at[2, z]], [from_z.at[k, 0]])
                    to_a = push(acc.at[2, z], from_a.at[0], a, 0)
                    for copy in to_z[3:]:
                        copy.wait_recv()
                    yield
                    to_a.wait_recv()

                    def total(at):
                        value = acc[3, z, at, :].astype(F32)
                        for k in range(3):
                            value = value + from_z[k, 1, at, :].astype(F32)
                        return value + from_a[0, at, :].astype(F32)

                def body(i, _):
                    at = pl.multiple_of(i * 256, 256)
                    out[pl.ds(low + at, 256), :] = total(pl.ds(at, 256))
                    return 0

                lax.fori_loop(0, size // 256, body, 0)
                for copy in started:
                    copy.wait_send()

            run_jobs([job(part) for part in range(4)], [0, 0, 0, 0])

        sizes = [size for _, size in self.rows]
        firsts = [order[0] for order in self.orders]
        count = 4 * per_job
        return [
            pl.pallas_call(
                kernel,
                out_shape=shape((self.size, LANES), F32),
                in_specs=[ANY],
                out_specs=VM,
                scratch_shapes=[pltpu.VMEM((4, 4, n, LANES), BF) for n in sizes]
                + [pltpu.VMEM((4, 4, n, LANES), BF) for n in sizes]
                + [pltpu.VMEM((2, 4, n, LANES), BF) for n in sizes]
                + [pltpu.VMEM((4 if first else 1, n, LANES), BF) for n, first in zip(sizes, firsts)]
                + [pltpu.VMEM((3, 1 if first else 2, n, LANES), BF) for n, first in zip(sizes, firsts)]
                + [
                    pltpu.SemaphoreType.DMA((16,)),
                    pltpu.SemaphoreType.DMA((count,)),
                    pltpu.SemaphoreType.DMA((count,)),
                ],
                compiler_params=params_of(collective_id=2, has_side_effects=True),
                name="scatter",
            )(buffer)
        ]

    def scatter_vectors(self, grads):
        d, z = lax.axis_index("dp"), lax.axis_index("ctx")
        value = grads.reshape(2, -1)
        for flip_dp, flip_ctx in ((4, 0), (2, 0), (1, 0), (0, 2), (0, 1)):
            bit = jnp.where((d & flip_dp) + (z & flip_ctx) > 0, 1, 0)
            halves = value.reshape(2, -1)
            keep = lax.dynamic_index_in_dim(halves, bit, 0, keepdims=False)
            give = lax.dynamic_index_in_dim(halves, 1 - bit, 0, keepdims=False)
            value = keep + exchange(give, flip_dp, flip_ctx)
        return value


def swap(values, n_dp):
    pairs = [
        (d * GROUP + z, ((d // GROUP) * GROUP + z) * GROUP + d % GROUP) for d in range(n_dp) for z in range(GROUP)
    ]
    return lax.ppermute(values, ("dp", "ctx"), pairs)


def trade(arrays, n_dp):
    result = [arrays[0]]
    for r in range(1, GROUP):
        pairs = [(d * GROUP + z, (d ^ r) * GROUP + z) for d in range(n_dp) for z in range(GROUP)]
        result.append(lax.ppermute(arrays[r], ("dp", "ctx"), pairs))
    return result


def per_device(
    n_dp,
    layer_input,
    out_cotangent,
    params,
    vectors,
    param_moment,
    vector_moment,
    param_square,
    vector_square,
):
    plan = BitMover(n_dp) if n_dp == 8 else Mover(n_dp)
    me = jnp.stack([lax.axis_index("dp"), lax.axis_index("ctx")]).astype(jnp.int32)
    place = me[0] % GROUP

    wholes = plan.gather_all([prepare(plan, me, params[layer, 0]) for layer in range(LAYERS)])
    lines = lax.all_gather(vectors.astype(BF), ("dp", "ctx"), axis=1, tiled=True).astype(F32)
    vecs = [lines[layer].reshape(12, D) for layer in range(LAYERS)]

    value = swap(layer_input, n_dp).astype(F32)
    grad = swap(out_cotangent, n_dp).astype(F32)

    saved = []
    for layer in range(LAYERS):
        vec, whole = vecs[layer], wholes[layer]
        bias = vec[7:11].reshape(CHUNKS, 1, WIDE)
        normed1, *sent = qkv_call(plan, me, value, vec, whole)
        heads = trade(sent, n_dp)
        *sent, lse = attend_call(me, heads)
        attended, hidden, normed2, upper, active, result = ff_call(
            plan, me, trade(sent, n_dp), value, vec, bias, whole
        )
        saved.append((value, normed1, heads, lse, attended, hidden, normed2, upper, active))
        value = result
    layer_output = swap(value.astype(BF), n_dp)

    owned, vec_owned = [None] * LAYERS, [None] * LAYERS
    for layer in reversed(range(LAYERS)):
        vec, whole = vecs[layer], wholes[layer]
        x, normed1, heads, lse, attended, hidden, normed2, upper, active = saved[layer]
        dyb, dub, dh, dhb, *rest = ff_back_call(plan, me, grad, upper, hidden, vec, whole)
        sent, bias_grad, vec_grad2 = rest[:GROUP], rest[GROUP], rest[GROUP + 1]
        buffer = ff_weight_call(plan, attended, normed2, active, dhb, dub, dyb)
        *sent, sums = attend_back_call(me, heads, trade(sent, n_dp), lse)
        mixed, grad, vec_grad1 = qkv_back_call(plan, me, trade(sent, n_dp), dh, x, vec, whole)
        buffer = qkv_weight_call(plan, normed1, mixed, buffer)
        spread = lax.dynamic_update_slice(jnp.zeros((2, D), F32), sums[0:2], (0, place * WIDE))
        vector_grads = jnp.concatenate(
            [
                vec_grad1[0:2],
                spread,
                vec_grad2[3:4],
                vec_grad2[1:3],
                bias_grad.reshape(4, D),
                vec_grad2[0:1],
            ]
        )
        owned[layer] = plan.scatter(buffer)
        vec_owned[layer] = plan.scatter_vectors(vector_grads)
    input_grad = swap(grad.astype(BF), n_dp).astype(F32)

    done = []
    for layer in reversed(range(LAYERS)):
        done = adam_call(plan, me, layer, owned[layer], params, param_moment, param_square, done)
    vector_grad = jnp.stack(vec_owned)
    vector_step = adam_parts(vector_grad, vector_moment, vector_square, vectors, 0.0)
    return (
        layer_output,
        input_grad,
        done[0],
        vector_grad,
        done[1],
        vector_step[0],
        done[2],
        vector_step[1],
        done[3],
        vector_step[2],
    )


def solution(mesh):
    tokens = P(("dp", "ctx"), None)
    slabs = P(None, "ctx", "dp", None)
    lines = P(None, ("dp", "ctx"))
    return jax.shard_map(
        functools.partial(per_device, mesh.shape["dp"]),
        mesh=mesh,
        in_specs=(tokens, tokens, slabs, lines, slabs, lines, slabs, lines),
        out_specs=(tokens, tokens, slabs, lines, slabs, lines, slabs, lines, slabs, lines),
        check_vma=False,
    )
```

```python
import functools

import jax
import jax.numpy as jnp
from jax import lax
from jax.experimental import pallas as pl
from jax.experimental.pallas import tpu as pltpu
from jax.sharding import PartitionSpec as P

D = 1024
HEADS = 16
HEAD = 64
FF = 4096
LAYERS = 2
STEP = 10
BF = jnp.bfloat16
F32 = jnp.float32
LANES = 128
GROUP = 4
WIDE = D // GROUP
CHUNKS = FF // WIDE

norm_eps = 1e-05
beta_one = 0.9
beta_two = 0.999
rate = 0.01
decay = 0.1
adam_eps = 1e-08
gelu_c = 0.7978845608028654
gelu_a = 0.044715

VMEM_LIMIT = 60 * 1024 * 1024

ROWS = (D, D, D, FF)
PANELS = (3 * D // 4 // LANES, D // 4 // LANES, FF // 4 // LANES, D // 4 // LANES)


def pieces_of(count):
    size = sum(r * p for r, p in zip(ROWS, PANELS)) // count
    result = []
    for d in range(count):
        low, high = d * size, (d + 1) * size
        held, start = [], 0
        for mat in range(4):
            end = start + ROWS[mat] * PANELS[mat]
            a, b = max(low, start), min(high, end)
            if a < b:
                held.append((mat, (a - start) // PANELS[mat], (b - start) // PANELS[mat], a - low))
            start = end
        result.append(held)
    return size, result


TURN = (0, 2, 1, 3)


def place_of(d):
    return (d & 1) * 2 + (d >> 1) % 2


def params_of(**extra):
    return pltpu.CompilerParams(vmem_limit_bytes=VMEM_LIMIT, **extra)


MESH = pl.DeviceIdType.MESH
ANY = pl.BlockSpec(memory_space=pl.ANY)
VM = pl.BlockSpec(memory_space=pltpu.VMEM)
SM = pl.BlockSpec(memory_space=pltpu.SMEM)


def shape(dims, dtype):
    return jax.ShapeDtypeStruct(dims, dtype)


def nt(a, b):
    return lax.dot_general(a, b, (((1,), (1,)), ((), ())), preferred_element_type=F32)


def tn(a, b):
    return lax.dot_general(a, b, (((0,), (0,)), ((), ())), preferred_element_type=F32)


def nn(a, b):
    return jnp.dot(a, b, preferred_element_type=F32)


def norm_parts(values):
    center = values - jnp.mean(values, axis=-1, keepdims=True)
    spread = jnp.mean(center * center, axis=-1, keepdims=True)
    scale = lax.rsqrt(spread + norm_eps)
    return center * scale, scale


def norm_back(values, gain, grad):
    hat, scale = norm_parts(values)
    dhat = grad * gain
    back = scale * (
        dhat
        - jnp.mean(dhat, axis=-1, keepdims=True)
        - hat * jnp.mean(dhat * hat, axis=-1, keepdims=True)
    )
    return back, jnp.sum(grad * hat, axis=0, keepdims=True), jnp.sum(grad, axis=0, keepdims=True)


def load_matrix(whole, target, mat, pieces, sem, split=False):
    for c in range(4):
        for d, held in enumerate(pieces):
            for m, k0, k1, base in held:
                if m != mat:
                    continue
                for j in range(PANELS[mat]):
                    panel, k = c * PANELS[mat] + j, k0
                    while k < k1:
                        n = min(k1 - k, D - k % D) if split else k1 - k
                        at = (panel * 4 + k // D, pl.ds(k % D, n)) if split else (panel, pl.ds(k, n))
                        pltpu.make_async_copy(
                            whole.at[c, d, pl.ds(base + j * (k1 - k0) + k - k0, n)], target.at[at], sem
                        ).start()
                        k += n


def wait_all(ref, sem):
    pltpu.make_async_copy(ref, ref, sem).wait()


def prep_kernel(plan, me, slabs, lines, *outs):
    for layer, out in enumerate(outs):
        out[plan.size :, :] = jnp.zeros((plan.span - plan.size, LANES), BF)
        for r in range(lines.shape[1] // LANES):
            at = plan.size + r
            out[at : at + 1, :] = lines[layer : layer + 1, r * LANES : (r + 1) * LANES].astype(BF)
    for d, held in enumerate(plan.pieces):

        @pl.when(me[0] == d)
        def _(held=held):
            for layer, out in enumerate(outs):
                for mat, k0, k1, base in held:
                    count, step = k1 - k0, PANELS[mat]
                    for j in range(step):
                        rows = slabs[layer, 0, pl.ds(base + j, count, stride=step), :]
                        out[pl.ds(base + j * count, count), :] = rows.astype(BF)


def prepare(plan, me, slabs, lines):
    lines = jnp.pad(lines, ((0, 0), (0, -lines.shape[1] % LANES)))
    return pl.pallas_call(
        functools.partial(prep_kernel, plan),
        out_shape=[shape((plan.span, LANES), BF)] * LAYERS,
        in_specs=[SM, VM, VM],
        out_specs=[VM] * LAYERS,
        compiler_params=params_of(),
        name="prep",
    )(me, slabs, lines)


def qkv_kernel(pieces, me, x, vec, whole, normed, out0, out1, out2, out3, weight, qkv, sem):
    load_matrix(whole, weight, 0, pieces, sem)
    hat, _ = norm_parts(x[...].astype(F32))
    normed[...] = (hat * vec[0:1, :] + vec[1:2, :]).astype(BF)
    wait_all(weight, sem)
    for b in range(3 * GROUP):
        kind, at = b // GROUP, b % GROUP
        acc = nn(normed[...], jnp.concatenate([weight[2 * b], weight[2 * b + 1]], axis=1))
        if kind != 1:
            row = 2 if kind == 0 else 3
            acc = acc + vec[row : row + 1, at * WIDE : (at + 1) * WIDE]
        qkv[b] = acc.astype(BF)
    mine = place_of(me[0])
    for r, out in enumerate((out0, out1, out2, out3)):
        for kind in range(3):
            out[:, kind * WIDE : (kind + 1) * WIDE] = qkv[kind * GROUP + (mine ^ TURN[r])]


def qkv_call(plan, me, x, vec, whole):
    rows = x.shape[0]
    return pl.pallas_call(
        functools.partial(qkv_kernel, plan.pieces),
        out_shape=[shape((rows, D), BF)] + [shape((rows, 3 * WIDE), BF)] * GROUP,
        in_specs=[SM, VM, VM, ANY],
        out_specs=[VM] * 5,
        scratch_shapes=[
            pltpu.VMEM((3 * D // LANES, D, LANES), BF),
            pltpu.VMEM((3 * GROUP, rows, WIDE), BF),
            pltpu.SemaphoreType.DMA,
        ],
        compiler_params=params_of(),
        name="qkv",
    )(me, x, vec, whole)


def diagonal(rows):
    return lax.broadcasted_iota(jnp.int32, (rows, rows), 1) <= lax.broadcasted_iota(jnp.int32, (rows, rows), 0)


def attend_kernel(me, in0, in1, in2, in3, out0, out1, out2, out3, lse, q, k, v, o):
    mine = place_of(me[0])
    rows = in0.shape[0]
    for r, ref in enumerate((in0, in1, in2, in3)):
        at = pl.ds(pl.multiple_of((mine ^ TURN[r]) * rows, rows), rows)
        q[at, :] = ref[:, 0:WIDE]
        k[at, :] = ref[:, WIDE : 2 * WIDE]
        v[at, :] = ref[:, 2 * WIDE : 3 * WIDE]
    seen = diagonal(rows)
    for h in range(WIDE // HEAD):
        cols = slice(h * HEAD, (h + 1) * HEAD)
        for i in range(GROUP):
            here = slice(i * rows, (i + 1) * rows)
            qi = q[here, cols]
            near = jnp.where(seen, nt(qi, k[here, cols]) * 0.125, -1000000000.0)
            top = jnp.max(near, axis=1, keepdims=True)
            if i:
                far = nt(qi, k[0 : i * rows, cols]) * 0.125
                top = jnp.maximum(top, jnp.max(far, axis=1, keepdims=True))
                far = jnp.exp(far - top)
            near = jnp.exp(near - top)
            total = jnp.sum(near, axis=1, keepdims=True)
            if i:
                total = total + jnp.sum(far, axis=1, keepdims=True)
            inv = 1.0 / total
            res = nn((near * inv).astype(BF), v[here, cols])
            if i:
                res = res + nn((far * inv).astype(BF), v[0 : i * rows, cols])
            o[i, :, cols] = res.astype(BF)
            lse[here, h : h + 1] = top + jnp.log(total)
    for r, out in enumerate((out0, out1, out2, out3)):
        out[...] = o[mine ^ TURN[r]]


def attend_call(me, heads):
    rows = heads[0].shape[0]
    span = GROUP * rows
    return pl.pallas_call(
        attend_kernel,
        out_shape=[shape((rows, WIDE), BF)] * GROUP + [shape((span, LANES), F32)],
        in_specs=[SM] + [VM] * GROUP,
        out_specs=[VM] * 5,
        scratch_shapes=[pltpu.VMEM((span, WIDE), BF)] * 3 + [pltpu.VMEM((GROUP, rows, WIDE), BF)],
        compiler_params=params_of(),
        name="attend",
    )(me, *heads)


def side(ref, at, count=2):
    return jnp.concatenate([ref[at + i] for i in range(count)], axis=1)


def rows_of(ref, at):
    return jnp.concatenate([ref[p, at, :] for p in range(D // LANES)], axis=1)


def ff_kernel(
    pieces, me, in0, in1, in2, in3, x, vec, bias, whole,
    attended, hidden, normed, upper, active, out,
    wo, we, wr, parts, sems,
):
    load_matrix(whole, wo, 1, pieces, sems.at[0])
    load_matrix(whole, we, 2, pieces, sems.at[1])
    load_matrix(whole, wr, 3, pieces, sems.at[2])
    mine = place_of(me[0])
    for r, ref in enumerate((in0, in1, in2, in3)):
        parts[mine ^ TURN[r]] = ref[...]
    for g in range(GROUP):
        attended[:, g * WIDE : (g + 1) * WIDE] = parts[g]
    wait_all(wo, sems.at[0])
    for g in range(GROUP):
        cols = slice(g * WIDE, (g + 1) * WIDE)
        hidden[:, cols] = x[:, cols] + nn(attended[...], side(wo, 2 * g)) + vec[4:5, cols]
    hat, _ = norm_parts(hidden[...])
    normed[...] = (hat * vec[5:6, :] + vec[6:7, :]).astype(BF)
    out[...] = hidden[...] + vec[11:12, :]
    wait_all(we, sems.at[1])
    wait_all(wr, sems.at[2])

    def body(n, _):
        u = nn(normed[...], side(we, 2 * n)) + bias[n]
        upper[n] = u
        act = (0.5 * u * (1.0 + jnp.tanh(gelu_c * (u + gelu_a * u * u * u)))).astype(BF)
        active[n] = act
        out[...] += nn(act, rows_of(wr, pl.ds(pl.multiple_of(n * WIDE, WIDE), WIDE)))
        return 0

    lax.fori_loop(0, CHUNKS, body, 0)


def ff_call(plan, me, heads, x, vec, bias, whole):
    rows = x.shape[0]
    return pl.pallas_call(
        functools.partial(ff_kernel, plan.pieces),
        out_shape=[
            shape((rows, D), BF),
            shape((rows, D), F32),
            shape((rows, D), BF),
            shape((CHUNKS, rows, WIDE), F32),
            shape((CHUNKS, rows, WIDE), BF),
            shape((rows, D), F32),
        ],
        in_specs=[SM] + [VM] * 7 + [ANY],
        out_specs=[VM] * 6,
        scratch_shapes=[
            pltpu.VMEM((D // LANES, D, LANES), BF),
            pltpu.VMEM((FF // LANES, D, LANES), BF),
            pltpu.VMEM((D // LANES, FF, LANES), BF),
            pltpu.VMEM((GROUP, rows, WIDE), BF),
            pltpu.SemaphoreType.DMA((3,)),
        ],
        compiler_params=params_of(),
        name="ff",
    )(me, *heads, x, vec, bias, whole)


def ff_back_kernel(
    pieces, me, dy, upper, hidden, vec, whole,
    dyb, dub, dh, dhb, out0, out1, out2, out3, bias_grad, vec_grad,
    wo, we, wr, acc, parts, sems,
):
    load_matrix(whole, wr, 3, pieces, sems.at[2])
    load_matrix(whole, we, 2, pieces, sems.at[1])
    load_matrix(whole, wo, 1, pieces, sems.at[0])
    dyb[...] = dy[...].astype(BF)
    vec_grad[0:1, :] = jnp.sum(dy[...], axis=0, keepdims=True)
    acc[...] = jnp.zeros_like(acc)
    wait_all(wr, sems.at[2])
    wait_all(we, sems.at[1])

    def body(n, _):
        dg = nt(dyb[...], rows_of(wr, pl.ds(pl.multiple_of(n * WIDE, WIDE), WIDE)))
        u = upper[n]
        t = jnp.tanh(gelu_c * (u + gelu_a * u * u * u))
        slope = 0.5 * (1.0 + t) + 0.5 * u * (1.0 - t * t) * (gelu_c * (1.0 + 3.0 * gelu_a * u * u))
        du = dg * slope
        bias_grad[n] = jnp.sum(du, axis=0, keepdims=True)
        low = du.astype(BF)
        dub[n] = low
        acc[...] += nt(low, side(we, 2 * n))
        return 0

    lax.fori_loop(0, CHUNKS, body, 0)
    back, gain, shift = norm_back(hidden[...], vec[5:6, :], acc[...])
    total = dy[...] + back
    vec_grad[1:2, :] = gain
    vec_grad[2:3, :] = shift
    vec_grad[3:4, :] = jnp.sum(total, axis=0, keepdims=True)
    vec_grad[4:8, :] = jnp.zeros((4, D), F32)
    dh[...] = total
    dhb[...] = total.astype(BF)
    wait_all(wo, sems.at[0])
    for g in range(GROUP):
        parts[g] = nt(dhb[...], rows_of(wo, slice(g * WIDE, (g + 1) * WIDE))).astype(BF)
    mine = place_of(me[0])
    for r, out in enumerate((out0, out1, out2, out3)):
        out[...] = parts[mine ^ TURN[r]]


def ff_back_call(plan, me, dy, upper, hidden, vec, whole):
    rows = dy.shape[0]
    return pl.pallas_call(
        functools.partial(ff_back_kernel, plan.pieces),
        out_shape=[
            shape((rows, D), BF),
            shape((CHUNKS, rows, WIDE), BF),
            shape((rows, D), F32),
            shape((rows, D), BF),
        ]
        + [shape((rows, WIDE), BF)] * GROUP
        + [shape((CHUNKS, 1, WIDE), F32), shape((8, D), F32)],
        in_specs=[SM] + [VM] * 4 + [ANY],
        out_specs=[VM] * 10,
        scratch_shapes=[
            pltpu.VMEM((D // LANES, D, LANES), BF),
            pltpu.VMEM((FF // LANES, D, LANES), BF),
            pltpu.VMEM((D // LANES, FF, LANES), BF),
            pltpu.VMEM((rows, D), F32),
            pltpu.VMEM((GROUP, rows, WIDE), BF),
            pltpu.SemaphoreType.DMA((3,)),
        ],
        compiler_params=params_of(),
        name="ff_back",
    )(me, dy, upper, hidden, vec, whole)


def attend_back_kernel(
    me, in0, in1, in2, in3, do0, do1, do2, do3, lse,
    out0, out1, out2, out3, sums,
    q, k, v, do, dq, dk, dv,
):
    mine = place_of(me[0])
    rows = in0.shape[0]
    for r, (ref, grad) in enumerate(((in0, do0), (in1, do1), (in2, do2), (in3, do3))):
        at = pl.ds(pl.multiple_of((mine ^ TURN[r]) * rows, rows), rows)
        q[at, :] = ref[:, 0:WIDE]
        k[at, :] = ref[:, WIDE : 2 * WIDE]
        v[at, :] = ref[:, 2 * WIDE : 3 * WIDE]
        do[at, :] = grad[...]
    seen = diagonal(rows)
    for h in range(WIDE // HEAD):
        cols = slice(h * HEAD, (h + 1) * HEAD)
        total = jnp.zeros((1, HEAD), F32)
        for i in reversed(range(GROUP)):
            here = slice(i * rows, (i + 1) * rows)
            past = slice(0, i * rows)
            qi, doi, ls = q[here, cols], do[here, cols], lse[here, h : h + 1]
            near = jnp.exp(jnp.where(seen, nt(qi, k[here, cols]) * 0.125, -1000000000.0) - ls)
            dnear = nt(doi, v[here, cols])
            inner = jnp.sum(near * dnear, axis=1, keepdims=True)
            if i:
                far = jnp.exp(nt(qi, k[past, cols]) * 0.125 - ls)
                dfar = nt(doi, v[past, cols])
                inner = inner + jnp.sum(far * dfar, axis=1, keepdims=True)
            snear = (near * (dnear - inner) * 0.125).astype(BF)
            res = nn(snear, k[here, cols])
            dkn = tn(snear, qi)
            dvn = tn(near.astype(BF), doi)
            last = i == GROUP - 1
            dk[here, cols] = dkn if last else dk[here, cols] + dkn
            dv[here, cols] = dvn if last else dv[here, cols] + dvn
            if i:
                sfar = (far * (dfar - inner) * 0.125).astype(BF)
                res = res + nn(sfar, k[past, cols])
                dkf = tn(sfar, qi)
                dvf = tn(far.astype(BF), doi)
                dk[past, cols] = dkf if last else dk[past, cols] + dkf
                dv[past, cols] = dvf if last else dv[past, cols] + dvf
            total = total + jnp.sum(res, axis=0, keepdims=True)
            dq[i, :, cols] = res.astype(BF)
        sums[0:1, cols] = total
    sums[1:2, :] = jnp.sum(dv[...], axis=0, keepdims=True)
    sums[2:8, :] = jnp.zeros((6, WIDE), F32)
    for r, out in enumerate((out0, out1, out2, out3)):
        at = pl.ds(pl.multiple_of((mine ^ TURN[r]) * rows, rows), rows)
        out[:, 0:WIDE] = dq[mine ^ TURN[r]]
        out[:, WIDE : 2 * WIDE] = dk[at, :].astype(BF)
        out[:, 2 * WIDE : 3 * WIDE] = dv[at, :].astype(BF)


def attend_back_call(me, heads, grads, lse):
    rows = heads[0].shape[0]
    span = GROUP * rows
    return pl.pallas_call(
        attend_back_kernel,
        out_shape=[shape((rows, 3 * WIDE), BF)] * GROUP + [shape((8, WIDE), F32)],
        in_specs=[SM] + [VM] * 9,
        out_specs=[VM] * 5,
        scratch_shapes=[pltpu.VMEM((span, WIDE), BF)] * 4
        + [pltpu.VMEM((GROUP, rows, WIDE), BF)]
        + [pltpu.VMEM((span, WIDE), F32)] * 2,
        compiler_params=params_of(),
        name="attend_back",
    )(me, *heads, *grads, lse)


def qkv_back_kernel(pieces, me, in0, in1, in2, in3, dh, x, vec, whole, mixed, dx, vec_grad, weight, acc, sem):
    load_matrix(whole, weight, 0, pieces, sem)
    mine = place_of(me[0])
    for r, ref in enumerate((in0, in1, in2, in3)):
        mixed[mine ^ TURN[r]] = ref[...]
    acc[...] = jnp.zeros_like(acc)
    wait_all(weight, sem)

    for b in range(3 * GROUP):
        kind, at = b // GROUP, b % GROUP
        acc[...] += nt(mixed[at, :, kind * WIDE : (kind + 1) * WIDE], side(weight, 2 * b))
    back, gain, shift = norm_back(x[...].astype(F32), vec[0:1, :], acc[...])
    dx[...] = dh[...] + back
    vec_grad[0:1, :] = gain
    vec_grad[1:2, :] = shift
    vec_grad[2:8, :] = jnp.zeros((6, D), F32)


def qkv_back_call(plan, me, grads, dh, x, vec, whole):
    rows = x.shape[0]
    return pl.pallas_call(
        functools.partial(qkv_back_kernel, plan.pieces),
        out_shape=[shape((GROUP, rows, 3 * WIDE), BF), shape((rows, D), F32), shape((8, D), F32)],
        in_specs=[SM] + [VM] * 7 + [ANY],
        out_specs=[VM] * 3,
        scratch_shapes=[
            pltpu.VMEM((3 * D // LANES, D, LANES), BF),
            pltpu.VMEM((rows, D), F32),
            pltpu.SemaphoreType.DMA,
        ],
        compiler_params=params_of(),
        name="qkv_back",
    )(me, *grads, dh, x, vec, whole)


def weight_items(pieces, core):
    items = []
    for d in range(core, len(pieces), 2):
        for mat, k0, k1, base in pieces[d]:
            count, step = k1 - k0, PANELS[mat]
            k = k0
            while k < k1:
                n = min(WIDE - k % WIDE, k1 - k) if mat == 3 else k1 - k0
                if step == 2:
                    groups = [range(j, 4 * step, step) for j in range(step)]
                else:
                    groups = [range(2 * i, 2 * i + 2) for i in range(2 * step)]
                for group in groups:
                    low = base + group[0] % step * count + k - k0
                    items.append((low, d, mat, base - k0, count, k, n, group))
                k += n
    return items


def weight_part(items, own, other, out):
    normed1, attended, normed2, active, mixed, dhb, dub, dyb = zip(own, other)
    everything = slice(None)

    def both(pair, *at):
        return jnp.concatenate([ref[at] for ref in pair], axis=0)

    def panels(pair, group):
        return jnp.concatenate([both(pair, everything, slice(p * LANES, (p + 1) * LANES)) for p in group], axis=1)

    turned = {}
    for _, d, mat, base, count, k, n, group in items:
        if (d, mat, k) not in turned:
            if mat == 3:
                lhs = both(active, k // WIDE, everything, slice(k % WIDE, k % WIDE + n))
            else:
                lhs = both((normed1, attended, normed2)[mat], everything, slice(k, k + n))
            turned[d, mat, k] = lhs.T
        if mat == 0:
            at = group[0] // 2
            rhs = both(mixed, at % GROUP, everything, slice(at // GROUP * WIDE, (at // GROUP + 1) * WIDE))
        elif mat == 2:
            rhs = both(dub, group[0] // 2)
        else:
            rhs = panels(dhb if mat == 1 else dyb, group)
        res = nn(turned[d, mat, k], rhs).astype(BF)
        step = PANELS[mat]
        for i, p in enumerate(group):
            at = base + k + (p % step) * count
            out[p // step, d // 2, at : at + n, :] = res[:, i * LANES : (i + 1) * LANES]


def weight_kernel(pieces, me, *refs):
    for core in range(2):

        @pl.when(me[0] % 2 == core)
        def _(core=core):
            weight_part(weight_items(pieces, core), refs[:8], refs[8:16], refs[16])


def weight_call(plan, me, own, other):
    return pl.pallas_call(
        functools.partial(weight_kernel, plan.pieces),
        out_shape=shape((4, plan.n_dp // 2, plan.size, LANES), BF),
        in_specs=[SM] + [VM] * 16,
        out_specs=VM,
        compiler_params=params_of(),
        name="weight_grads",
    )(me, *own, *other)


def adam_parts(grad, moment, square, master, weight_decay):
    moment_next = beta_one * moment + (1.0 - beta_one) * grad
    square_next = beta_two * square + (1.0 - beta_two) * grad * grad
    corrected = moment_next / (1.0 - beta_one**STEP)
    scaled = square_next / (1.0 - beta_two**STEP)
    update = -rate * (corrected / (jnp.sqrt(scaled) + adam_eps) + weight_decay * master)
    return moment_next, square_next, update


def adam_kernel(plan, me, owned, master, moment, square, *refs):
    grad, moment_next, square_next, update = refs[-4:]
    for d, held in enumerate(plan.pieces):

        @pl.when(me[0] == d)
        def _(held=held):
            for mat, k0, k1, base in held:
                size, step = k1 - k0, PANELS[mat]
                for j in range(step):
                    grad[0, 0, pl.ds(base + j, size, stride=step), :] = owned[pl.ds(base + j * size, size), :]

    new = adam_parts(grad[0, 0], moment[0, 0], square[0, 0], master[0, 0], decay)
    moment_next[0, 0], square_next[0, 0], update[0, 0] = new


def adam_call(plan, me, layer, owned, master, moment, square, before):
    block = pl.BlockSpec((1, 1) + master.shape[2:], lambda i: (layer, 0, 0, 0))
    whole = pl.BlockSpec(owned.shape, lambda i: (0, 0))
    first = 5
    return pl.pallas_call(
        functools.partial(adam_kernel, plan),
        grid=(1,),
        out_shape=[shape(master.shape, F32)] * 4,
        in_specs=[SM, whole] + [block] * 3 + [ANY] * len(before),
        out_specs=[block] * 4,
        input_output_aliases={first + i: i for i in range(len(before))},
        compiler_params=params_of(),
        name="adam",
    )(me, owned, master, moment, square, *before)


class Wire:
    def __init__(self, send, recv):
        self.d, self.z = lax.axis_index("dp"), lax.axis_index("ctx")
        self.place = place_of(self.d)
        self.send, self.recv, self.next = send, recv, 0

    def copy(self, src, dst, d, z, at=None):
        slot = self.next
        self.next += 1
        return pltpu.make_async_remote_copy(
            src_ref=src, dst_ref=dst, send_sem=self.send.at[slot], recv_sem=self.recv.at[slot],
            device_id=(d, z), device_id_type=MESH,
        )

    def push(self, src, dst, flip_dp, flip_ctx):
        copy = self.copy(src, dst, self.d ^ flip_dp, self.z ^ flip_ctx)
        copy.start()
        return copy

    def greet(self, flips, swaps=False):
        barrier = pltpu.get_barrier_semaphore()
        for fd, fz in flips:
            pl.semaphore_signal(barrier, inc=1, device_id=(self.d ^ fd, self.z ^ fz), device_id_type=MESH)
        if not swaps:
            pl.semaphore_wait(barrier, len(flips))
            return

        @pl.when(self.place != self.z)
        def _():
            pl.semaphore_signal(barrier, inc=1, device_id=self.opposite(), device_id_type=MESH)
            pl.semaphore_wait(barrier, len(flips) + 1)

        @pl.when(self.place == self.z)
        def _():
            pl.semaphore_wait(barrier, len(flips))

    def opposite(self):
        return (self.d - self.d % GROUP + place_of(self.z), self.place)

    def swap(self, src, dst):
        copy = self.copy(src, dst, *self.opposite())

        @pl.when(self.place != self.z)
        def _():
            copy.start()

        @pl.when(self.place == self.z)
        def _():
            dst[...] = src[...]

        def finish():
            @pl.when(self.place != self.z)
            def _():
                copy.wait()

        return finish

    def post(self, blocks, into):
        base = self.next
        self.next += GROUP
        first = self.d - self.d % GROUP

        def copy(g, sender):
            return pltpu.make_async_remote_copy(
                src_ref=blocks.at[g], dst_ref=into.at[self.place],
                send_sem=self.send.at[base + g], recv_sem=self.recv.at[base + sender],
                device_id=(first + place_of(g), self.z), device_id_type=MESH,
            )

        def send(g):
            @pl.when(self.place != g)
            def _():
                copy(g, self.place).start()

            @pl.when(self.place == g)
            def _():
                into[g] = blocks[g]

        def finish():
            for r in range(1, GROUP):
                copy(0, self.place ^ r).wait_recv()
            for g in range(GROUP):

                @pl.when(self.place != g)
                def _(g=g):
                    copy(g, self.place).wait_send()

        return send, finish

    def trade(self, blocks, into):
        copies = []
        for r in (2, 3, 1):
            copies.append(self.push(blocks.at[self.place ^ TURN[r]], into.at[self.place], r, 0))
        into[self.place] = blocks[self.place]
        return copies


def drive(jobs, late):
    live = list(zip(jobs, late))
    step = 0
    while live:
        rest = []
        for job, wait in live:
            if step >= wait:
                try:
                    next(job)
                except StopIteration:
                    continue
                yield
            rest.append((job, wait))
        live = rest
        step += 1


def take(steps, count=1):
    for _ in range(count):
        next(steps, None)


def paced(steps, pace):
    owed = [0.0]

    def advance():
        owed[0] += pace
        while owed[0] >= 1.0:
            owed[0] -= 1.0
            next(steps, None)

    return advance


def unpack_vectors(raw, vec, n_dp, size):
    share = 12 * D // (4 * n_dp) // LANES
    per_row = D // LANES
    for d in range(n_dp):
        for z in range(4):
            lines = raw[z, d].astype(F32)
            for r in range(share):
                at = (d * 4 + z) * share + r
                col = at % per_row * LANES
                vec[at // per_row : at // per_row + 1, col : col + LANES] = lines[r : r + 1, :]


def qkv_part(wire, normed, weight, vec, blocks, heads, copies):
    for r in (2, 3, 1, 0):
        at = wire.place ^ TURN[r]
        cols = pl.ds(pl.multiple_of(at * WIDE, WIDE), WIDE)
        for kind in range(3):
            acc = nn(normed[...], side(weight, 2 * (kind * GROUP + at)))
            if kind != 1:
                row = 2 if kind == 0 else 3
                acc = acc + vec[row : row + 1, cols]
            blocks[at, :, kind * WIDE : (kind + 1) * WIDE] = acc.astype(BF)
            yield
        if r:
            copies.append(wire.push(blocks.at[at], heads.at[wire.place], r, 0))
        else:
            heads[at] = blocks[at]


def spread_heads(heads, q, k, v):
    rows = heads.shape[1]
    for g in range(GROUP):
        at = slice(g * rows, (g + 1) * rows)
        q[at, :] = heads[g, :, 0:WIDE]
        k[at, :] = heads[g, :, WIDE : 2 * WIDE]
        v[at, :] = heads[g, :, 2 * WIDE : 3 * WIDE]


def attend_part(q, k, v, o, lse, send):
    rows = o.shape[1]
    seen = diagonal(rows)
    for i in reversed(range(GROUP)):
        for h in range(WIDE // HEAD):
            cols = slice(h * HEAD, (h + 1) * HEAD)
            here = slice(i * rows, (i + 1) * rows)
            qi = q[here, cols]
            near = jnp.where(seen, nt(qi, k[here, cols]) * 0.125, -1000000000.0)
            top = jnp.max(near, axis=1, keepdims=True)
            if i:
                far = nt(qi, k[0 : i * rows, cols]) * 0.125
                top = jnp.maximum(top, jnp.max(far, axis=1, keepdims=True))
                far = jnp.exp(far - top)
            near = jnp.exp(near - top)
            total = jnp.sum(near, axis=1, keepdims=True)
            if i:
                total = total + jnp.sum(far, axis=1, keepdims=True)
            inv = 1.0 / total
            res = nn((near * inv).astype(BF), v[here, cols])
            if i:
                res = res + nn((far * inv).astype(BF), v[0 : i * rows, cols])
            o[i, :, cols] = res.astype(BF)
            lse[here, h : h + 1] = top + jnp.log(total)
            yield
        send(i)


def ff_part(x, parts, vec, weights, wr_rows, sems, attended, hidden, normed, upper, active, out):
    wo, we, wr = weights
    for g in range(GROUP):
        attended[:, g * WIDE : (g + 1) * WIDE] = parts[g]
    wait_all(wo, sems[0])
    for g in range(GROUP):
        cols = slice(g * WIDE, (g + 1) * WIDE)
        hidden[:, cols] = x[:, cols].astype(F32) + nn(attended[...], side(wo, 2 * g)) + vec[4:5, cols]
        yield
    hat, _ = norm_parts(hidden[...])
    normed[...] = (hat * vec[5:6, :] + vec[6:7, :]).astype(BF)
    out[...] = hidden[...] + vec[11:12, :]
    wait_all(we, sems[1])
    wait_all(wr, sems[2])
    yield
    for n in range(CHUNKS):
        row, col = 7 + n // GROUP, n % GROUP * WIDE
        u = nn(normed[...], side(we, 2 * n)) + vec[row : row + 1, col : col + WIDE]
        upper[n] = u
        act = (0.5 * u * (1.0 + jnp.tanh(gelu_c * (u + gelu_a * u * u * u)))).astype(BF)
        active[n] = act
        out[...] += nn(act, wr_rows(n))
        yield


def ring_reader(upper, ring, sems):
    def fetch(n):
        return pltpu.make_async_copy(upper.at[n], ring.at[n % 2], sems[n % 2])

    fetch(0).start()

    def read(n):
        if n + 1 < CHUNKS:
            fetch(n + 1).start()
        fetch(n).wait()
        return ring[n % 2]

    return read


def ff_back_part(dy, read_upper, hidden, vec, weights, sems, dyb, dub, dh, dhb, blocks, acc, bias_grad, vec_grad):
    wo, we, wr = weights
    dyb[...] = dy[...].astype(BF)
    vec_grad[0:1, :] = jnp.sum(dy[...].astype(F32), axis=0, keepdims=True)
    acc[...] = jnp.zeros_like(acc)
    if sems:
        wait_all(wr, sems[2])
        wait_all(we, sems[1])
    for n in range(CHUNKS):
        at = n * WIDE % D
        dg = nt(dyb[...], side_rows(wr, n * WIDE // D, slice(at, at + WIDE)))
        u = read_upper(n)
        t = jnp.tanh(gelu_c * (u + gelu_a * u * u * u))
        slope = 0.5 * (1.0 + t) + 0.5 * u * (1.0 - t * t) * (gelu_c * (1.0 + 3.0 * gelu_a * u * u))
        du = dg * slope
        row, col = n // GROUP, n % GROUP * WIDE
        bias_grad[row : row + 1, col : col + WIDE] = jnp.sum(du, axis=0, keepdims=True)
        low = du.astype(BF)
        dub[n] = low
        acc[...] += nt(low, side(we, 2 * n))
        yield
    back, gain, shift = norm_back(hidden[...], vec[5:6, :], acc[...])
    total = dy[...].astype(F32) + back
    vec_grad[1:2, :] = gain
    vec_grad[2:3, :] = shift
    vec_grad[3:4, :] = jnp.sum(total, axis=0, keepdims=True)
    dh[...] = total
    dhb[...] = total.astype(BF)
    if sems:
        wait_all(wo, sems[0])
    yield
    for g in range(GROUP):
        blocks[g] = nt(dhb[...], rows_of(wo, slice(g * WIDE, (g + 1) * WIDE))).astype(BF)
    yield


def side_rows(ref, at, rows):
    return jnp.concatenate([ref[p * 4 + at, rows, :] for p in range(D // LANES)], axis=1)


def attend_back_part(q, k, v, do, lse, dm, dk, dv, sums, send):
    rows = dm.shape[1]
    seen = diagonal(rows)
    sums[...] = jnp.zeros_like(sums)
    for i in reversed(range(GROUP)):
        here = slice(i * rows, (i + 1) * rows)
        past = slice(0, i * rows)
        last = i == GROUP - 1
        for h in range(WIDE // HEAD):
            cols = slice(h * HEAD, (h + 1) * HEAD)
            qi, doi, ls = q[here, cols], do[i, :, cols], lse[here, h : h + 1]
            near = jnp.exp(jnp.where(seen, nt(qi, k[here, cols]) * 0.125, -1000000000.0) - ls)
            dnear = nt(doi, v[here, cols])
            inner = jnp.sum(near * dnear, axis=1, keepdims=True)
            if i:
                far = jnp.exp(nt(qi, k[past, cols]) * 0.125 - ls)
                dfar = nt(doi, v[past, cols])
                inner = inner + jnp.sum(far * dfar, axis=1, keepdims=True)
            snear = (near * (dnear - inner) * 0.125).astype(BF)
            res = nn(snear, k[here, cols])
            dkn = tn(snear, qi)
            dvn = tn(near.astype(BF), doi)
            dk[here, cols] = dkn if last else dk[here, cols] + dkn
            dv[here, cols] = dvn if last else dv[here, cols] + dvn
            if i:
                sfar = (far * (dfar - inner) * 0.125).astype(BF)
                res = res + nn(sfar, k[past, cols])
                dkf = tn(sfar, qi)
                dvf = tn(far.astype(BF), doi)
                dk[past, cols] = dkf if last else dk[past, cols] + dkf
                dv[past, cols] = dvf if last else dv[past, cols] + dvf
            sums[0:1, cols] += jnp.sum(res, axis=0, keepdims=True)
            dm[i, :, cols] = res.astype(BF)
            yield
        dm[i, :, WIDE : 2 * WIDE] = dk[here, :].astype(BF)
        dm[i, :, 2 * WIDE : 3 * WIDE] = dv[here, :].astype(BF)
        sums[1:2, :] += jnp.sum(dv[here, :], axis=0, keepdims=True)
        send(i)


def qkv_back_part(mixed, weight, acc):
    for b in range(3 * GROUP):
        kind, at = b // GROUP, b % GROUP
        acc[...] += nt(mixed[at, :, kind * WIDE : (kind + 1) * WIDE], side(weight, 2 * b))
        yield


class Mover:
    def __init__(self, n_dp):
        self.n_dp = n_dp
        self.size, self.pieces = pieces_of(n_dp)
        self.line = 12 * D // (4 * n_dp)
        self.span = self.size + 16

    def gather_all(self, helds):
        wholes = [lax.all_gather(held, ("ctx", "dp"), axis=0, tiled=True) for held in helds]
        return [whole.reshape(4, self.n_dp, self.span, LANES) for whole in wholes]

    def vectors(self, whole):
        rows = -(-self.line // LANES)
        lines = whole[:, :, self.size : self.size + rows].reshape(4, self.n_dp, -1)[:, :, : self.line]
        return lines.transpose(1, 0, 2).reshape(12, D).astype(F32)

    def scatter(self, buffer):
        none = jnp.zeros_like(buffer)
        core = lax.axis_index("dp") % 2
        pair = jnp.stack([jnp.where(core == 0, buffer, none), jnp.where(core == 1, buffer, none)], axis=2)
        flat = pair.reshape(-1, LANES)
        return lax.psum_scatter(flat, ("ctx", "dp"), scatter_dimension=0, tiled=True).astype(F32)

    def scatter_vectors(self, grads):
        return lax.psum_scatter(grads.reshape(-1), ("dp", "ctx"), scatter_dimension=0, tiled=True)


CORE = 1
FLIPS = ((1, 0), (2, 0), (3, 0), (4, 0), (0, 1), (0, 2), (0, 3))


class BitMover(Mover):
    def __init__(self, n_dp):
        super().__init__(n_dp)
        self.gap, self.pace, self.pace_back = 5, (1.3, 4, 2), (1.5, 4, 2, 2)
        self.even = self.cut(((4, 4), (2, 2), (4, 4), (2, 2), (4, 4), (2, 2), (4, 4), (2, 2)))
        self.skew = self.cut(((5, 3), (3, 1), (5, 2), (3, 2), (5, 3), (3, 1), (5, 2), (3, 2)))

    def cut(self, plan):
        unit, row, chunks = self.size // 48, 0, []
        for i, pair in enumerate(plan):
            for units, (a, b) in zip(pair, ((2, 4), (4, 2))):
                chunks.append((row, units * unit, (i % 2 == 0, a, b), i // 2))
                row += units * unit
        return chunks

    def gather_jobs(self, wire, local, helds, wholes, plans, done):
        d, z = wire.d, wire.z

        def job(layer, part):
            low, size, (z_first, a, b), _ = plans[layer][part]
            if part == len(plans[layer]) - 1:
                size = self.span - low
            rows = pl.ds(low, size)
            held, whole = helds[layer].at[rows], wholes[layer]
            started = []

            def push(src, dst, fd, fz):
                started.append(wire.push(src, dst, fd, fz))
                return started[-1]

            def line(dd, fd):
                ref = whole.at[:, dd, rows]
                return push(ref, ref, fd, 0)

            own = pltpu.make_async_copy(held, whole.at[z, d, rows], local.at[layer * len(plans[0]) + part])
            own.start()
            mine = [push(held, whole.at[z, d, rows], 0, k) for k in (3, 2, 1)]
            if z_first:
                yield
                own.wait()
                for copy in mine:
                    copy.wait_recv()
                first = line(d, a)
                second = line(d, b)
                cores = [line(d, CORE)]
                yield
                first.wait_recv()
                third = line(d ^ a, b)
                cores.append(line(d ^ a, CORE))
                yield
                second.wait_recv()
                cores.append(line(d ^ b, CORE))
                yield
                third.wait_recv()
                cores.append(line(d ^ a ^ b, CORE))
            else:
                first = push(held, whole.at[z, d, rows], a, 0)
                yield
                first.wait_recv()
                other = whole.at[z, d ^ a, rows]
                theirs = [push(other, other, 0, k) for k in (3, 2, 1)]
                yield
                own.wait()
                for copy in mine:
                    copy.wait_recv()
                second = line(d, b)
                cores = [line(d, CORE)]
                yield
                for copy in theirs:
                    copy.wait_recv()
                third = line(d ^ a, b)
                cores.append(line(d ^ a, CORE))
                yield
                second.wait_recv()
                cores.append(line(d ^ b, CORE))
                yield
                third.wait_recv()
                cores.append(line(d ^ a ^ b, CORE))
            yield
            for copy in cores:
                copy.wait_recv()
            for copy in started:
                copy.wait_send()
            done[layer] += 1

        jobs = [job(layer, part) for layer, plan in enumerate(plans) for part in range(len(plan))]
        return drive(jobs, [chunk[3] + self.gap * layer for layer, plan in enumerate(plans) for chunk in plan])

    def forward_first(self, helds, tokens):
        rows = tokens.shape[0]
        span = GROUP * rows
        plans = (self.even, self.skew)
        pieces, count, pace = self.pieces, len(self.even), self.pace
        slots = 2 * count * 14 + 16

        def kernel(
            held0, held1, tokens,
            whole0, whole1, value, vec, normed1, heads_out, lse, attended, hidden, normed2, upper, active, out,
            swapped, heads, blocks, q, k, v, o, parts, raw, wa, wo, we, wr, local, sems, send, recv,
        ):
            wire = Wire(send, recv)
            wire.greet(FLIPS, swaps=True)
            done = [0, 0]
            comm = self.gather_jobs(wire, local, (held0, held1), (whole0, whole1), plans, done)
            take(comm, 6)
            swap_in = wire.swap(tokens, swapped)
            while done[0] < count:
                next(comm)
            load_vec = pltpu.make_async_copy(whole0.at[:, :, pl.ds(self.size, 16)], raw, sems.at[4])
            load_vec.start()
            load_matrix(whole0, wa, 0, pieces, sems.at[3])
            load_matrix(whole0, wo, 1, pieces, sems.at[0])
            swap_in()
            value[...] = swapped[...]
            load_vec.wait()
            unpack_vectors(raw, vec, self.n_dp, self.size)
            hat, _ = norm_parts(swapped[...].astype(F32))
            normed1[...] = (hat * vec[0:1, :] + vec[1:2, :]).astype(BF)
            wait_all(wa, sems.at[3])
            advance = paced(comm, pace[0])
            copies = []
            for _ in qkv_part(wire, normed1, wa, vec, blocks, heads, copies):
                advance()
            load_matrix(whole0, we, 2, pieces, sems.at[1])
            load_matrix(whole0, wr, 3, pieces, sems.at[2])
            take(comm, pace[1])
            for copy in copies:
                copy.wait()
            spread_heads(heads, q, k, v)
            heads_out[...] = heads[...]
            send_o, finish = wire.post(o, parts)
            for _ in attend_part(q, k, v, o, lse, send_o):
                advance()
            take(comm, pace[2])
            finish()
            for _ in ff_part(
                swapped, parts, vec, (wo, we, wr), lambda n: rows_of(wr, slice(n * WIDE, (n + 1) * WIDE)), [sems.at[i] for i in range(3)],
                attended, hidden, normed2, upper, active, out,
            ):
                advance()
            for _ in comm:
                pass

        return pl.pallas_call(
            kernel,
            out_shape=[shape((4, self.n_dp, self.span, LANES), BF)] * 2
            + [
                shape((rows, D), BF),
                shape((12, D), F32),
                shape((rows, D), BF),
                shape((GROUP, rows, 3 * WIDE), BF),
                shape((span, LANES), F32),
                shape((rows, D), BF),
                shape((rows, D), F32),
                shape((rows, D), BF),
                shape((CHUNKS, rows, WIDE), F32),
                shape((CHUNKS, rows, WIDE), BF),
                shape((rows, D), F32),
            ],
            in_specs=[VM] * 3,
            out_specs=[ANY] * 2 + [VM] * 11,
            scratch_shapes=[pltpu.VMEM((rows, D), BF)]
            + [pltpu.VMEM((GROUP, rows, 3 * WIDE), BF)] * 2
            + [pltpu.VMEM((span, WIDE), BF)] * 3
            + [pltpu.VMEM((GROUP, rows, WIDE), BF)] * 2
            + [
                pltpu.VMEM((4, self.n_dp, 16, LANES), BF),
                pltpu.VMEM((3 * D // LANES, D, LANES), BF),
                pltpu.VMEM((D // LANES, D, LANES), BF),
                pltpu.VMEM((FF // LANES, D, LANES), BF),
                pltpu.VMEM((D // LANES, FF, LANES), BF),
                pltpu.SemaphoreType.DMA((2 * count,)),
                pltpu.SemaphoreType.DMA((5,)),
                pltpu.SemaphoreType.DMA((slots,)),
                pltpu.SemaphoreType.DMA((slots,)),
            ],
            compiler_params=params_of(collective_id=1, has_side_effects=True),
            name="forward_first",
        )(*helds, tokens)

    def scatter_jobs(self, wire, parts):
        d, z = wire.d, wire.z

        def job(grads, acc, from_b, from_a, from_z, order, size, put, local):
            z_first, a, b = order
            started = []

            def push(src, dst, fd, fz):
                started.append(wire.push(src, dst, fd, fz))
                return started[-1]

            places = [(d ^ (ja * a)) // 2 for ja in (1, 0)]
            if acc is None:
                piece = [lambda k, p=p: grads.at[k, p] for p in places]
                pieces = [grads.at[:, p] for p in places]
            else:
                piece = [lambda k, i=i: acc.at[i, k] for i in range(2)]
                pieces = [acc.at[i] for i in range(2)]
            block = min(64, size)

            def add(into, more):
                def body(i, _):
                    at = pl.ds(pl.multiple_of(i * block, block), block)
                    for x, y in zip(into, more):
                        x[at, :] = x[at, :] + y[at, :]
                    return 0

                lax.fori_loop(0, size // block, body, 0)

            def every(i, more):
                add([piece[i](k) for k in range(4)], [more(k) for k in range(4)])

            to_b = [push(grads.at[:, p ^ (b // 2)], from_b.at[i], b, 0) for i, p in enumerate(places)]
            loads = []
            if acc is not None:
                for i in range(2):
                    loads.append(pltpu.make_async_copy(grads.at[:, places[i]], acc.at[i], local[i]))
                    loads[-1].start()
            yield
            for load in loads:
                load.wait()
            to_b[0].wait_recv()
            every(0, lambda k: from_b.at[0, k])
            if z_first:
                to_a = push(pieces[0], from_a, a, 0)
                yield
                to_b[1].wait_recv()
                every(1, lambda k: from_b.at[1, k])
                yield
                to_a.wait_recv()
                every(1, lambda k: from_a.at[k])
                to_z = [push(piece[1](z ^ k), from_z.at[k - 1, 0], 0, k) for k in (3, 2, 1)]
                yield
                more = [from_z.at[k, 0] for k in range(3)]
                last = to_z
            else:
                to_z = [push(piece[0](z ^ k), from_z.at[k - 1, 0], 0, k) for k in (3, 2, 1)]
                yield
                to_b[1].wait_recv()
                every(1, lambda k: from_b.at[1, k])
                to_z1 = [push(piece[1](z ^ k), from_z.at[k - 1, 1], 0, k) for k in (3, 2, 1)]
                yield
                for copy in to_z:
                    copy.wait_recv()
                for k in range(3):
                    add([piece[0](z)], [from_z.at[k, 0]])
                to_a = push(piece[0](z), from_a.at[0], a, 0)
                yield
                more = [from_z.at[k, 1] for k in range(3)] + [from_a.at[0]]
                last = to_z1 + [to_a]
            for copy in last:
                copy.wait_recv()

            def body(i, _):
                at = pl.multiple_of(i * block, block)
                here = pl.ds(at, block)
                value = piece[1](z)[here, :].astype(F32)
                for ref in more:
                    value = value + ref[here, :].astype(F32)
                put(at, block, value)
                return 0

            lax.fori_loop(0, size // block, body, 0)
            for copy in started:
                copy.wait_send()

        return [job(*part) for part in parts]

    def scatter_scratch(self, plan, with_acc):
        result = []
        for _, n, order, _ in plan:
            if with_acc:
                result.append(pltpu.VMEM((2, 4, n, LANES), BF))
            result.append(pltpu.VMEM((2, 4, n, LANES), BF))
            result.append(pltpu.VMEM((4 if order[0] else 1, n, LANES), BF))
            result.append(pltpu.VMEM((3, 1 if order[0] else 2, n, LANES), BF))
        return result

    def scatter_parts(self, plan, grads, scratch, owned, local):
        each = len(scratch) // len(plan)
        parts = []
        for i, (low, n, order, _) in enumerate(plan):
            refs = scratch[i * each : (i + 1) * each]
            acc, (from_b, from_a, from_z) = (refs[0] if each == 4 else None), refs[-3:]

            def put(at, block, value, low=low):
                owned[pl.ds(low + at, block), :] = value

            waits = [local.at[2 * i], local.at[2 * i + 1]] if each == 4 else None
            parts.append((grads.at[:, :, pl.ds(low, n)], acc, from_b, from_a, from_z, order, n, put, waits))
        return parts

    def backward_first(self, me, grads, saved, dy, vec, whole):
        x, normed1, heads, lse, attended, hidden, normed2, upper, active = saved
        rows = x.shape[0]
        span = GROUP * rows
        plan, pieces, pace = self.skew, self.pieces, self.pace_back
        count = len(plan)
        slots = count * 12 + 24
        scratch_count = 4 * count

        def kernel(
            grads, x, normed1, heads, lse, attended, hidden, normed2, upper, active, dy, vec, whole,
            owned, dx, dyb, dub, dhb, mixed, bias_grad, vec_grad, sums,
            o_normed1, o_attended, o_normed2, o_active, o_mixed, o_dhb, o_dub, o_dyb,
            *scratch,
        ):
            bufs = scratch[:scratch_count]
            q, k, v, do, blocks, dk, dv, dm, acc, dh, ring, wo, we, wr, local, sems, send, recv = scratch[scratch_count:]
            sems = [sems.at[i] for i in range(8)]
            load_matrix(whole, wr, 3, pieces, sems[2], split=True)
            load_matrix(whole, we, 2, pieces, sems[1])
            load_matrix(whole, wo, 1, pieces, sems[0])
            for g in range(GROUP):
                for i, ref in enumerate((q, k, v)):
                    pltpu.make_async_copy(
                        heads.at[g, :, pl.ds(i * WIDE, WIDE)], ref.at[pl.ds(g * rows, rows)], sems[5]
                    ).start()
            wire = Wire(send, recv)
            wire.greet(FLIPS)
            comm = drive(
                self.scatter_jobs(wire, self.scatter_parts(plan, grads, bufs, owned, local)), [chunk[3] for chunk in plan]
            )
            advance = paced(comm, pace[0])
            take(comm, pace[1])
            core = [wire.push(a, b, CORE, 0) for a, b in (
                (normed1, o_normed1), (attended, o_attended), (normed2, o_normed2), (active, o_active))]
            vec_grad[...] = jnp.zeros_like(vec_grad)
            read_upper = ring_reader(upper, ring, sems[3:5])
            for _ in ff_back_part(
                dy, read_upper, hidden, vec, (wo, we, wr), sems, dyb, dub, dh, dhb, blocks, acc, bias_grad, vec_grad
            ):
                advance()
            load_matrix(whole, wr, 0, pieces, sems[6])
            core += [wire.push(a, b, CORE, 0) for a, b in ((dyb, o_dyb), (dub, o_dub), (dhb, o_dhb))]
            copies = wire.trade(blocks, do)
            take(comm, pace[2])
            for ref in (q, k, v):
                wait_all(ref, sems[5])
            for copy in copies:
                copy.wait()
            send_m, finish = wire.post(dm, mixed)
            for _ in attend_back_part(q, k, v, do, lse, dm, dk, dv, sums, send_m):
                advance()
            acc[...] = jnp.zeros_like(acc)
            take(comm, pace[3])
            finish()
            core.append(wire.push(mixed, o_mixed, CORE, 0))
            wait_all(wr.at[pl.ds(0, 3 * D // LANES)], sems[6])
            for _ in qkv_back_part(mixed, wr, acc):
                advance()
            back, gain, shift = norm_back(x[...].astype(F32), vec[0:1, :], acc[...])
            dx[...] = dh[...] + back
            vec_grad[4:5, :] = gain
            vec_grad[5:6, :] = shift
            for _ in comm:
                pass
            for copy in core:
                copy.wait()

        token = shape((rows, D), BF)
        wide = shape((CHUNKS, rows, WIDE), BF)
        triple = shape((GROUP, rows, 3 * WIDE), BF)
        return pl.pallas_call(
            kernel,
            out_shape=[
                shape((self.size, LANES), F32),
                shape((rows, D), F32),
                token,
                wide,
                token,
                triple,
                shape((4, D), F32),
                shape((8, D), F32),
                shape((8, WIDE), F32),
            ]
            + [token, token, token, wide, triple, token, wide, token],
            in_specs=[ANY, VM, ANY, ANY, VM, ANY, VM, ANY, ANY, ANY, VM, VM, ANY],
            out_specs=[VM] * 9 + [ANY] * 8,
            scratch_shapes=self.scatter_scratch(plan, True)
            + [pltpu.VMEM((span, WIDE), BF)] * 3
            + [pltpu.VMEM((GROUP, rows, WIDE), BF)] * 2
            + [pltpu.VMEM((span, WIDE), F32)] * 2
            + [
                pltpu.VMEM((GROUP, rows, 3 * WIDE), BF),
                pltpu.VMEM((rows, D), F32),
                pltpu.VMEM((rows, D), F32),
                pltpu.VMEM((2, rows, WIDE), F32),
                pltpu.VMEM((D // LANES, D, LANES), BF),
                pltpu.VMEM((FF // LANES, D, LANES), BF),
                pltpu.VMEM((4 * D // LANES, D, LANES), BF),
                pltpu.SemaphoreType.DMA((2 * count,)),
                pltpu.SemaphoreType.DMA((8,)),
                pltpu.SemaphoreType.DMA((slots,)),
                pltpu.SemaphoreType.DMA((slots,)),
            ],
            compiler_params=params_of(collective_id=2, has_side_effects=True),
            name="backward_first",
        )(grads, x, normed1, heads, lse, attended, hidden, normed2, upper, active, dy, vec, whole)

    def middle(self, x, cotangent, vec, whole):
        rows = x.shape[0]
        span = GROUP * rows
        pieces = self.pieces
        slots = 40

        def kernel(
            x, cotangent, vec, whole,
            output, dx, normed1, attended, normed2, active, mixed, dhb, dub, dyb,
            o_normed1, o_attended, o_normed2, o_active, o_mixed, o_dhb, o_dub, o_dyb, bias_grad, vec_grad, sums,
            dy, result, returned, heads, blocks, q, k, v, o, parts, do, lse, hidden, upper, acc, dh, dk, dv, wa, wo, we, wr,
            sems, send, recv,
        ):
            sems = [sems.at[i] for i in range(4)]
            load_matrix(whole, wa, 0, pieces, sems[3])
            load_matrix(whole, wo, 1, pieces, sems[0])
            wire = Wire(send, recv)
            hat, _ = norm_parts(x[...])
            normed1[...] = (hat * vec[0:1, :] + vec[1:2, :]).astype(BF)
            wire.greet(FLIPS, swaps=True)
            wait_all(wa, sems[3])
            copies = []
            for _ in qkv_part(wire, normed1, wa, vec, blocks, heads, copies):
                pass
            load_matrix(whole, we, 2, pieces, sems[1])
            load_matrix(whole, wr, 3, pieces, sems[2], split=True)
            core = [wire.push(normed1, o_normed1, CORE, 0)]
            for copy in copies:
                copy.wait()
            swap_in = wire.swap(cotangent, dy)
            spread_heads(heads, q, k, v)
            send_o, finish = wire.post(o, parts)
            for _ in attend_part(q, k, v, o, lse, send_o):
                pass
            finish()
            for _ in ff_part(
                x, parts, vec, (wo, we, wr), lambda n: side_rows(wr, n // GROUP, slice(n % GROUP * WIDE, (n % GROUP + 1) * WIDE)),
                sems, attended, hidden, normed2, upper, active, dx,
            ):
                pass
            core += [wire.push(a, b, CORE, 0) for a, b in (
                (attended, o_attended), (normed2, o_normed2), (active, o_active))]
            result[...] = dx[...].astype(BF)
            swap_out = wire.swap(result, returned)
            swap_in()
            vec_grad[...] = jnp.zeros_like(vec_grad)
            for _ in ff_back_part(
                dy, lambda n: upper[n], hidden, vec, (wo, we, wr), None, dyb, dub, dh, dhb, o, acc, bias_grad, vec_grad
            ):
                pass
            copies = wire.trade(o, do)
            core += [wire.push(a, b, CORE, 0) for a, b in ((dyb, o_dyb), (dub, o_dub), (dhb, o_dhb))]
            for copy in copies:
                copy.wait()
            send_m, finish = wire.post(blocks, mixed)
            for _ in attend_back_part(q, k, v, do, lse, blocks, dk, dv, sums, send_m):
                pass
            acc[...] = jnp.zeros_like(acc)
            finish()
            core.append(wire.push(mixed, o_mixed, CORE, 0))
            for _ in qkv_back_part(mixed, wa, acc):
                pass
            back, gain, shift = norm_back(x[...], vec[0:1, :], acc[...])
            dx[...] = dh[...] + back
            vec_grad[4:5, :] = gain
            vec_grad[5:6, :] = shift
            swap_out()
            output[...] = returned[...]
            for copy in core:
                copy.wait()

        token = shape((rows, D), BF)
        wide = shape((CHUNKS, rows, WIDE), BF)
        triple = shape((GROUP, rows, 3 * WIDE), BF)
        kept = [token, token, token, wide, triple, token, wide, token]
        return pl.pallas_call(
            kernel,
            out_shape=[token, shape((rows, D), F32)] + kept * 2
            + [shape((4, D), F32), shape((8, D), F32), shape((8, WIDE), F32)],
            in_specs=[VM, VM, VM, ANY],
            out_specs=[VM] * 10 + [ANY] * 8 + [VM] * 3,
            scratch_shapes=[pltpu.VMEM((rows, D), BF)] * 3
            + [pltpu.VMEM((GROUP, rows, 3 * WIDE), BF)] * 2
            + [pltpu.VMEM((span, WIDE), BF)] * 3
            + [pltpu.VMEM((GROUP, rows, WIDE), BF)] * 3
            + [
                pltpu.VMEM((span, LANES), F32),
                pltpu.VMEM((rows, D), F32),
                pltpu.VMEM((CHUNKS, rows, WIDE), F32),
                pltpu.VMEM((rows, D), F32),
                pltpu.VMEM((rows, D), F32),
                pltpu.VMEM((span, WIDE), F32),
                pltpu.VMEM((span, WIDE), F32),
                pltpu.VMEM((3 * D // LANES, D, LANES), BF),
                pltpu.VMEM((D // LANES, D, LANES), BF),
                pltpu.VMEM((FF // LANES, D, LANES), BF),
                pltpu.VMEM((4 * D // LANES, D, LANES), BF),
                pltpu.SemaphoreType.DMA((4,)),
                pltpu.SemaphoreType.DMA((slots,)),
                pltpu.SemaphoreType.DMA((slots,)),
            ],
            compiler_params=params_of(collective_id=4, has_side_effects=True),
            name="middle",
        )(x, cotangent, vec, whole)

    def scatter_first(self, own, other, vectors0, vectors1):
        plan, pieces, thirds = self.even, self.pieces, self.size // 3
        count = len(plan)
        slots = count * 12 + 24
        scratch_count = 3 * count

        def kernel(*refs):
            own, other, vectors, (owned, vec_owned) = refs[:8], refs[8:16], (refs[16:19], refs[19:22]), refs[22:24]
            scratch = refs[24:]
            bufs = scratch[:scratch_count]
            grads, lines, got, small, from_b, from_a, from_z, send, recv = scratch[scratch_count:]
            wire = Wire(send, recv)
            wire.greet([flip for flip in FLIPS if flip[0] != 3])
            mine = pl.ds(pl.multiple_of(wire.place * WIDE, WIDE), WIDE)
            for i, (bias_grad, vec_grad, sums) in enumerate(vectors):
                lines[i, 0:2, :] = vec_grad[4:6, :]
                lines[i, 2:4, :] = jnp.zeros((2, D), F32)
                lines[i, 2:4, mine] = sums[0:2, :]
                lines[i, 4:5, :] = vec_grad[3:4, :]
                lines[i, 5:7, :] = vec_grad[1:3, :]
                lines[i, 7:11, :] = bias_grad[...]
                lines[i, 11:12, :] = vec_grad[0:1, :]
            trade = wire.push(lines, got, CORE, 0)

            def make(group):
                for core in range(2):
                    items = [item for item in weight_items(pieces, core) if item[0] // thirds == group]

                    @pl.when(wire.d % 2 == core)
                    def _(items=items):
                        weight_part(items, own, other, grads)

            def put(at, block, value):
                vec_owned[pl.ds(at, block), :] = value

            parts = self.scatter_parts(plan, grads, bufs, owned, None)
            jobs = self.scatter_jobs(wire, parts)
            made = [0]

            def after(job, rows):
                while made[0] * thirds < rows:
                    make(made[0])
                    made[0] += 1
                yield from job

            jobs = [after(job, low + n) for job, (low, n, _, _) in zip(jobs, plan)]

            def vector_job():
                trade.wait()
                lines[...] = lines[...] + got[...]
                share, per_row = self.line // LANES, D // LANES
                small[...] = jnp.zeros_like(small)
                for core in range(2):

                    @pl.when(wire.d % 2 == core)
                    def _(core=core):
                        for d in range(core, self.n_dp, 2):
                            for z in range(4):
                                for r in range(share):
                                    at = (d * 4 + z) * share + r
                                    row, col = at // per_row, at % per_row * LANES
                                    for i in range(2):
                                        here = slice(i * 4 + r, i * 4 + r + 1)
                                        small[z, d // 2, here, :] = lines[i, row : row + 1, col : col + LANES]

                yield from self.scatter_jobs(wire, [(small, None, from_b, from_a, from_z, (True, 2, 4), 8, put, None)])[0]

            jobs.append(vector_job())
            for _ in drive(jobs, [chunk[3] for chunk in plan] + [1]):
                pass

        return pl.pallas_call(
            kernel,
            out_shape=[shape((self.size, LANES), F32), shape((8, LANES), F32)],
            in_specs=[VM] * 22,
            out_specs=[VM] * 2,
            scratch_shapes=self.scatter_scratch(plan, False)
            + [
                pltpu.VMEM((4, self.n_dp // 2, self.size, LANES), BF),
                pltpu.VMEM((2, 12, D), F32),
                pltpu.VMEM((2, 12, D), F32),
                pltpu.VMEM((4, self.n_dp // 2, 8, LANES), F32),
                pltpu.VMEM((2, 4, 8, LANES), F32),
                pltpu.VMEM((4, 8, LANES), F32),
                pltpu.VMEM((3, 1, 8, LANES), F32),
                pltpu.SemaphoreType.DMA((slots,)),
                pltpu.SemaphoreType.DMA((slots,)),
            ],
            compiler_params=params_of(collective_id=3, has_side_effects=True),
            name="scatter_first",
        )(*own, *other, *vectors0, *vectors1)


def swap(values, n_dp):
    pairs = [
        (d * GROUP + z, ((d // GROUP) * GROUP + place_of(z)) * GROUP + place_of(d % GROUP))
        for d in range(n_dp)
        for z in range(GROUP)
    ]
    return lax.ppermute(values, ("dp", "ctx"), pairs)


def send_core(values, n_dp):
    pairs = [(d * GROUP + z, (d ^ 1) * GROUP + z) for d in range(n_dp) for z in range(GROUP)]
    return lax.ppermute(values, ("dp", "ctx"), pairs)


def trade(arrays, n_dp):
    result = [arrays[0]]
    for r in range(1, GROUP):
        pairs = [(d * GROUP + z, (d ^ r) * GROUP + z) for d in range(n_dp) for z in range(GROUP)]
        result.append(lax.ppermute(arrays[r], ("dp", "ctx"), pairs))
    return result


def per_device(
    n_dp,
    layer_input,
    out_cotangent,
    params,
    vectors,
    param_moment,
    vector_moment,
    param_square,
    vector_square,
):
    plan = BitMover(n_dp) if n_dp == 8 else Mover(n_dp)
    me = jnp.stack([lax.axis_index("dp"), lax.axis_index("ctx")]).astype(jnp.int32)
    place = place_of(me[0])

    helds = prepare(plan, me, params, vectors)
    fused = n_dp == 8
    if fused:
        whole0, whole1, value0, vec0, normed1, heads, *rest, value = plan.forward_first(helds, layer_input)
        wholes, vecs = [whole0, whole1], [vec0, plan.vectors(whole1)]
        first = (value0, normed1, heads, *rest)
    else:
        wholes = plan.gather_all(helds)
        vecs = [plan.vectors(whole) for whole in wholes]
        value = swap(layer_input, n_dp).astype(F32)
        grad = swap(out_cotangent, n_dp).astype(F32)

    saved = [None] * LAYERS
    for layer in range(LAYERS if fused else 0, LAYERS):
        vec, whole = vecs[layer], wholes[layer]
        bias = vec[7:11].reshape(CHUNKS, 1, WIDE)
        normed1, *sent = qkv_call(plan, me, value, vec, whole)
        heads = trade(sent, n_dp)
        *sent, lse = attend_call(me, heads)
        attended, hidden, normed2, upper, active, result = ff_call(
            plan, me, trade(sent, n_dp), value, vec, bias, whole
        )
        saved[layer] = (value, normed1, heads, lse, attended, hidden, normed2, upper, active)
        value = result
    if not fused:
        layer_output = swap(value.astype(BF), n_dp)

    def lines_of(gain_one, shift_one, sums, bias_output, gain_two, shift_two, bias_expand, bias_reduce):
        spread = lax.dynamic_update_slice(jnp.zeros((2, D), F32), sums[0:2], (0, place * WIDE))
        rows = [gain_one, shift_one, spread, bias_output, gain_two, shift_two, bias_expand, bias_reduce]
        return jnp.concatenate([row.reshape(-1, D) for row in rows])

    owned, lines = [None] * LAYERS, [None] * LAYERS
    for layer in reversed(range(LAYERS if fused else 0, LAYERS)):
        vec, whole = vecs[layer], wholes[layer]
        x, normed1, heads, lse, attended, hidden, normed2, upper, active = saved[layer]
        dyb, dub, dh, dhb, *rest = ff_back_call(plan, me, grad, upper, hidden, vec, whole)
        sent, bias_grad, vec2 = rest[:GROUP], rest[GROUP], rest[GROUP + 1]
        *sent, sums = attend_back_call(me, heads, trade(sent, n_dp), lse)
        mixed, grad, vec1 = qkv_back_call(plan, me, trade(sent, n_dp), dh, x, vec, whole)
        own = (normed1, attended, normed2, active, mixed, dhb, dub, dyb)
        buffer = weight_call(plan, me, own, [send_core(x, n_dp) for x in own])
        lines[layer] = lines_of(vec1[0], vec1[1], sums, vec2[3], vec2[1], vec2[2], bias_grad, vec2[0])
        owned[layer] = plan.scatter(buffer)
    if fused:
        layer_output, grad, *kept, bias_grad, vec2, sums = plan.middle(value, out_cotangent, vecs[1], whole1)
        buffer = weight_call(plan, me, kept[:8], kept[8:])
        vectors1 = (bias_grad, vec2, sums)
        owned[1], grad, dyb, dub, dhb, mixed, bias_grad, vec2, sums, *other = plan.backward_first(
            me, buffer, first, grad, vec0, whole0
        )
        _, normed1, _, _, attended, _, normed2, _, active = first
        own = (normed1, attended, normed2, active, mixed, dhb, dub, dyb)
        owned[0], vec_sums = plan.scatter_first(own, other, (bias_grad, vec2, sums), vectors1)
        share = plan.line // LANES
        vec_owned = [vec_sums[4 * layer : 4 * layer + share].reshape(-1) for layer in range(LAYERS)]
    else:
        vec_owned = [plan.scatter_vectors(line) for line in lines]
    input_grad = swap(grad.astype(BF), n_dp).astype(F32)

    done = []
    for layer in reversed(range(LAYERS)):
        done = adam_call(plan, me, layer, owned[layer], params, param_moment, param_square, done)
    vector_grad = jnp.stack(vec_owned)
    vector_step = adam_parts(vector_grad, vector_moment, vector_square, vectors, 0.0)
    return (
        layer_output,
        input_grad,
        done[0],
        vector_grad,
        done[1],
        vector_step[0],
        done[2],
        vector_step[1],
        done[3],
        vector_step[2],
    )


def solution(mesh):
    tokens = P(("dp", "ctx"), None)
    slabs = P(None, "ctx", "dp", None)
    lines = P(None, ("dp", "ctx"))
    return jax.shard_map(
        functools.partial(per_device, mesh.shape["dp"]),
        mesh=mesh,
        in_specs=(tokens, tokens, slabs, lines, slabs, lines, slabs, lines),
        out_specs=(tokens, tokens, slabs, lines, slabs, lines, slabs, lines, slabs, lines),
        check_vma=False,
    )
```

```python
import functools

import jax
import jax.numpy as jnp
from jax import lax
from jax.experimental import pallas as pl
from jax.experimental.pallas import tpu as pltpu
from jax.sharding import PartitionSpec as P

D = 1024
HEADS = 16
HEAD = 64
FF = 4096
LAYERS = 2
STEP = 10
BF = jnp.bfloat16
F32 = jnp.float32
LANES = 128
GROUP = 4
WIDE = D // GROUP
CHUNKS = FF // WIDE

norm_eps = 1e-05
beta_one = 0.9
beta_two = 0.999
rate = 0.01
decay = 0.1
adam_eps = 1e-08
gelu_c = 0.7978845608028654
gelu_a = 0.044715

VMEM_LIMIT = 60 * 1024 * 1024

ROWS = (D, D, D, FF)
PANELS = (3 * D // 4 // LANES, D // 4 // LANES, FF // 4 // LANES, D // 4 // LANES)


def pieces_of(count):
    size = sum(r * p for r, p in zip(ROWS, PANELS)) // count
    result = []
    for d in range(count):
        low, high = d * size, (d + 1) * size
        held, start = [], 0
        for mat in range(4):
            end = start + ROWS[mat] * PANELS[mat]
            a, b = max(low, start), min(high, end)
            if a < b:
                held.append((mat, (a - start) // PANELS[mat], (b - start) // PANELS[mat], a - low))
            start = end
        result.append(held)
    return size, result


TURN = (0, 2, 1, 3)


def place_of(d):
    return (d & 1) * 2 + (d >> 1) % 2


def params_of(**extra):
    return pltpu.CompilerParams(vmem_limit_bytes=VMEM_LIMIT, **extra)


MESH = pl.DeviceIdType.MESH
ANY = pl.BlockSpec(memory_space=pl.ANY)
VM = pl.BlockSpec(memory_space=pltpu.VMEM)
SM = pl.BlockSpec(memory_space=pltpu.SMEM)


def shape(dims, dtype):
    return jax.ShapeDtypeStruct(dims, dtype)


def nt(a, b):
    return lax.dot_general(a, b, (((1,), (1,)), ((), ())), preferred_element_type=F32)


def tn(a, b):
    return lax.dot_general(a, b, (((0,), (0,)), ((), ())), preferred_element_type=F32)


def nn(a, b):
    return jnp.dot(a, b, preferred_element_type=F32)


def norm_parts(values):
    center = values - jnp.mean(values, axis=-1, keepdims=True)
    spread = jnp.mean(center * center, axis=-1, keepdims=True)
    scale = lax.rsqrt(spread + norm_eps)
    return center * scale, scale


def norm_back(values, gain, grad):
    hat, scale = norm_parts(values)
    dhat = grad * gain
    back = scale * (
        dhat
        - jnp.mean(dhat, axis=-1, keepdims=True)
        - hat * jnp.mean(dhat * hat, axis=-1, keepdims=True)
    )
    return back, jnp.sum(grad * hat, axis=0, keepdims=True), jnp.sum(grad, axis=0, keepdims=True)


def load_matrix(whole, target, mat, pieces, sem, split=False):
    for c in range(4):
        for d, held in enumerate(pieces):
            for m, k0, k1, base in held:
                if m != mat:
                    continue
                for j in range(PANELS[mat]):
                    panel, k = c * PANELS[mat] + j, k0
                    while k < k1:
                        n = min(k1 - k, D - k % D) if split else k1 - k
                        at = (panel * 4 + k // D, pl.ds(k % D, n)) if split else (panel, pl.ds(k, n))
                        pltpu.make_async_copy(
                            whole.at[c, d, pl.ds(base + j * (k1 - k0) + k - k0, n)], target.at[at], sem
                        ).start()
                        k += n


def wait_all(ref, sem):
    pltpu.make_async_copy(ref, ref, sem).wait()


def prep_kernel(plan, me, slabs, lines, *outs):
    for layer, out in enumerate(outs):
        out[plan.size :, :] = jnp.zeros((plan.span - plan.size, LANES), BF)
        for r in range(lines.shape[1] // LANES):
            at = plan.size + r
            out[at : at + 1, :] = lines[layer : layer + 1, r * LANES : (r + 1) * LANES].astype(BF)
    for d, held in enumerate(plan.pieces):

        @pl.when(me[0] == d)
        def _(held=held):
            for layer, out in enumerate(outs):
                for mat, k0, k1, base in held:
                    count, step = k1 - k0, PANELS[mat]
                    for j in range(step):
                        rows = slabs[layer, 0, pl.ds(base + j, count, stride=step), :]
                        out[pl.ds(base + j * count, count), :] = rows.astype(BF)


def prepare(plan, me, slabs, lines):
    lines = jnp.pad(lines, ((0, 0), (0, -lines.shape[1] % LANES)))
    return pl.pallas_call(
        functools.partial(prep_kernel, plan),
        out_shape=[shape((plan.span, LANES), BF)] * LAYERS,
        in_specs=[SM, VM, VM],
        out_specs=[VM] * LAYERS,
        compiler_params=params_of(),
        name="prep",
    )(me, slabs, lines)


def qkv_kernel(pieces, me, x, vec, whole, normed, out0, out1, out2, out3, weight, qkv, sem):
    load_matrix(whole, weight, 0, pieces, sem)
    hat, _ = norm_parts(x[...].astype(F32))
    normed[...] = (hat * vec[0:1, :] + vec[1:2, :]).astype(BF)
    wait_all(weight, sem)
    for b in range(3 * GROUP):
        kind, at = b // GROUP, b % GROUP
        acc = nn(normed[...], jnp.concatenate([weight[2 * b], weight[2 * b + 1]], axis=1))
        if kind != 1:
            row = 2 if kind == 0 else 3
            acc = acc + vec[row : row + 1, at * WIDE : (at + 1) * WIDE]
        qkv[b] = acc.astype(BF)
    mine = place_of(me[0])
    for r, out in enumerate((out0, out1, out2, out3)):
        for kind in range(3):
            out[:, kind * WIDE : (kind + 1) * WIDE] = qkv[kind * GROUP + (mine ^ TURN[r])]


def qkv_call(plan, me, x, vec, whole):
    rows = x.shape[0]
    return pl.pallas_call(
        functools.partial(qkv_kernel, plan.pieces),
        out_shape=[shape((rows, D), BF)] + [shape((rows, 3 * WIDE), BF)] * GROUP,
        in_specs=[SM, VM, VM, ANY],
        out_specs=[VM] * 5,
        scratch_shapes=[
            pltpu.VMEM((3 * D // LANES, D, LANES), BF),
            pltpu.VMEM((3 * GROUP, rows, WIDE), BF),
            pltpu.SemaphoreType.DMA,
        ],
        compiler_params=params_of(),
        name="qkv",
    )(me, x, vec, whole)


def diagonal(rows):
    return lax.broadcasted_iota(jnp.int32, (rows, rows), 1) <= lax.broadcasted_iota(jnp.int32, (rows, rows), 0)


def attend_kernel(me, in0, in1, in2, in3, out0, out1, out2, out3, lse, q, k, v, o):
    mine = place_of(me[0])
    rows = in0.shape[0]
    for r, ref in enumerate((in0, in1, in2, in3)):
        at = pl.ds(pl.multiple_of((mine ^ TURN[r]) * rows, rows), rows)
        q[at, :] = ref[:, 0:WIDE]
        k[at, :] = ref[:, WIDE : 2 * WIDE]
        v[at, :] = ref[:, 2 * WIDE : 3 * WIDE]
    seen = diagonal(rows)
    for h in range(WIDE // HEAD):
        cols = slice(h * HEAD, (h + 1) * HEAD)
        for i in range(GROUP):
            here = slice(i * rows, (i + 1) * rows)
            qi = q[here, cols]
            near = jnp.where(seen, nt(qi, k[here, cols]) * 0.125, -1000000000.0)
            top = jnp.max(near, axis=1, keepdims=True)
            if i:
                far = nt(qi, k[0 : i * rows, cols]) * 0.125
                top = jnp.maximum(top, jnp.max(far, axis=1, keepdims=True))
                far = jnp.exp(far - top)
            near = jnp.exp(near - top)
            total = jnp.sum(near, axis=1, keepdims=True)
            if i:
                total = total + jnp.sum(far, axis=1, keepdims=True)
            inv = 1.0 / total
            res = nn((near * inv).astype(BF), v[here, cols])
            if i:
                res = res + nn((far * inv).astype(BF), v[0 : i * rows, cols])
            o[i, :, cols] = res.astype(BF)
            lse[here, h : h + 1] = top + jnp.log(total)
    for r, out in enumerate((out0, out1, out2, out3)):
        out[...] = o[mine ^ TURN[r]]


def attend_call(me, heads):
    rows = heads[0].shape[0]
    span = GROUP * rows
    return pl.pallas_call(
        attend_kernel,
        out_shape=[shape((rows, WIDE), BF)] * GROUP + [shape((span, LANES), F32)],
        in_specs=[SM] + [VM] * GROUP,
        out_specs=[VM] * 5,
        scratch_shapes=[pltpu.VMEM((span, WIDE), BF)] * 3 + [pltpu.VMEM((GROUP, rows, WIDE), BF)],
        compiler_params=params_of(),
        name="attend",
    )(me, *heads)


def side(ref, at, count=2):
    return jnp.concatenate([ref[at + i] for i in range(count)], axis=1)


def rows_of(ref, at):
    return jnp.concatenate([ref[p, at, :] for p in range(D // LANES)], axis=1)


def ff_kernel(
    pieces, me, in0, in1, in2, in3, x, vec, bias, whole,
    attended, hidden, normed, upper, active, out,
    wo, we, wr, parts, sems,
):
    load_matrix(whole, wo, 1, pieces, sems.at[0])
    load_matrix(whole, we, 2, pieces, sems.at[1])
    load_matrix(whole, wr, 3, pieces, sems.at[2])
    mine = place_of(me[0])
    for r, ref in enumerate((in0, in1, in2, in3)):
        parts[mine ^ TURN[r]] = ref[...]
    for g in range(GROUP):
        attended[:, g * WIDE : (g + 1) * WIDE] = parts[g]
    wait_all(wo, sems.at[0])
    for g in range(GROUP):
        cols = slice(g * WIDE, (g + 1) * WIDE)
        hidden[:, cols] = x[:, cols] + nn(attended[...], side(wo, 2 * g)) + vec[4:5, cols]
    hat, _ = norm_parts(hidden[...])
    normed[...] = (hat * vec[5:6, :] + vec[6:7, :]).astype(BF)
    out[...] = hidden[...] + vec[11:12, :]
    wait_all(we, sems.at[1])
    wait_all(wr, sems.at[2])

    def body(n, _):
        u = nn(normed[...], side(we, 2 * n)) + bias[n]
        upper[n] = u
        act = (0.5 * u * (1.0 + jnp.tanh(gelu_c * (u + gelu_a * u * u * u)))).astype(BF)
        active[n] = act
        out[...] += nn(act, rows_of(wr, pl.ds(pl.multiple_of(n * WIDE, WIDE), WIDE)))
        return 0

    lax.fori_loop(0, CHUNKS, body, 0)


def ff_call(plan, me, heads, x, vec, bias, whole):
    rows = x.shape[0]
    return pl.pallas_call(
        functools.partial(ff_kernel, plan.pieces),
        out_shape=[
            shape((rows, D), BF),
            shape((rows, D), F32),
            shape((rows, D), BF),
            shape((CHUNKS, rows, WIDE), F32),
            shape((CHUNKS, rows, WIDE), BF),
            shape((rows, D), F32),
        ],
        in_specs=[SM] + [VM] * 7 + [ANY],
        out_specs=[VM] * 6,
        scratch_shapes=[
            pltpu.VMEM((D // LANES, D, LANES), BF),
            pltpu.VMEM((FF // LANES, D, LANES), BF),
            pltpu.VMEM((D // LANES, FF, LANES), BF),
            pltpu.VMEM((GROUP, rows, WIDE), BF),
            pltpu.SemaphoreType.DMA((3,)),
        ],
        compiler_params=params_of(),
        name="ff",
    )(me, *heads, x, vec, bias, whole)


def ff_back_kernel(
    pieces, me, dy, upper, hidden, vec, whole,
    dyb, dub, dh, dhb, out0, out1, out2, out3, bias_grad, vec_grad,
    wo, we, wr, acc, parts, sems,
):
    load_matrix(whole, wr, 3, pieces, sems.at[2])
    load_matrix(whole, we, 2, pieces, sems.at[1])
    load_matrix(whole, wo, 1, pieces, sems.at[0])
    dyb[...] = dy[...].astype(BF)
    vec_grad[0:1, :] = jnp.sum(dy[...], axis=0, keepdims=True)
    acc[...] = jnp.zeros_like(acc)
    wait_all(wr, sems.at[2])
    wait_all(we, sems.at[1])

    def body(n, _):
        dg = nt(dyb[...], rows_of(wr, pl.ds(pl.multiple_of(n * WIDE, WIDE), WIDE)))
        u = upper[n]
        t = jnp.tanh(gelu_c * (u + gelu_a * u * u * u))
        slope = 0.5 * (1.0 + t) + 0.5 * u * (1.0 - t * t) * (gelu_c * (1.0 + 3.0 * gelu_a * u * u))
        du = dg * slope
        bias_grad[n] = jnp.sum(du, axis=0, keepdims=True)
        low = du.astype(BF)
        dub[n] = low
        acc[...] += nt(low, side(we, 2 * n))
        return 0

    lax.fori_loop(0, CHUNKS, body, 0)
    back, gain, shift = norm_back(hidden[...], vec[5:6, :], acc[...])
    total = dy[...] + back
    vec_grad[1:2, :] = gain
    vec_grad[2:3, :] = shift
    vec_grad[3:4, :] = jnp.sum(total, axis=0, keepdims=True)
    vec_grad[4:8, :] = jnp.zeros((4, D), F32)
    dh[...] = total
    dhb[...] = total.astype(BF)
    wait_all(wo, sems.at[0])
    for g in range(GROUP):
        parts[g] = nt(dhb[...], rows_of(wo, slice(g * WIDE, (g + 1) * WIDE))).astype(BF)
    mine = place_of(me[0])
    for r, out in enumerate((out0, out1, out2, out3)):
        out[...] = parts[mine ^ TURN[r]]


def ff_back_call(plan, me, dy, upper, hidden, vec, whole):
    rows = dy.shape[0]
    return pl.pallas_call(
        functools.partial(ff_back_kernel, plan.pieces),
        out_shape=[
            shape((rows, D), BF),
            shape((CHUNKS, rows, WIDE), BF),
            shape((rows, D), F32),
            shape((rows, D), BF),
        ]
        + [shape((rows, WIDE), BF)] * GROUP
        + [shape((CHUNKS, 1, WIDE), F32), shape((8, D), F32)],
        in_specs=[SM] + [VM] * 4 + [ANY],
        out_specs=[VM] * 10,
        scratch_shapes=[
            pltpu.VMEM((D // LANES, D, LANES), BF),
            pltpu.VMEM((FF // LANES, D, LANES), BF),
            pltpu.VMEM((D // LANES, FF, LANES), BF),
            pltpu.VMEM((rows, D), F32),
            pltpu.VMEM((GROUP, rows, WIDE), BF),
            pltpu.SemaphoreType.DMA((3,)),
        ],
        compiler_params=params_of(),
        name="ff_back",
    )(me, dy, upper, hidden, vec, whole)


def attend_back_kernel(
    me, in0, in1, in2, in3, do0, do1, do2, do3, lse,
    out0, out1, out2, out3, sums,
    q, k, v, do, dq, dk, dv,
):
    mine = place_of(me[0])
    rows = in0.shape[0]
    for r, (ref, grad) in enumerate(((in0, do0), (in1, do1), (in2, do2), (in3, do3))):
        at = pl.ds(pl.multiple_of((mine ^ TURN[r]) * rows, rows), rows)
        q[at, :] = ref[:, 0:WIDE]
        k[at, :] = ref[:, WIDE : 2 * WIDE]
        v[at, :] = ref[:, 2 * WIDE : 3 * WIDE]
        do[at, :] = grad[...]
    seen = diagonal(rows)
    for h in range(WIDE // HEAD):
        cols = slice(h * HEAD, (h + 1) * HEAD)
        total = jnp.zeros((1, HEAD), F32)
        for i in reversed(range(GROUP)):
            here = slice(i * rows, (i + 1) * rows)
            past = slice(0, i * rows)
            qi, doi, ls = q[here, cols], do[here, cols], lse[here, h : h + 1]
            near = jnp.exp(jnp.where(seen, nt(qi, k[here, cols]) * 0.125, -1000000000.0) - ls)
            dnear = nt(doi, v[here, cols])
            inner = jnp.sum(near * dnear, axis=1, keepdims=True)
            if i:
                far = jnp.exp(nt(qi, k[past, cols]) * 0.125 - ls)
                dfar = nt(doi, v[past, cols])
                inner = inner + jnp.sum(far * dfar, axis=1, keepdims=True)
            snear = (near * (dnear - inner) * 0.125).astype(BF)
            res = nn(snear, k[here, cols])
            dkn = tn(snear, qi)
            dvn = tn(near.astype(BF), doi)
            last = i == GROUP - 1
            dk[here, cols] = dkn if last else dk[here, cols] + dkn
            dv[here, cols] = dvn if last else dv[here, cols] + dvn
            if i:
                sfar = (far * (dfar - inner) * 0.125).astype(BF)
                res = res + nn(sfar, k[past, cols])
                dkf = tn(sfar, qi)
                dvf = tn(far.astype(BF), doi)
                dk[past, cols] = dkf if last else dk[past, cols] + dkf
                dv[past, cols] = dvf if last else dv[past, cols] + dvf
            total = total + jnp.sum(res, axis=0, keepdims=True)
            dq[i, :, cols] = res.astype(BF)
        sums[0:1, cols] = total
    sums[1:2, :] = jnp.sum(dv[...], axis=0, keepdims=True)
    sums[2:8, :] = jnp.zeros((6, WIDE), F32)
    for r, out in enumerate((out0, out1, out2, out3)):
        at = pl.ds(pl.multiple_of((mine ^ TURN[r]) * rows, rows), rows)
        out[:, 0:WIDE] = dq[mine ^ TURN[r]]
        out[:, WIDE : 2 * WIDE] = dk[at, :].astype(BF)
        out[:, 2 * WIDE : 3 * WIDE] = dv[at, :].astype(BF)


def attend_back_call(me, heads, grads, lse):
    rows = heads[0].shape[0]
    span = GROUP * rows
    return pl.pallas_call(
        attend_back_kernel,
        out_shape=[shape((rows, 3 * WIDE), BF)] * GROUP + [shape((8, WIDE), F32)],
        in_specs=[SM] + [VM] * 9,
        out_specs=[VM] * 5,
        scratch_shapes=[pltpu.VMEM((span, WIDE), BF)] * 4
        + [pltpu.VMEM((GROUP, rows, WIDE), BF)]
        + [pltpu.VMEM((span, WIDE), F32)] * 2,
        compiler_params=params_of(),
        name="attend_back",
    )(me, *heads, *grads, lse)


def qkv_back_kernel(pieces, me, in0, in1, in2, in3, dh, x, vec, whole, mixed, dx, vec_grad, weight, acc, sem):
    load_matrix(whole, weight, 0, pieces, sem)
    mine = place_of(me[0])
    for r, ref in enumerate((in0, in1, in2, in3)):
        mixed[mine ^ TURN[r]] = ref[...]
    acc[...] = jnp.zeros_like(acc)
    wait_all(weight, sem)

    for b in range(3 * GROUP):
        kind, at = b // GROUP, b % GROUP
        acc[...] += nt(mixed[at, :, kind * WIDE : (kind + 1) * WIDE], side(weight, 2 * b))
    back, gain, shift = norm_back(x[...].astype(F32), vec[0:1, :], acc[...])
    dx[...] = dh[...] + back
    vec_grad[0:1, :] = gain
    vec_grad[1:2, :] = shift
    vec_grad[2:8, :] = jnp.zeros((6, D), F32)


def qkv_back_call(plan, me, grads, dh, x, vec, whole):
    rows = x.shape[0]
    return pl.pallas_call(
        functools.partial(qkv_back_kernel, plan.pieces),
        out_shape=[shape((GROUP, rows, 3 * WIDE), BF), shape((rows, D), F32), shape((8, D), F32)],
        in_specs=[SM] + [VM] * 7 + [ANY],
        out_specs=[VM] * 3,
        scratch_shapes=[
            pltpu.VMEM((3 * D // LANES, D, LANES), BF),
            pltpu.VMEM((rows, D), F32),
            pltpu.SemaphoreType.DMA,
        ],
        compiler_params=params_of(),
        name="qkv_back",
    )(me, *grads, dh, x, vec, whole)


def weight_items(pieces, core):
    items = []
    for d in range(core, len(pieces), 2):
        for mat, k0, k1, base in pieces[d]:
            count, step = k1 - k0, PANELS[mat]
            k = k0
            while k < k1:
                n = min(WIDE - k % WIDE, k1 - k) if mat == 3 else k1 - k0
                if step == 2:
                    groups = [range(j, 4 * step, step) for j in range(step)]
                else:
                    groups = [range(2 * i, 2 * i + 2) for i in range(2 * step)]
                for group in groups:
                    low = base + group[0] % step * count + k - k0
                    items.append((low, d, mat, base - k0, count, k, n, group))
                k += n
    return items


def weight_part(items, own, other, out, arrive):
    normed1, attended, normed2, active, mixed, dhb, dub, dyb = zip(own, other)
    everything = slice(None)

    def both(pair, *at):
        arrive(pair[0])
        return jnp.concatenate([ref[at] for ref in pair], axis=0)

    def panels(pair, group):
        return jnp.concatenate([both(pair, everything, slice(p * LANES, (p + 1) * LANES)) for p in group], axis=1)

    turned = {}
    for _, d, mat, base, count, k, n, group in items:
        if (d, mat, k) not in turned:
            if mat == 3:
                lhs = both(active, k // WIDE, everything, slice(k % WIDE, k % WIDE + n))
            else:
                lhs = both((normed1, attended, normed2)[mat], everything, slice(k, k + n))
            turned[d, mat, k] = lhs.T
        if mat == 0:
            at = group[0] // 2
            rhs = both(mixed, at % GROUP, everything, slice(at // GROUP * WIDE, (at // GROUP + 1) * WIDE))
        elif mat == 2:
            rhs = both(dub, group[0] // 2)
        else:
            rhs = panels(dhb if mat == 1 else dyb, group)
        res = nn(turned[d, mat, k], rhs).astype(BF)
        step = PANELS[mat]
        for i, p in enumerate(group):
            at = base + k + (p % step) * count
            out[p // step, d // 2, at : at + n, :] = res[:, i * LANES : (i + 1) * LANES]


LOAD_ORDER = (0, 4, 1, 5, 2, 6, 3, 7)


class Loader:
    def __init__(self, sources, targets, sems):
        self.copies = [pltpu.make_async_copy(a, b, sems.at[i]) for i, (a, b) in enumerate(zip(sources, targets))]
        self.targets, self.pending = targets, []
        for i in LOAD_ORDER:
            self.copies[i].start()
            self.copies[i + 8].start()

    def begin(self):
        self.pending = list(range(8))

    def arrive(self, ref):
        for i in list(self.pending):
            if self.targets[i] is ref:
                self.finish((i,))

    def finish(self, which=None):
        for i in list(self.pending) if which is None else which:
            self.copies[i].wait()
            self.copies[i + 8].wait()
            self.pending.remove(i)


def weight_kernel(pieces, thirds, me, *refs):
    held, (out, grads, sems, leave) = refs[17:33], (refs[16], *refs[33:])
    loader = Loader(refs[:16], held, sems)
    flushes = []
    groups = grads.shape[2] // thirds
    for group in range(groups):
        for core in range(2):

            @pl.when(me[0] % 2 == core)
            def _(core=core):
                if group == 0:
                    loader.begin()
                items = [item for item in weight_items(pieces, core) if item[0] // thirds == group]
                weight_part(items, held[:8], held[8:], grads, loader.arrive)
                loader.finish()

        rows = pl.ds(group * thirds, thirds)
        flushes.append(pltpu.make_async_copy(grads.at[:, :, rows], out.at[:, :, rows], leave.at[group]))
        flushes[-1].start()
    for copy in flushes:
        copy.wait()


def weight_call(plan, me, own, other):
    dims = (4, plan.n_dp // 2, plan.size, LANES)
    thirds = plan.size // 3
    return pl.pallas_call(
        functools.partial(weight_kernel, plan.pieces, thirds),
        out_shape=shape(dims, BF),
        in_specs=[SM] + [ANY] * 16,
        out_specs=ANY,
        scratch_shapes=[pltpu.VMEM(x.shape, BF) for x in (*own, *other)]
        + [pltpu.VMEM(dims, BF), pltpu.SemaphoreType.DMA((16,)), pltpu.SemaphoreType.DMA((3,))],
        compiler_params=params_of(),
        name="weight_grads",
    )(me, *own, *other)


def adam_parts(grad, moment, square, master, weight_decay):
    moment_next = beta_one * moment + (1.0 - beta_one) * grad
    square_next = beta_two * square + (1.0 - beta_two) * grad * grad
    corrected = moment_next / (1.0 - beta_one**STEP)
    scaled = square_next / (1.0 - beta_two**STEP)
    update = -rate * (corrected / (jnp.sqrt(scaled) + adam_eps) + weight_decay * master)
    return moment_next, square_next, update


def adam_kernel(plan, me, owned, master, moment, square, *refs):
    grad, moment_next, square_next, update = refs[-4:]
    for d, held in enumerate(plan.pieces):

        @pl.when(me[0] == d)
        def _(held=held):
            for mat, k0, k1, base in held:
                size, step = k1 - k0, PANELS[mat]
                for j in range(step):
                    grad[0, 0, pl.ds(base + j, size, stride=step), :] = owned[pl.ds(base + j * size, size), :]

    new = adam_parts(grad[0, 0], moment[0, 0], square[0, 0], master[0, 0], decay)
    moment_next[0, 0], square_next[0, 0], update[0, 0] = new


def adam_call(plan, me, layer, owned, master, moment, square, before):
    block = pl.BlockSpec((1, 1) + master.shape[2:], lambda i: (layer, 0, 0, 0))
    whole = pl.BlockSpec(owned.shape, lambda i: (0, 0))
    first = 5
    return pl.pallas_call(
        functools.partial(adam_kernel, plan),
        grid=(1,),
        out_shape=[shape(master.shape, F32)] * 4,
        in_specs=[SM, whole] + [block] * 3 + [ANY] * len(before),
        out_specs=[block] * 4,
        input_output_aliases={first + i: i for i in range(len(before))},
        compiler_params=params_of(),
        name="adam",
    )(me, owned, master, moment, square, *before)


class Wire:
    def __init__(self, send, recv):
        self.d, self.z = lax.axis_index("dp"), lax.axis_index("ctx")
        self.place = place_of(self.d)
        self.send, self.recv, self.next = send, recv, 0

    def copy(self, src, dst, d, z, at=None):
        slot = self.next
        self.next += 1
        return pltpu.make_async_remote_copy(
            src_ref=src, dst_ref=dst, send_sem=self.send.at[slot], recv_sem=self.recv.at[slot],
            device_id=(d, z), device_id_type=MESH,
        )

    def push(self, src, dst, flip_dp, flip_ctx):
        copy = self.copy(src, dst, self.d ^ flip_dp, self.z ^ flip_ctx)
        copy.start()
        return copy

    def greet(self, flips, swaps=False):
        barrier = pltpu.get_barrier_semaphore()
        for fd, fz in flips:
            pl.semaphore_signal(barrier, inc=1, device_id=(self.d ^ fd, self.z ^ fz), device_id_type=MESH)
        if not swaps:
            pl.semaphore_wait(barrier, len(flips))
            return

        @pl.when(self.place != self.z)
        def _():
            pl.semaphore_signal(barrier, inc=1, device_id=self.opposite(), device_id_type=MESH)
            pl.semaphore_wait(barrier, len(flips) + 1)

        @pl.when(self.place == self.z)
        def _():
            pl.semaphore_wait(barrier, len(flips))

    def opposite(self):
        return (self.d - self.d % GROUP + place_of(self.z), self.place)

    def swap(self, src, dst):
        copy = self.copy(src, dst, *self.opposite())

        @pl.when(self.place != self.z)
        def _():
            copy.start()

        @pl.when(self.place == self.z)
        def _():
            dst[...] = src[...]

        def finish():
            @pl.when(self.place != self.z)
            def _():
                copy.wait()

        return finish

    def post(self, blocks, into):
        base = self.next
        self.next += GROUP
        first = self.d - self.d % GROUP

        def copy(g, sender):
            return pltpu.make_async_remote_copy(
                src_ref=blocks.at[g], dst_ref=into.at[self.place],
                send_sem=self.send.at[base + g], recv_sem=self.recv.at[base + sender],
                device_id=(first + place_of(g), self.z), device_id_type=MESH,
            )

        def send(g):
            @pl.when(self.place != g)
            def _():
                copy(g, self.place).start()

            @pl.when(self.place == g)
            def _():
                into[g] = blocks[g]

        def finish():
            for r in range(1, GROUP):
                copy(0, self.place ^ r).wait_recv()
            for g in range(GROUP):

                @pl.when(self.place != g)
                def _(g=g):
                    copy(g, self.place).wait_send()

        return send, finish

    def trade(self, blocks, into):
        copies = []
        for r in (2, 3, 1):
            copies.append(self.push(blocks.at[self.place ^ TURN[r]], into.at[self.place], r, 0))
        into[self.place] = blocks[self.place]
        return copies


def drive(jobs, late):
    live = list(zip(jobs, late))
    step = 0
    while live:
        rest = []
        for job, wait in live:
            if step >= wait:
                try:
                    next(job)
                except StopIteration:
                    continue
                yield
            rest.append((job, wait))
        live = rest
        step += 1


def take(steps, count=1):
    for _ in range(count):
        next(steps, None)


def paced(steps, pace):
    owed = [0.0]

    def advance():
        owed[0] += pace
        while owed[0] >= 1.0:
            owed[0] -= 1.0
            next(steps, None)

    return advance


def unpack_vectors(raw, vec, n_dp, size):
    share = 12 * D // (4 * n_dp) // LANES
    per_row = D // LANES
    for d in range(n_dp):
        for z in range(4):
            lines = raw[z, d].astype(F32)
            for r in range(share):
                at = (d * 4 + z) * share + r
                col = at % per_row * LANES
                vec[at // per_row : at // per_row + 1, col : col + LANES] = lines[r : r + 1, :]


def share_normed(wire, normed, everyone):
    mine = everyone.at[wire.place]
    everyone[wire.place] = normed[...]
    return wire.push(mine, mine, 2, 0), wire.push(mine, mine, 1, 0)


def qkv_part(wire, shared, everyone, weight, vec, q, k, v):
    far, near = shared
    rows = everyone.shape[1]
    cols = pl.ds(pl.multiple_of(wire.place * WIDE, WIDE), WIDE)

    def block(g):
        at = pl.ds(pl.multiple_of(g * rows, rows), rows)
        for kind, target in enumerate((q, k, v)):
            acc = nn(everyone[g], side(weight, 2 * (kind * GROUP + wire.place)))
            if kind != 1:
                row = 2 if kind == 0 else 3
                acc = acc + vec[row : row + 1, cols]
            low = acc.astype(BF)
            target[at, :] = (low.astype(F32) * 0.125).astype(BF) if kind == 0 else low
            yield

    yield from block(wire.place)
    near.wait_recv()
    yield from block(wire.place ^ TURN[1])
    far.wait_recv()
    other = everyone.at[wire.place ^ TURN[2]]
    relay = wire.push(other, other, 1, 0)
    yield from block(wire.place ^ TURN[2])
    relay.wait_recv()
    yield from block(wire.place ^ TURN[3])
    for copy in (far, near, relay):
        copy.wait_send()


def attend_part(q, k, v, o, lse, send):
    rows = o.shape[1]
    seen = diagonal(rows)
    for i in reversed(range(GROUP)):
        for h in range(WIDE // HEAD):
            cols = slice(h * HEAD, (h + 1) * HEAD)
            here = slice(i * rows, (i + 1) * rows)
            qi = q[here, cols]
            near = jnp.where(seen, nt(qi, k[here, cols]), -1000000000.0)
            top = jnp.max(near, axis=1, keepdims=True)
            if i:
                far = nt(qi, k[0 : i * rows, cols])
                top = jnp.maximum(top, jnp.max(far, axis=1, keepdims=True))
                far = jnp.exp(far - top)
            near = jnp.exp(near - top)
            total = jnp.sum(near, axis=1, keepdims=True)
            if i:
                total = total + jnp.sum(far, axis=1, keepdims=True)
            res = nn(near.astype(BF), v[here, cols])
            if i:
                res = res + nn(far.astype(BF), v[0 : i * rows, cols])
            o[i, :, cols] = (res * (1.0 / total)).astype(BF)
            lse[here, h : h + 1] = top + jnp.log(total)
            yield
        send(i)


def ff_part(x, parts, vec, weights, wr_rows, sems, attended, hidden, normed, upper, active, out, made):
    wo, we, wr = weights
    for g in range(GROUP):
        attended[:, g * WIDE : (g + 1) * WIDE] = parts[g]
    wait_all(wo, sems[0])
    for g in range(GROUP):
        cols = slice(g * WIDE, (g + 1) * WIDE)
        hidden[:, cols] = x[:, cols].astype(F32) + nn(attended[...], side(wo, 2 * g)) + vec[4:5, cols]
        yield
    hat, _ = norm_parts(hidden[...])
    normed[...] = (hat * vec[5:6, :] + vec[6:7, :]).astype(BF)
    out[...] = hidden[...] + vec[11:12, :]
    wait_all(we, sems[1])
    wait_all(wr, sems[2])
    yield
    for n in range(CHUNKS):
        row, col = 7 + n // GROUP, n % GROUP * WIDE
        u = nn(normed[...], side(we, 2 * n)) + vec[row : row + 1, col : col + WIDE]
        upper[n] = u
        act = (0.5 * u * (1.0 + jnp.tanh(gelu_c * (u + gelu_a * u * u * u)))).astype(BF)
        active[n] = act
        yield
        if n % GROUP == GROUP - 1:
            quarter = jnp.concatenate([active[n - i] for i in reversed(range(GROUP))], axis=1)
            out[...] += nn(quarter, wr_rows(n // GROUP))
            made(n)
            yield


def ring_reader(upper, ring, sems):
    def fetch(n):
        return pltpu.make_async_copy(upper.at[n], ring.at[n % 2], sems[n % 2])

    fetch(0).start()

    def read(n):
        if n + 1 < CHUNKS:
            fetch(n + 1).start()
        fetch(n).wait()
        return ring[n % 2]

    return read


def ff_back_part(dy, read_upper, hidden, vec, weights, sems, dyb, dub, dh, dhb, blocks, acc, bias_grad, vec_grad):
    wo, we, wr = weights
    dyb[...] = dy[...].astype(BF)
    vec_grad[0:1, :] = jnp.sum(dy[...].astype(F32), axis=0, keepdims=True)
    if sems:
        wait_all(wr, sems[2])
        wait_all(we, sems[1])
    for n in range(CHUNKS):
        at = n * WIDE % D
        dg = nt(dyb[...], side_rows(wr, n * WIDE // D, slice(at, at + WIDE)))
        u = read_upper(n)
        t = jnp.tanh(gelu_c * (u + gelu_a * u * u * u))
        slope = 0.5 * (1.0 + t) + 0.5 * u * (1.0 - t * t) * (gelu_c * (1.0 + 3.0 * gelu_a * u * u))
        du = dg * slope
        row, col = n // GROUP, n % GROUP * WIDE
        bias_grad[row : row + 1, col : col + WIDE] = jnp.sum(du, axis=0, keepdims=True)
        low = du.astype(BF)
        dub[n] = low
        yield
        if n % GROUP == GROUP - 1:
            quarter = jnp.concatenate([dub[n - i] for i in reversed(range(GROUP))], axis=1)
            more = nt(quarter, side(we, 2 * (n - GROUP + 1), 2 * GROUP))
            acc[...] = more if n < GROUP else acc[...] + more
            yield
    back, gain, shift = norm_back(hidden[...], vec[5:6, :], acc[...])
    total = dy[...].astype(F32) + back
    vec_grad[1:2, :] = gain
    vec_grad[2:3, :] = shift
    vec_grad[3:4, :] = jnp.sum(total, axis=0, keepdims=True)
    dh[...] = total
    dhb[...] = total.astype(BF)
    if sems:
        wait_all(wo, sems[0])
    yield
    for g in range(GROUP):
        blocks[g] = nt(dhb[...], rows_of(wo, slice(g * WIDE, (g + 1) * WIDE))).astype(BF)
    yield


def side_rows(ref, at, rows):
    return jnp.concatenate([ref[p * 4 + at, rows, :] for p in range(D // LANES)], axis=1)


def attend_back_part(q, k, v, do, lse, dm, dk, dv, sums, send):
    rows = dm.shape[1]
    seen = diagonal(rows)
    sums[...] = jnp.zeros_like(sums)
    for i in reversed(range(GROUP)):
        here = slice(i * rows, (i + 1) * rows)
        past = slice(0, i * rows)
        last = i == GROUP - 1
        for h in range(WIDE // HEAD):
            cols = slice(h * HEAD, (h + 1) * HEAD)
            qi, doi, ls = q[here, cols], do[i, :, cols], lse[here, h : h + 1]
            near = jnp.exp(jnp.where(seen, nt(qi, k[here, cols]), -1000000000.0) - ls)
            dnear = nt(doi, v[here, cols])
            inner = jnp.sum(near * dnear, axis=1, keepdims=True)
            if i:
                far = jnp.exp(nt(qi, k[past, cols]) - ls)
                dfar = nt(doi, v[past, cols])
                inner = inner + jnp.sum(far * dfar, axis=1, keepdims=True)
            snear = (near * (dnear - inner)).astype(BF)
            res = nn(snear, k[here, cols])
            dkn = tn(snear, qi)
            dvn = tn(near.astype(BF), doi)
            dk[here, cols] = dkn if last else dk[here, cols] + dkn
            dv[here, cols] = dvn if last else dv[here, cols] + dvn
            if i:
                sfar = (far * (dfar - inner)).astype(BF)
                res = res + nn(sfar, k[past, cols])
                dkf = tn(sfar, qi)
                dvf = tn(far.astype(BF), doi)
                dk[past, cols] = dkf if last else dk[past, cols] + dkf
                dv[past, cols] = dvf if last else dv[past, cols] + dvf
            res = res * 0.125
            sums[0:1, cols] += jnp.sum(res, axis=0, keepdims=True)
            dm[i, :, cols] = res.astype(BF)
            yield
        dm[i, :, WIDE : 2 * WIDE] = dk[here, :].astype(BF)
        dm[i, :, 2 * WIDE : 3 * WIDE] = dv[here, :].astype(BF)
        sums[1:2, :] += jnp.sum(dv[here, :], axis=0, keepdims=True)
        send(i)


def qkv_back_part(mixed, weight, acc):
    for kind in range(3):
        part = jnp.concatenate([mixed[g, :, kind * WIDE : (kind + 1) * WIDE] for g in range(GROUP)], axis=1)
        more = nt(part, side(weight, 2 * GROUP * kind, 2 * GROUP))
        acc[...] = acc[...] + more if kind else more
        for _ in range(3):
            yield


class Mover:
    def __init__(self, n_dp):
        self.n_dp = n_dp
        self.size, self.pieces = pieces_of(n_dp)
        self.line = 12 * D // (4 * n_dp)
        self.span = self.size + 16

    def gather_all(self, helds):
        wholes = [lax.all_gather(held, ("ctx", "dp"), axis=0, tiled=True) for held in helds]
        return [whole.reshape(4, self.n_dp, self.span, LANES) for whole in wholes]

    def vectors(self, whole):
        rows = -(-self.line // LANES)
        lines = whole[:, :, self.size : self.size + rows].reshape(4, self.n_dp, -1)[:, :, : self.line]
        return lines.transpose(1, 0, 2).reshape(12, D).astype(F32)

    def scatter(self, buffer):
        none = jnp.zeros_like(buffer)
        core = lax.axis_index("dp") % 2
        pair = jnp.stack([jnp.where(core == 0, buffer, none), jnp.where(core == 1, buffer, none)], axis=2)
        flat = pair.reshape(-1, LANES)
        return lax.psum_scatter(flat, ("ctx", "dp"), scatter_dimension=0, tiled=True).astype(F32)

    def scatter_vectors(self, grads):
        return lax.psum_scatter(grads.reshape(-1), ("dp", "ctx"), scatter_dimension=0, tiled=True)


CORE = 1
FLIPS = ((1, 0), (2, 0), (3, 0), (4, 0), (0, 1), (0, 2), (0, 3))


class BitMover(Mover):
    def __init__(self, n_dp):
        super().__init__(n_dp)
        self.gap, self.pace, self.pace_back = 8, (1.3, 4, 2), (1.5, 4, 2, 2)
        self.even = self.cut(((4, 4), (2, 2), (4, 4), (2, 2), (4, 4), (2, 2), (4, 4), (2, 2)))
        self.skew = self.cut(((5, 3), (3, 2), (4, 3), (3, 1), (5, 3), (3, 2), (4, 3), (2, 2)))

    def cut(self, plan):
        unit, row, chunks = self.size // 48, 0, []
        for i, pair in enumerate(plan):
            for units, (a, b) in zip(pair, ((2, 4), (4, 2))):
                chunks.append((row, units * unit, (i % 2 == 0, a, b), i // 2 * 2))
                row += units * unit
        return chunks

    def gather_jobs(self, wire, local, helds, wholes, plans, done):
        d, z = wire.d, wire.z

        def job(layer, part):
            low, size, (z_first, a, b), _ = plans[layer][part]
            if part == len(plans[layer]) - 1:
                size = self.span - low
            rows = pl.ds(low, size)
            held, whole = helds[layer].at[rows], wholes[layer]
            started = []

            def push(src, dst, fd, fz):
                started.append(wire.push(src, dst, fd, fz))
                return started[-1]

            def line(dd, fd):
                ref = whole.at[:, dd, rows]
                return push(ref, ref, fd, 0)

            own = pltpu.make_async_copy(held, whole.at[z, d, rows], local.at[layer * len(plans[0]) + part])
            own.start()
            mine = [push(held, whole.at[z, d, rows], 0, k) for k in (3, 2, 1)]
            if z_first:
                yield
                own.wait()
                for copy in mine:
                    copy.wait_recv()
                first = line(d, a)
                second = line(d, b)
                cores = [line(d, CORE)]
                yield
                first.wait_recv()
                third = line(d ^ a, b)
                cores.append(line(d ^ a, CORE))
                yield
                second.wait_recv()
                cores.append(line(d ^ b, CORE))
                yield
                third.wait_recv()
                cores.append(line(d ^ a ^ b, CORE))
            else:
                first = push(held, whole.at[z, d, rows], a, 0)
                yield
                first.wait_recv()
                other = whole.at[z, d ^ a, rows]
                theirs = [push(other, other, 0, k) for k in (3, 2, 1)]
                yield
                own.wait()
                for copy in mine:
                    copy.wait_recv()
                second = line(d, b)
                cores = [line(d, CORE)]
                yield
                for copy in theirs:
                    copy.wait_recv()
                third = line(d ^ a, b)
                cores.append(line(d ^ a, CORE))
                yield
                second.wait_recv()
                cores.append(line(d ^ b, CORE))
                yield
                third.wait_recv()
                cores.append(line(d ^ a ^ b, CORE))
            yield
            for copy in cores:
                copy.wait_recv()
            for copy in started:
                copy.wait_send()
            done[layer] += 1

        jobs = [job(layer, part) for layer, plan in enumerate(plans) for part in range(len(plan))]
        return drive(jobs, [chunk[3] + self.gap * layer for layer, plan in enumerate(plans) for chunk in plan])

    def forward_first(self, helds, tokens):
        rows = tokens.shape[0]
        span = GROUP * rows
        plans = (self.even, self.skew)
        pieces, count, pace = self.pieces, len(self.even), self.pace
        slots = 2 * count * 14 + 16

        def kernel(
            held0, held1, tokens,
            whole0, whole1, value, vec, normed1, heads_out, lse, attended, hidden, normed2, upper_out, active_out, out,
            upper, active, swapped, everyone, q, k, v, o, parts, raw, wa, wo, we, wr, local, sems, send, recv,
        ):
            wire = Wire(send, recv)
            leaving = []

            def leave(src, dst):
                leaving.append(pltpu.make_async_copy(src, dst, sems.at[5 + len(leaving)]))
                leaving[-1].start()

            def made(n):
                if n % 4 == 3:
                    for src, dst in ((upper, upper_out), (active, active_out)):
                        leave(src.at[pl.ds(n - 3, 4)], dst.at[pl.ds(n - 3, 4)])

            wire.greet(FLIPS, swaps=True)
            done = [0, 0]
            comm = self.gather_jobs(wire, local, (held0, held1), (whole0, whole1), plans, done)
            take(comm, 6)
            swap_in = wire.swap(tokens, swapped)
            while done[0] < count:
                next(comm)
            load_vec = pltpu.make_async_copy(whole0.at[:, :, pl.ds(self.size, 16)], raw, sems.at[4])
            load_vec.start()
            load_matrix(whole0, wa, 0, pieces, sems.at[3])
            load_matrix(whole0, wo, 1, pieces, sems.at[0])
            swap_in()
            value[...] = swapped[...]
            load_vec.wait()
            unpack_vectors(raw, vec, self.n_dp, self.size)
            hat, _ = norm_parts(swapped[...].astype(F32))
            normed1[...] = (hat * vec[0:1, :] + vec[1:2, :]).astype(BF)
            shared = share_normed(wire, normed1, everyone)
            wait_all(wa, sems.at[3])
            advance = paced(comm, pace[0])
            for _ in qkv_part(wire, shared, everyone, wa, vec, q, k, v):
                advance()
            load_matrix(whole0, we, 2, pieces, sems.at[1])
            load_matrix(whole0, wr, 3, pieces, sems.at[2])
            take(comm, pace[1])
            for i, ref in enumerate((q, k, v)):
                leave(ref, heads_out.at[i])
            send_o, finish = wire.post(o, parts)
            for _ in attend_part(q, k, v, o, lse, send_o):
                advance()
            take(comm, pace[2])
            finish()
            for _ in ff_part(
                swapped, parts, vec, (wo, we, wr), lambda n: rows_of(wr, slice(n * D, (n + 1) * D)), [sems.at[i] for i in range(3)],
                attended, hidden, normed2, upper, active, out, made,
            ):
                advance()
            for _ in comm:
                pass
            for copy in leaving:
                copy.wait()

        return pl.pallas_call(
            kernel,
            out_shape=[shape((4, self.n_dp, self.span, LANES), BF)] * 2
            + [
                shape((rows, D), BF),
                shape((12, D), F32),
                shape((rows, D), BF),
                shape((3, span, WIDE), BF),
                shape((span, LANES), F32),
                shape((rows, D), BF),
                shape((rows, D), F32),
                shape((rows, D), BF),
                shape((CHUNKS, rows, WIDE), F32),
                shape((CHUNKS, rows, WIDE), BF),
                shape((rows, D), F32),
            ],
            in_specs=[VM] * 3,
            out_specs=[ANY] * 2 + [VM] * 3 + [ANY] + [VM] * 4 + [ANY] * 2 + [VM],
            scratch_shapes=[
                pltpu.VMEM((CHUNKS, rows, WIDE), F32),
                pltpu.VMEM((CHUNKS, rows, WIDE), BF),
                pltpu.VMEM((rows, D), BF),
            ]
            + [pltpu.VMEM((GROUP, rows, D), BF)]
            + [pltpu.VMEM((span, WIDE), BF)] * 3
            + [pltpu.VMEM((GROUP, rows, WIDE), BF)] * 2
            + [
                pltpu.VMEM((4, self.n_dp, 16, LANES), BF),
                pltpu.VMEM((3 * D // LANES, D, LANES), BF),
                pltpu.VMEM((D // LANES, D, LANES), BF),
                pltpu.VMEM((FF // LANES, D, LANES), BF),
                pltpu.VMEM((D // LANES, FF, LANES), BF),
                pltpu.SemaphoreType.DMA((2 * count,)),
                pltpu.SemaphoreType.DMA((16,)),
                pltpu.SemaphoreType.DMA((slots,)),
                pltpu.SemaphoreType.DMA((slots,)),
            ],
            compiler_params=params_of(collective_id=1, has_side_effects=True),
            name="forward_first",
        )(*helds, tokens)

    def scatter_jobs(self, wire, parts):
        d, z = wire.d, wire.z

        def job(grads, acc, from_b, from_a, from_z, order, size, put, local):
            z_first, a, b = order
            started = []

            def push(src, dst, fd, fz):
                started.append(wire.push(src, dst, fd, fz))
                return started[-1]

            places = [(d ^ (ja * a)) // 2 for ja in (1, 0)]
            if acc is None:
                piece = [lambda k, p=p: grads.at[k, p] for p in places]
                pieces = [grads.at[:, p] for p in places]
            else:
                piece = [lambda k, i=i: acc.at[i, k] for i in range(2)]
                pieces = [acc.at[i] for i in range(2)]
            block = min(64, size)

            def add(into, more):
                def body(i, _):
                    at = pl.ds(pl.multiple_of(i * block, block), block)
                    for x, y in zip(into, more):
                        x[at, :] = x[at, :] + y[at, :]
                    return 0

                lax.fori_loop(0, size // block, body, 0)

            def every(i, more):
                add([piece[i](k) for k in range(4)], [more(k) for k in range(4)])

            to_b = [push(grads.at[:, p ^ (b // 2)], from_b.at[i], b, 0) for i, p in enumerate(places)]
            loads = []
            if acc is not None:
                for i in range(2):
                    loads.append(pltpu.make_async_copy(grads.at[:, places[i]], acc.at[i], local[i]))
                    loads[-1].start()
            yield
            for load in loads:
                load.wait()
            to_b[0].wait_recv()
            every(0, lambda k: from_b.at[0, k])
            if z_first:
                to_a = push(pieces[0], from_a, a, 0)
                yield
                to_b[1].wait_recv()
                every(1, lambda k: from_b.at[1, k])
                yield
                to_a.wait_recv()
                every(1, lambda k: from_a.at[k])
                to_z = [push(piece[1](z ^ k), from_z.at[k - 1, 0], 0, k) for k in (3, 2, 1)]
                yield
                more = [from_z.at[k, 0] for k in range(3)]
                last = to_z
            else:
                to_z = [push(piece[0](z ^ k), from_z.at[k - 1, 0], 0, k) for k in (3, 2, 1)]
                yield
                to_b[1].wait_recv()
                every(1, lambda k: from_b.at[1, k])
                to_z1 = [push(piece[1](z ^ k), from_z.at[k - 1, 1], 0, k) for k in (3, 2, 1)]
                yield
                for copy in to_z:
                    copy.wait_recv()
                for k in range(3):
                    add([piece[0](z)], [from_z.at[k, 0]])
                to_a = push(piece[0](z), from_a.at[0], a, 0)
                yield
                more = [from_z.at[k, 1] for k in range(3)] + [from_a.at[0]]
                last = to_z1 + [to_a]
            for copy in last:
                copy.wait_recv()

            def body(i, _):
                at = pl.multiple_of(i * block, block)
                here = pl.ds(at, block)
                value = piece[1](z)[here, :].astype(F32)
                for ref in more:
                    value = value + ref[here, :].astype(F32)
                put(at, block, value)
                return 0

            lax.fori_loop(0, size // block, body, 0)
            for copy in started:
                copy.wait_send()

        return [job(*part) for part in parts]

    def scatter_scratch(self, plan, with_acc):
        result = []
        for _, n, order, _ in plan:
            if with_acc:
                result.append(pltpu.VMEM((2, 4, n, LANES), BF))
            result.append(pltpu.VMEM((2, 4, n, LANES), BF))
            result.append(pltpu.VMEM((4 if order[0] else 1, n, LANES), BF))
            result.append(pltpu.VMEM((3, 1 if order[0] else 2, n, LANES), BF))
        return result

    def scatter_parts(self, plan, grads, scratch, owned, local):
        each = len(scratch) // len(plan)
        parts = []
        for i, (low, n, order, _) in enumerate(plan):
            refs = scratch[i * each : (i + 1) * each]
            acc, (from_b, from_a, from_z) = (refs[0] if each == 4 else None), refs[-3:]

            def put(at, block, value, low=low):
                owned[pl.ds(low + at, block), :] = value

            waits = [local.at[2 * i], local.at[2 * i + 1]] if each == 4 else None
            parts.append((grads.at[:, :, pl.ds(low, n)], acc, from_b, from_a, from_z, order, n, put, waits))
        return parts

    def backward_first(self, me, grads, saved, dy, vec, whole):
        x, normed1, heads, lse, attended, hidden, normed2, upper, active = saved
        rows = x.shape[0]
        span = GROUP * rows
        plan, pieces, pace = self.skew, self.pieces, self.pace_back
        count = len(plan)
        slots = count * 12 + 24
        scratch_count = 4 * count

        def kernel(
            grads, x, normed1, heads, lse, attended, hidden, normed2, upper, active, dy, vec, whole,
            owned, dx, dyb, dub_out, dhb, mixed_out, bias_grad, vec_grad, sums,
            o_normed1, o_attended, o_normed2, o_active, o_mixed, o_dhb, o_dub, o_dyb,
            *scratch,
        ):
            bufs = scratch[:scratch_count]
            dub, mixed, q, k, v, do, blocks, dk, dv, dm, acc, dh, ring, wo, we, wr, local, sems, send, recv = scratch[scratch_count:]
            sems = [sems.at[i] for i in range(10)]
            load_matrix(whole, wr, 3, pieces, sems[2], split=True)
            load_matrix(whole, we, 2, pieces, sems[1])
            load_matrix(whole, wo, 1, pieces, sems[0])
            for i, ref in enumerate((q, k, v)):
                pltpu.make_async_copy(heads.at[i], ref, sems[5]).start()
            wire = Wire(send, recv)
            wire.greet(FLIPS)
            comm = drive(
                self.scatter_jobs(wire, self.scatter_parts(plan, grads, bufs, owned, local)), [chunk[3] for chunk in plan]
            )
            advance = paced(comm, pace[0])
            take(comm, pace[1])
            core = [wire.push(a, b, CORE, 0) for a, b in (
                (normed1, o_normed1), (attended, o_attended), (normed2, o_normed2), (active, o_active))]
            vec_grad[...] = jnp.zeros_like(vec_grad)
            read_upper = ring_reader(upper, ring, sems[3:5])
            for _ in ff_back_part(
                dy, read_upper, hidden, vec, (wo, we, wr), sems, dyb, dub, dh, dhb, blocks, acc, bias_grad, vec_grad
            ):
                advance()
            load_matrix(whole, wr, 0, pieces, sems[6])
            leaving = [pltpu.make_async_copy(dub, dub_out, sems[8]), pltpu.make_async_copy(mixed, mixed_out, sems[9])]
            leaving[0].start()
            core += [wire.push(a, b, CORE, 0) for a, b in ((dyb, o_dyb), (dub, o_dub), (dhb, o_dhb))]
            copies = wire.trade(blocks, do)
            take(comm, pace[2])
            for ref in (q, k, v):
                wait_all(ref, sems[5])
            for copy in copies:
                copy.wait()
            send_m, finish = wire.post(dm, mixed)
            for _ in attend_back_part(q, k, v, do, lse, dm, dk, dv, sums, send_m):
                advance()
            take(comm, pace[3])
            finish()
            core.append(wire.push(mixed, o_mixed, CORE, 0))
            leaving[1].start()
            wait_all(wr.at[pl.ds(0, 3 * D // LANES)], sems[6])
            for _ in qkv_back_part(mixed, wr, acc):
                advance()
            back, gain, shift = norm_back(x[...].astype(F32), vec[0:1, :], acc[...])
            dx[...] = dh[...] + back
            vec_grad[4:5, :] = gain
            vec_grad[5:6, :] = shift
            for _ in comm:
                pass
            for copy in core + leaving:
                copy.wait()

        token = shape((rows, D), BF)
        wide = shape((CHUNKS, rows, WIDE), BF)
        triple = shape((GROUP, rows, 3 * WIDE), BF)
        return pl.pallas_call(
            kernel,
            out_shape=[
                shape((self.size, LANES), F32),
                shape((rows, D), F32),
                token,
                wide,
                token,
                triple,
                shape((4, D), F32),
                shape((8, D), F32),
                shape((8, WIDE), F32),
            ]
            + [token, token, token, wide, triple, token, wide, token],
            in_specs=[ANY, VM, ANY, ANY, VM, ANY, VM, ANY, ANY, ANY, VM, VM, ANY],
            out_specs=[VM] * 3 + [ANY, VM, ANY] + [VM] * 3 + [ANY] * 8,
            scratch_shapes=self.scatter_scratch(plan, True)
            + [pltpu.VMEM((CHUNKS, rows, WIDE), BF), pltpu.VMEM((GROUP, rows, 3 * WIDE), BF)]
            + [pltpu.VMEM((span, WIDE), BF)] * 3
            + [pltpu.VMEM((GROUP, rows, WIDE), BF)] * 2
            + [pltpu.VMEM((span, WIDE), F32)] * 2
            + [
                pltpu.VMEM((GROUP, rows, 3 * WIDE), BF),
                pltpu.VMEM((rows, D), F32),
                pltpu.VMEM((rows, D), F32),
                pltpu.VMEM((2, rows, WIDE), F32),
                pltpu.VMEM((D // LANES, D, LANES), BF),
                pltpu.VMEM((FF // LANES, D, LANES), BF),
                pltpu.VMEM((4 * D // LANES, D, LANES), BF),
                pltpu.SemaphoreType.DMA((2 * count,)),
                pltpu.SemaphoreType.DMA((10,)),
                pltpu.SemaphoreType.DMA((slots,)),
                pltpu.SemaphoreType.DMA((slots,)),
            ],
            compiler_params=params_of(collective_id=2, has_side_effects=True),
            name="backward_first",
        )(grads, x, normed1, heads, lse, attended, hidden, normed2, upper, active, dy, vec, whole)

    def middle(self, x, cotangent, vec, whole):
        rows = x.shape[0]
        span = GROUP * rows
        pieces = self.pieces
        slots = 40

        def kernel(
            x, cotangent, vec, whole,
            output, dx, normed1, attended, normed2, active_out, mixed_out, dhb, dub_out, dyb,
            o_normed1, o_attended, o_normed2, o_active, o_mixed, o_dhb, o_dub, o_dyb, bias_grad, vec_grad, sums,
            active, mixed, dub, dy, result, returned, everyone, blocks, q, k, v, o, parts, do, lse, hidden, upper, acc, dh, dk, dv, wa, wo, we, wr,
            sems, send, recv,
        ):
            sems = [sems.at[i] for i in range(7)]
            leaving = []

            def leave(src, dst):
                leaving.append(pltpu.make_async_copy(src, dst, sems[4 + len(leaving)]))
                leaving[-1].start()

            load_matrix(whole, wa, 0, pieces, sems[3])
            wire = Wire(send, recv)
            hat, _ = norm_parts(x[...])
            normed1[...] = (hat * vec[0:1, :] + vec[1:2, :]).astype(BF)
            wire.greet(FLIPS, swaps=True)
            shared = share_normed(wire, normed1, everyone)
            core = [wire.push(normed1, o_normed1, CORE, 0)]
            load_matrix(whole, wo, 1, pieces, sems[0])
            wait_all(wa, sems[3])
            for _ in qkv_part(wire, shared, everyone, wa, vec, q, k, v):
                pass
            load_matrix(whole, we, 2, pieces, sems[1])
            load_matrix(whole, wr, 3, pieces, sems[2], split=True)
            swap_in = wire.swap(cotangent, dy)
            send_o, finish = wire.post(o, parts)
            for _ in attend_part(q, k, v, o, lse, send_o):
                pass
            finish()
            for _ in ff_part(
                x, parts, vec, (wo, we, wr), lambda n: side_rows(wr, n, slice(0, D)),
                sems, attended, hidden, normed2, upper, active, dx, lambda n: None,
            ):
                pass
            core += [wire.push(a, b, CORE, 0) for a, b in (
                (attended, o_attended), (normed2, o_normed2), (active, o_active))]
            leave(active, active_out)
            result[...] = dx[...].astype(BF)
            swap_out = wire.swap(result, returned)
            swap_in()
            vec_grad[...] = jnp.zeros_like(vec_grad)
            for _ in ff_back_part(
                dy, lambda n: upper[n], hidden, vec, (wo, we, wr), None, dyb, dub, dh, dhb, o, acc, bias_grad, vec_grad
            ):
                pass
            leave(dub, dub_out)
            copies = wire.trade(o, do)
            core += [wire.push(a, b, CORE, 0) for a, b in ((dyb, o_dyb), (dub, o_dub), (dhb, o_dhb))]
            for copy in copies:
                copy.wait()
            send_m, finish = wire.post(blocks, mixed)
            for _ in attend_back_part(q, k, v, do, lse, blocks, dk, dv, sums, send_m):
                pass
            finish()
            core.append(wire.push(mixed, o_mixed, CORE, 0))
            leave(mixed, mixed_out)
            for _ in qkv_back_part(mixed, wa, acc):
                pass
            back, gain, shift = norm_back(x[...], vec[0:1, :], acc[...])
            dx[...] = dh[...] + back
            vec_grad[4:5, :] = gain
            vec_grad[5:6, :] = shift
            swap_out()
            output[...] = returned[...]
            for copy in core + leaving:
                copy.wait()

        token = shape((rows, D), BF)
        wide = shape((CHUNKS, rows, WIDE), BF)
        triple = shape((GROUP, rows, 3 * WIDE), BF)
        kept = [token, token, token, wide, triple, token, wide, token]
        return pl.pallas_call(
            kernel,
            out_shape=[token, shape((rows, D), F32)] + kept * 2
            + [shape((4, D), F32), shape((8, D), F32), shape((8, WIDE), F32)],
            in_specs=[VM, VM, VM, ANY],
            out_specs=[VM] * 5 + [ANY, ANY, VM, ANY, VM] + [ANY] * 8 + [VM] * 3,
            scratch_shapes=[
                pltpu.VMEM((CHUNKS, rows, WIDE), BF),
                pltpu.VMEM((GROUP, rows, 3 * WIDE), BF),
                pltpu.VMEM((CHUNKS, rows, WIDE), BF),
            ]
            + [pltpu.VMEM((rows, D), BF)] * 3
            + [pltpu.VMEM((GROUP, rows, D), BF), pltpu.VMEM((GROUP, rows, 3 * WIDE), BF)]
            + [pltpu.VMEM((span, WIDE), BF)] * 3
            + [pltpu.VMEM((GROUP, rows, WIDE), BF)] * 3
            + [
                pltpu.VMEM((span, LANES), F32),
                pltpu.VMEM((rows, D), F32),
                pltpu.VMEM((CHUNKS, rows, WIDE), F32),
                pltpu.VMEM((rows, D), F32),
                pltpu.VMEM((rows, D), F32),
                pltpu.VMEM((span, WIDE), F32),
                pltpu.VMEM((span, WIDE), F32),
                pltpu.VMEM((3 * D // LANES, D, LANES), BF),
                pltpu.VMEM((D // LANES, D, LANES), BF),
                pltpu.VMEM((FF // LANES, D, LANES), BF),
                pltpu.VMEM((4 * D // LANES, D, LANES), BF),
                pltpu.SemaphoreType.DMA((7,)),
                pltpu.SemaphoreType.DMA((slots,)),
                pltpu.SemaphoreType.DMA((slots,)),
            ],
            compiler_params=params_of(collective_id=4, has_side_effects=True),
            name="middle",
        )(x, cotangent, vec, whole)

    def scatter_first(self, own, other, vectors0, vectors1):
        plan, pieces, thirds = self.even, self.pieces, self.size // 3
        count = len(plan)
        slots = count * 12 + 24
        scratch_count = 3 * count

        def kernel(*refs):
            vectors, (owned, vec_owned) = (refs[16:19], refs[19:22]), refs[22:24]
            scratch = refs[24:]
            bufs, scratch = scratch[:scratch_count], scratch[scratch_count:]
            held, scratch = scratch[:16], scratch[16:]
            loader = Loader(refs[:16], held, scratch[0])
            grads, lines, got, small, from_b, from_a, from_z, send, recv = scratch[1:]
            wire = Wire(send, recv)
            wire.greet([flip for flip in FLIPS if flip[0] != 3])
            mine = pl.ds(pl.multiple_of(wire.place * WIDE, WIDE), WIDE)
            for i, (bias_grad, vec_grad, sums) in enumerate(vectors):
                lines[i, 0:2, :] = vec_grad[4:6, :]
                lines[i, 2:4, :] = jnp.zeros((2, D), F32)
                lines[i, 2:4, mine] = sums[0:2, :]
                lines[i, 4:5, :] = vec_grad[3:4, :]
                lines[i, 5:7, :] = vec_grad[1:3, :]
                lines[i, 7:11, :] = bias_grad[...]
                lines[i, 11:12, :] = vec_grad[0:1, :]
            trade = wire.push(lines, got, CORE, 0)

            def make(group):
                for core in range(2):
                    items = [item for item in weight_items(pieces, core) if item[0] // thirds == group]

                    @pl.when(wire.d % 2 == core)
                    def _(items=items):
                        if group == 0:
                            loader.begin()
                        weight_part(items, held[:8], held[8:], grads, loader.arrive)
                        loader.finish()

            def put(at, block, value):
                vec_owned[pl.ds(at, block), :] = value

            parts = self.scatter_parts(plan, grads, bufs, owned, None)
            jobs = self.scatter_jobs(wire, parts)
            made = [0]

            def after(job, rows):
                while made[0] * thirds < rows:
                    make(made[0])
                    made[0] += 1
                yield from job

            jobs = [after(job, low + n) for job, (low, n, _, _) in zip(jobs, plan)]

            def vector_job():
                trade.wait()
                lines[...] = lines[...] + got[...]
                share, per_row = self.line // LANES, D // LANES
                small[...] = jnp.zeros_like(small)
                for core in range(2):

                    @pl.when(wire.d % 2 == core)
                    def _(core=core):
                        for d in range(core, self.n_dp, 2):
                            for z in range(4):
                                for r in range(share):
                                    at = (d * 4 + z) * share + r
                                    row, col = at // per_row, at % per_row * LANES
                                    for i in range(2):
                                        here = slice(i * 4 + r, i * 4 + r + 1)
                                        small[z, d // 2, here, :] = lines[i, row : row + 1, col : col + LANES]

                yield from self.scatter_jobs(wire, [(small, None, from_b, from_a, from_z, (True, 2, 4), 8, put, None)])[0]

            jobs.append(vector_job())
            for _ in drive(jobs, [chunk[3] for chunk in plan] + [1]):
                pass

        return pl.pallas_call(
            kernel,
            out_shape=[shape((self.size, LANES), F32), shape((8, LANES), F32)],
            in_specs=[ANY] * 16 + [VM] * 6,
            out_specs=[VM] * 2,
            scratch_shapes=self.scatter_scratch(plan, False)
            + [pltpu.VMEM(x.shape, BF) for x in (*own, *other)]
            + [
                pltpu.SemaphoreType.DMA((16,)),
                pltpu.VMEM((4, self.n_dp // 2, self.size, LANES), BF),
                pltpu.VMEM((2, 12, D), F32),
                pltpu.VMEM((2, 12, D), F32),
                pltpu.VMEM((4, self.n_dp // 2, 8, LANES), F32),
                pltpu.VMEM((2, 4, 8, LANES), F32),
                pltpu.VMEM((4, 8, LANES), F32),
                pltpu.VMEM((3, 1, 8, LANES), F32),
                pltpu.SemaphoreType.DMA((slots,)),
                pltpu.SemaphoreType.DMA((slots,)),
            ],
            compiler_params=params_of(collective_id=3, has_side_effects=True),
            name="scatter_first",
        )(*own, *other, *vectors0, *vectors1)


def swap(values, n_dp):
    pairs = [
        (d * GROUP + z, ((d // GROUP) * GROUP + place_of(z)) * GROUP + place_of(d % GROUP))
        for d in range(n_dp)
        for z in range(GROUP)
    ]
    return lax.ppermute(values, ("dp", "ctx"), pairs)


def send_core(values, n_dp):
    pairs = [(d * GROUP + z, (d ^ 1) * GROUP + z) for d in range(n_dp) for z in range(GROUP)]
    return lax.ppermute(values, ("dp", "ctx"), pairs)


def trade(arrays, n_dp):
    result = [arrays[0]]
    for r in range(1, GROUP):
        pairs = [(d * GROUP + z, (d ^ r) * GROUP + z) for d in range(n_dp) for z in range(GROUP)]
        result.append(lax.ppermute(arrays[r], ("dp", "ctx"), pairs))
    return result


def per_device(
    n_dp,
    layer_input,
    out_cotangent,
    params,
    vectors,
    param_moment,
    vector_moment,
    param_square,
    vector_square,
):
    plan = BitMover(n_dp) if n_dp == 8 else Mover(n_dp)
    me = jnp.stack([lax.axis_index("dp"), lax.axis_index("ctx")]).astype(jnp.int32)
    place = place_of(me[0])

    helds = prepare(plan, me, params, vectors)
    fused = n_dp == 8
    if fused:
        whole0, whole1, value0, vec0, normed1, heads, *rest, value = plan.forward_first(helds, layer_input)
        wholes, vecs = [whole0, whole1], [vec0, plan.vectors(whole1)]
        first = (value0, normed1, heads, *rest)
    else:
        wholes = plan.gather_all(helds)
        vecs = [plan.vectors(whole) for whole in wholes]
        value = swap(layer_input, n_dp).astype(F32)
        grad = swap(out_cotangent, n_dp).astype(F32)

    saved = [None] * LAYERS
    for layer in range(LAYERS if fused else 0, LAYERS):
        vec, whole = vecs[layer], wholes[layer]
        bias = vec[7:11].reshape(CHUNKS, 1, WIDE)
        normed1, *sent = qkv_call(plan, me, value, vec, whole)
        heads = trade(sent, n_dp)
        *sent, lse = attend_call(me, heads)
        attended, hidden, normed2, upper, active, result = ff_call(
            plan, me, trade(sent, n_dp), value, vec, bias, whole
        )
        saved[layer] = (value, normed1, heads, lse, attended, hidden, normed2, upper, active)
        value = result
    if not fused:
        layer_output = swap(value.astype(BF), n_dp)

    def lines_of(gain_one, shift_one, sums, bias_output, gain_two, shift_two, bias_expand, bias_reduce):
        spread = lax.dynamic_update_slice(jnp.zeros((2, D), F32), sums[0:2], (0, place * WIDE))
        rows = [gain_one, shift_one, spread, bias_output, gain_two, shift_two, bias_expand, bias_reduce]
        return jnp.concatenate([row.reshape(-1, D) for row in rows])

    owned, lines = [None] * LAYERS, [None] * LAYERS
    for layer in reversed(range(LAYERS if fused else 0, LAYERS)):
        vec, whole = vecs[layer], wholes[layer]
        x, normed1, heads, lse, attended, hidden, normed2, upper, active = saved[layer]
        dyb, dub, dh, dhb, *rest = ff_back_call(plan, me, grad, upper, hidden, vec, whole)
        sent, bias_grad, vec2 = rest[:GROUP], rest[GROUP], rest[GROUP + 1]
        *sent, sums = attend_back_call(me, heads, trade(sent, n_dp), lse)
        mixed, grad, vec1 = qkv_back_call(plan, me, trade(sent, n_dp), dh, x, vec, whole)
        own = (normed1, attended, normed2, active, mixed, dhb, dub, dyb)
        buffer = weight_call(plan, me, own, [send_core(x, n_dp) for x in own])
        lines[layer] = lines_of(vec1[0], vec1[1], sums, vec2[3], vec2[1], vec2[2], bias_grad, vec2[0])
        owned[layer] = plan.scatter(buffer)
    if fused:
        layer_output, grad, *kept, bias_grad, vec2, sums = plan.middle(value, out_cotangent, vecs[1], whole1)
        buffer = weight_call(plan, me, kept[:8], kept[8:])
        vectors1 = (bias_grad, vec2, sums)
        owned[1], grad, dyb, dub, dhb, mixed, bias_grad, vec2, sums, *other = plan.backward_first(
            me, buffer, first, grad, vec0, whole0
        )
        _, normed1, _, _, attended, _, normed2, _, active = first
        own = (normed1, attended, normed2, active, mixed, dhb, dub, dyb)
        owned[0], vec_sums = plan.scatter_first(own, other, (bias_grad, vec2, sums), vectors1)
        share = plan.line // LANES
        vec_owned = [vec_sums[4 * layer : 4 * layer + share].reshape(-1) for layer in range(LAYERS)]
    else:
        vec_owned = [plan.scatter_vectors(line) for line in lines]
    input_grad = swap(grad.astype(BF), n_dp).astype(F32)

    done = []
    for layer in reversed(range(LAYERS)):
        done = adam_call(plan, me, layer, owned[layer], params, param_moment, param_square, done)
    vector_grad = jnp.stack(vec_owned)
    vector_step = adam_parts(vector_grad, vector_moment, vector_square, vectors, 0.0)
    return (
        layer_output,
        input_grad,
        done[0],
        vector_grad,
        done[1],
        vector_step[0],
        done[2],
        vector_step[1],
        done[3],
        vector_step[2],
    )


def solution(mesh):
    tokens = P(("dp", "ctx"), None)
    slabs = P(None, "ctx", "dp", None)
    lines = P(None, ("dp", "ctx"))
    return jax.shard_map(
        functools.partial(per_device, mesh.shape["dp"]),
        mesh=mesh,
        in_specs=(tokens, tokens, slabs, lines, slabs, lines, slabs, lines),
        out_specs=(tokens, tokens, slabs, lines, slabs, lines, slabs, lines, slabs, lines),
        check_vma=False,
    )
```

```python
import functools

import jax
import jax.numpy as jnp
from jax import lax
from jax.experimental import pallas as pl
from jax.experimental.pallas import tpu as pltpu
from jax.sharding import PartitionSpec as P

D = 1024
HEADS = 16
HEAD = 64
FF = 4096
LAYERS = 2
STEP = 10
BF = jnp.bfloat16
F32 = jnp.float32
LANES = 128
GROUP = 4
WIDE = D // GROUP
CHUNKS = FF // WIDE

norm_eps = 1e-05
beta_one = 0.9
beta_two = 0.999
rate = 0.01
decay = 0.1
adam_eps = 1e-08
gelu_c = 0.7978845608028654
gelu_a = 0.044715

VMEM_LIMIT = 60 * 1024 * 1024

ROWS = (D, D, D, FF)
PANELS = (3 * D // 4 // LANES, D // 4 // LANES, FF // 4 // LANES, D // 4 // LANES)


def pieces_of(count):
    size = sum(r * p for r, p in zip(ROWS, PANELS)) // count
    result = []
    for d in range(count):
        low, high = d * size, (d + 1) * size
        held, start = [], 0
        for mat in range(4):
            end = start + ROWS[mat] * PANELS[mat]
            a, b = max(low, start), min(high, end)
            if a < b:
                held.append((mat, (a - start) // PANELS[mat], (b - start) // PANELS[mat], a - low))
            start = end
        result.append(held)
    return size, result


TURN = (0, 2, 1, 3)


def place_of(d):
    return (d & 1) * 2 + (d >> 1) % 2


def params_of(**extra):
    return pltpu.CompilerParams(vmem_limit_bytes=VMEM_LIMIT, **extra)


MESH = pl.DeviceIdType.MESH
ANY = pl.BlockSpec(memory_space=pl.ANY)
VM = pl.BlockSpec(memory_space=pltpu.VMEM)
SM = pl.BlockSpec(memory_space=pltpu.SMEM)


def shape(dims, dtype):
    return jax.ShapeDtypeStruct(dims, dtype)


def nt(a, b):
    return lax.dot_general(a, b, (((1,), (1,)), ((), ())), preferred_element_type=F32)


def tn(a, b):
    return lax.dot_general(a, b, (((0,), (0,)), ((), ())), preferred_element_type=F32)


def nn(a, b):
    return jnp.dot(a, b, preferred_element_type=F32)


def norm_parts(values):
    center = values - jnp.mean(values, axis=-1, keepdims=True)
    spread = jnp.mean(center * center, axis=-1, keepdims=True)
    scale = lax.rsqrt(spread + norm_eps)
    return center * scale, scale


def norm_back(values, gain, grad):
    hat, scale = norm_parts(values)
    dhat = grad * gain
    back = scale * (
        dhat
        - jnp.mean(dhat, axis=-1, keepdims=True)
        - hat * jnp.mean(dhat * hat, axis=-1, keepdims=True)
    )
    return back, jnp.sum(grad * hat, axis=0, keepdims=True), jnp.sum(grad, axis=0, keepdims=True)


def load_matrix(whole, target, mat, pieces, sem, split=False):
    for c in range(4):
        for d, held in enumerate(pieces):
            for m, k0, k1, base in held:
                if m != mat:
                    continue
                for j in range(PANELS[mat]):
                    panel, k = c * PANELS[mat] + j, k0
                    while k < k1:
                        n = min(k1 - k, D - k % D) if split else k1 - k
                        at = (panel * 4 + k // D, pl.ds(k % D, n)) if split else (panel, pl.ds(k, n))
                        pltpu.make_async_copy(
                            whole.at[c, d, pl.ds(base + j * (k1 - k0) + k - k0, n)], target.at[at], sem
                        ).start()
                        k += n


def wait_all(ref, sem):
    pltpu.make_async_copy(ref, ref, sem).wait()


def prep_kernel(plan, me, slabs, lines, *outs):
    for layer, out in enumerate(outs):
        out[plan.size :, :] = jnp.zeros((plan.span - plan.size, LANES), BF)
        for r in range(lines.shape[1] // LANES):
            at = plan.size + r
            out[at : at + 1, :] = lines[layer : layer + 1, r * LANES : (r + 1) * LANES].astype(BF)
    for d, held in enumerate(plan.pieces):

        @pl.when(me[0] == d)
        def _(held=held):
            for layer, out in enumerate(outs):
                for mat, k0, k1, base in held:
                    count, step = k1 - k0, PANELS[mat]
                    for j in range(step):
                        rows = slabs[layer, 0, pl.ds(base + j, count, stride=step), :]
                        out[pl.ds(base + j * count, count), :] = rows.astype(BF)


def prepare(plan, me, slabs, lines):
    lines = jnp.pad(lines, ((0, 0), (0, -lines.shape[1] % LANES)))
    return pl.pallas_call(
        functools.partial(prep_kernel, plan),
        out_shape=[shape((plan.span, LANES), BF)] * LAYERS,
        in_specs=[SM, VM, VM],
        out_specs=[VM] * LAYERS,
        compiler_params=params_of(),
        name="prep",
    )(me, slabs, lines)


def qkv_kernel(pieces, me, x, vec, whole, normed, out0, out1, out2, out3, weight, qkv, sem):
    load_matrix(whole, weight, 0, pieces, sem)
    hat, _ = norm_parts(x[...].astype(F32))
    normed[...] = (hat * vec[0:1, :] + vec[1:2, :]).astype(BF)
    wait_all(weight, sem)
    for b in range(3 * GROUP):
        kind, at = b // GROUP, b % GROUP
        acc = nn(normed[...], jnp.concatenate([weight[2 * b], weight[2 * b + 1]], axis=1))
        if kind != 1:
            row = 2 if kind == 0 else 3
            acc = acc + vec[row : row + 1, at * WIDE : (at + 1) * WIDE]
        qkv[b] = acc.astype(BF)
    mine = place_of(me[0])
    for r, out in enumerate((out0, out1, out2, out3)):
        for kind in range(3):
            out[:, kind * WIDE : (kind + 1) * WIDE] = qkv[kind * GROUP + (mine ^ TURN[r])]


def qkv_call(plan, me, x, vec, whole):
    rows = x.shape[0]
    return pl.pallas_call(
        functools.partial(qkv_kernel, plan.pieces),
        out_shape=[shape((rows, D), BF)] + [shape((rows, 3 * WIDE), BF)] * GROUP,
        in_specs=[SM, VM, VM, ANY],
        out_specs=[VM] * 5,
        scratch_shapes=[
            pltpu.VMEM((3 * D // LANES, D, LANES), BF),
            pltpu.VMEM((3 * GROUP, rows, WIDE), BF),
            pltpu.SemaphoreType.DMA,
        ],
        compiler_params=params_of(),
        name="qkv",
    )(me, x, vec, whole)


def diagonal(rows):
    return lax.broadcasted_iota(jnp.int32, (rows, rows), 1) <= lax.broadcasted_iota(jnp.int32, (rows, rows), 0)


def attend_kernel(me, in0, in1, in2, in3, out0, out1, out2, out3, lse, q, k, v, o):
    mine = place_of(me[0])
    rows = in0.shape[0]
    for r, ref in enumerate((in0, in1, in2, in3)):
        at = pl.ds(pl.multiple_of((mine ^ TURN[r]) * rows, rows), rows)
        q[at, :] = ref[:, 0:WIDE]
        k[at, :] = ref[:, WIDE : 2 * WIDE]
        v[at, :] = ref[:, 2 * WIDE : 3 * WIDE]
    seen = diagonal(rows)
    for h in range(WIDE // HEAD):
        cols = slice(h * HEAD, (h + 1) * HEAD)
        for i in range(GROUP):
            here = slice(i * rows, (i + 1) * rows)
            qi = q[here, cols]
            near = jnp.where(seen, nt(qi, k[here, cols]) * 0.125, -1000000000.0)
            top = jnp.max(near, axis=1, keepdims=True)
            if i:
                far = nt(qi, k[0 : i * rows, cols]) * 0.125
                top = jnp.maximum(top, jnp.max(far, axis=1, keepdims=True))
                far = jnp.exp(far - top)
            near = jnp.exp(near - top)
            total = jnp.sum(near, axis=1, keepdims=True)
            if i:
                total = total + jnp.sum(far, axis=1, keepdims=True)
            inv = 1.0 / total
            res = nn((near * inv).astype(BF), v[here, cols])
            if i:
                res = res + nn((far * inv).astype(BF), v[0 : i * rows, cols])
            o[i, :, cols] = res.astype(BF)
            lse[here, h : h + 1] = top + jnp.log(total)
    for r, out in enumerate((out0, out1, out2, out3)):
        out[...] = o[mine ^ TURN[r]]


def attend_call(me, heads):
    rows = heads[0].shape[0]
    span = GROUP * rows
    return pl.pallas_call(
        attend_kernel,
        out_shape=[shape((rows, WIDE), BF)] * GROUP + [shape((span, LANES), F32)],
        in_specs=[SM] + [VM] * GROUP,
        out_specs=[VM] * 5,
        scratch_shapes=[pltpu.VMEM((span, WIDE), BF)] * 3 + [pltpu.VMEM((GROUP, rows, WIDE), BF)],
        compiler_params=params_of(),
        name="attend",
    )(me, *heads)


def side(ref, at, count=2):
    return jnp.concatenate([ref[at + i] for i in range(count)], axis=1)


def rows_of(ref, at):
    return jnp.concatenate([ref[p, at, :] for p in range(D // LANES)], axis=1)


def ff_kernel(
    pieces, me, in0, in1, in2, in3, x, vec, bias, whole,
    attended, hidden, normed, upper, active, out,
    wo, we, wr, parts, sems,
):
    load_matrix(whole, wo, 1, pieces, sems.at[0])
    load_matrix(whole, we, 2, pieces, sems.at[1])
    load_matrix(whole, wr, 3, pieces, sems.at[2])
    mine = place_of(me[0])
    for r, ref in enumerate((in0, in1, in2, in3)):
        parts[mine ^ TURN[r]] = ref[...]
    for g in range(GROUP):
        attended[:, g * WIDE : (g + 1) * WIDE] = parts[g]
    wait_all(wo, sems.at[0])
    for g in range(GROUP):
        cols = slice(g * WIDE, (g + 1) * WIDE)
        hidden[:, cols] = x[:, cols] + nn(attended[...], side(wo, 2 * g)) + vec[4:5, cols]
    hat, _ = norm_parts(hidden[...])
    normed[...] = (hat * vec[5:6, :] + vec[6:7, :]).astype(BF)
    out[...] = hidden[...] + vec[11:12, :]
    wait_all(we, sems.at[1])
    wait_all(wr, sems.at[2])

    def body(n, _):
        u = nn(normed[...], side(we, 2 * n)) + bias[n]
        upper[n] = u
        act = (0.5 * u * (1.0 + jnp.tanh(gelu_c * (u + gelu_a * u * u * u)))).astype(BF)
        active[n] = act
        out[...] += nn(act, rows_of(wr, pl.ds(pl.multiple_of(n * WIDE, WIDE), WIDE)))
        return 0

    lax.fori_loop(0, CHUNKS, body, 0)


def ff_call(plan, me, heads, x, vec, bias, whole):
    rows = x.shape[0]
    return pl.pallas_call(
        functools.partial(ff_kernel, plan.pieces),
        out_shape=[
            shape((rows, D), BF),
            shape((rows, D), F32),
            shape((rows, D), BF),
            shape((CHUNKS, rows, WIDE), F32),
            shape((CHUNKS, rows, WIDE), BF),
            shape((rows, D), F32),
        ],
        in_specs=[SM] + [VM] * 7 + [ANY],
        out_specs=[VM] * 6,
        scratch_shapes=[
            pltpu.VMEM((D // LANES, D, LANES), BF),
            pltpu.VMEM((FF // LANES, D, LANES), BF),
            pltpu.VMEM((D // LANES, FF, LANES), BF),
            pltpu.VMEM((GROUP, rows, WIDE), BF),
            pltpu.SemaphoreType.DMA((3,)),
        ],
        compiler_params=params_of(),
        name="ff",
    )(me, *heads, x, vec, bias, whole)


def ff_back_kernel(
    pieces, me, dy, upper, hidden, vec, whole,
    dyb, dub, dh, dhb, out0, out1, out2, out3, bias_grad, vec_grad,
    wo, we, wr, acc, parts, sems,
):
    load_matrix(whole, wr, 3, pieces, sems.at[2])
    load_matrix(whole, we, 2, pieces, sems.at[1])
    load_matrix(whole, wo, 1, pieces, sems.at[0])
    dyb[...] = dy[...].astype(BF)
    vec_grad[0:1, :] = jnp.sum(dy[...], axis=0, keepdims=True)
    acc[...] = jnp.zeros_like(acc)
    wait_all(wr, sems.at[2])
    wait_all(we, sems.at[1])

    def body(n, _):
        dg = nt(dyb[...], rows_of(wr, pl.ds(pl.multiple_of(n * WIDE, WIDE), WIDE)))
        u = upper[n]
        t = jnp.tanh(gelu_c * (u + gelu_a * u * u * u))
        slope = 0.5 * (1.0 + t) + 0.5 * u * (1.0 - t * t) * (gelu_c * (1.0 + 3.0 * gelu_a * u * u))
        du = dg * slope
        bias_grad[n] = jnp.sum(du, axis=0, keepdims=True)
        low = du.astype(BF)
        dub[n] = low
        acc[...] += nt(low, side(we, 2 * n))
        return 0

    lax.fori_loop(0, CHUNKS, body, 0)
    back, gain, shift = norm_back(hidden[...], vec[5:6, :], acc[...])
    total = dy[...] + back
    vec_grad[1:2, :] = gain
    vec_grad[2:3, :] = shift
    vec_grad[3:4, :] = jnp.sum(total, axis=0, keepdims=True)
    vec_grad[4:8, :] = jnp.zeros((4, D), F32)
    dh[...] = total
    dhb[...] = total.astype(BF)
    wait_all(wo, sems.at[0])
    for g in range(GROUP):
        parts[g] = nt(dhb[...], rows_of(wo, slice(g * WIDE, (g + 1) * WIDE))).astype(BF)
    mine = place_of(me[0])
    for r, out in enumerate((out0, out1, out2, out3)):
        out[...] = parts[mine ^ TURN[r]]


def ff_back_call(plan, me, dy, upper, hidden, vec, whole):
    rows = dy.shape[0]
    return pl.pallas_call(
        functools.partial(ff_back_kernel, plan.pieces),
        out_shape=[
            shape((rows, D), BF),
            shape((CHUNKS, rows, WIDE), BF),
            shape((rows, D), F32),
            shape((rows, D), BF),
        ]
        + [shape((rows, WIDE), BF)] * GROUP
        + [shape((CHUNKS, 1, WIDE), F32), shape((8, D), F32)],
        in_specs=[SM] + [VM] * 4 + [ANY],
        out_specs=[VM] * 10,
        scratch_shapes=[
            pltpu.VMEM((D // LANES, D, LANES), BF),
            pltpu.VMEM((FF // LANES, D, LANES), BF),
            pltpu.VMEM((D // LANES, FF, LANES), BF),
            pltpu.VMEM((rows, D), F32),
            pltpu.VMEM((GROUP, rows, WIDE), BF),
            pltpu.SemaphoreType.DMA((3,)),
        ],
        compiler_params=params_of(),
        name="ff_back",
    )(me, dy, upper, hidden, vec, whole)


def attend_back_kernel(
    me, in0, in1, in2, in3, do0, do1, do2, do3, lse,
    out0, out1, out2, out3, sums,
    q, k, v, do, dq, dk, dv,
):
    mine = place_of(me[0])
    rows = in0.shape[0]
    for r, (ref, grad) in enumerate(((in0, do0), (in1, do1), (in2, do2), (in3, do3))):
        at = pl.ds(pl.multiple_of((mine ^ TURN[r]) * rows, rows), rows)
        q[at, :] = ref[:, 0:WIDE]
        k[at, :] = ref[:, WIDE : 2 * WIDE]
        v[at, :] = ref[:, 2 * WIDE : 3 * WIDE]
        do[at, :] = grad[...]
    seen = diagonal(rows)
    for h in range(WIDE // HEAD):
        cols = slice(h * HEAD, (h + 1) * HEAD)
        total = jnp.zeros((1, HEAD), F32)
        for i in reversed(range(GROUP)):
            here = slice(i * rows, (i + 1) * rows)
            past = slice(0, i * rows)
            qi, doi, ls = q[here, cols], do[here, cols], lse[here, h : h + 1]
            near = jnp.exp(jnp.where(seen, nt(qi, k[here, cols]) * 0.125, -1000000000.0) - ls)
            dnear = nt(doi, v[here, cols])
            inner = jnp.sum(near * dnear, axis=1, keepdims=True)
            if i:
                far = jnp.exp(nt(qi, k[past, cols]) * 0.125 - ls)
                dfar = nt(doi, v[past, cols])
                inner = inner + jnp.sum(far * dfar, axis=1, keepdims=True)
            snear = (near * (dnear - inner) * 0.125).astype(BF)
            res = nn(snear, k[here, cols])
            dkn = tn(snear, qi)
            dvn = tn(near.astype(BF), doi)
            last = i == GROUP - 1
            dk[here, cols] = dkn if last else dk[here, cols] + dkn
            dv[here, cols] = dvn if last else dv[here, cols] + dvn
            if i:
                sfar = (far * (dfar - inner) * 0.125).astype(BF)
                res = res + nn(sfar, k[past, cols])
                dkf = tn(sfar, qi)
                dvf = tn(far.astype(BF), doi)
                dk[past, cols] = dkf if last else dk[past, cols] + dkf
                dv[past, cols] = dvf if last else dv[past, cols] + dvf
            total = total + jnp.sum(res, axis=0, keepdims=True)
            dq[i, :, cols] = res.astype(BF)
        sums[0:1, cols] = total
    sums[1:2, :] = jnp.sum(dv[...], axis=0, keepdims=True)
    sums[2:8, :] = jnp.zeros((6, WIDE), F32)
    for r, out in enumerate((out0, out1, out2, out3)):
        at = pl.ds(pl.multiple_of((mine ^ TURN[r]) * rows, rows), rows)
        out[:, 0:WIDE] = dq[mine ^ TURN[r]]
        out[:, WIDE : 2 * WIDE] = dk[at, :].astype(BF)
        out[:, 2 * WIDE : 3 * WIDE] = dv[at, :].astype(BF)


def attend_back_call(me, heads, grads, lse):
    rows = heads[0].shape[0]
    span = GROUP * rows
    return pl.pallas_call(
        attend_back_kernel,
        out_shape=[shape((rows, 3 * WIDE), BF)] * GROUP + [shape((8, WIDE), F32)],
        in_specs=[SM] + [VM] * 9,
        out_specs=[VM] * 5,
        scratch_shapes=[pltpu.VMEM((span, WIDE), BF)] * 4
        + [pltpu.VMEM((GROUP, rows, WIDE), BF)]
        + [pltpu.VMEM((span, WIDE), F32)] * 2,
        compiler_params=params_of(),
        name="attend_back",
    )(me, *heads, *grads, lse)


def qkv_back_kernel(pieces, me, in0, in1, in2, in3, dh, x, vec, whole, mixed, dx, vec_grad, weight, acc, sem):
    load_matrix(whole, weight, 0, pieces, sem)
    mine = place_of(me[0])
    for r, ref in enumerate((in0, in1, in2, in3)):
        mixed[mine ^ TURN[r]] = ref[...]
    acc[...] = jnp.zeros_like(acc)
    wait_all(weight, sem)

    for b in range(3 * GROUP):
        kind, at = b // GROUP, b % GROUP
        acc[...] += nt(mixed[at, :, kind * WIDE : (kind + 1) * WIDE], side(weight, 2 * b))
    back, gain, shift = norm_back(x[...].astype(F32), vec[0:1, :], acc[...])
    dx[...] = dh[...] + back
    vec_grad[0:1, :] = gain
    vec_grad[1:2, :] = shift
    vec_grad[2:8, :] = jnp.zeros((6, D), F32)


def qkv_back_call(plan, me, grads, dh, x, vec, whole):
    rows = x.shape[0]
    return pl.pallas_call(
        functools.partial(qkv_back_kernel, plan.pieces),
        out_shape=[shape((GROUP, rows, 3 * WIDE), BF), shape((rows, D), F32), shape((8, D), F32)],
        in_specs=[SM] + [VM] * 7 + [ANY],
        out_specs=[VM] * 3,
        scratch_shapes=[
            pltpu.VMEM((3 * D // LANES, D, LANES), BF),
            pltpu.VMEM((rows, D), F32),
            pltpu.SemaphoreType.DMA,
        ],
        compiler_params=params_of(),
        name="qkv_back",
    )(me, *grads, dh, x, vec, whole)


def weight_items(pieces, core):
    items = []
    for d in range(core, len(pieces), 2):
        for mat, k0, k1, base in pieces[d]:
            count, step = k1 - k0, PANELS[mat]
            k = k0
            while k < k1:
                n = min(WIDE - k % WIDE, k1 - k) if mat == 3 else k1 - k0
                if step == 2:
                    groups = [range(j, 4 * step, step) for j in range(step)]
                else:
                    groups = [range(2 * i, 2 * i + 2) for i in range(2 * step)]
                for group in groups:
                    low = base + group[0] % step * count + k - k0
                    items.append((low, d, mat, base - k0, count, k, n, group))
                k += n
    return items


def weight_part(items, own, other, out, arrive):
    normed1, attended, normed2, active, mixed, dhb, dub, dyb = zip(own, other)
    everything = slice(None)

    def both(pair, *at):
        arrive(pair[0])
        return jnp.concatenate([ref[at] for ref in pair], axis=0)

    def panels(pair, group):
        return jnp.concatenate([both(pair, everything, slice(p * LANES, (p + 1) * LANES)) for p in group], axis=1)

    turned = {}
    for _, d, mat, base, count, k, n, group in items:
        if (d, mat, k) not in turned:
            if mat == 3:
                lhs = both(active, k // WIDE, everything, slice(k % WIDE, k % WIDE + n))
            else:
                lhs = both((normed1, attended, normed2)[mat], everything, slice(k, k + n))
            turned[d, mat, k] = lhs.T
        if mat == 0:
            at = group[0] // 2
            rhs = both(mixed, at % GROUP, everything, slice(at // GROUP * WIDE, (at // GROUP + 1) * WIDE))
        elif mat == 2:
            rhs = both(dub, group[0] // 2)
        else:
            rhs = panels(dhb if mat == 1 else dyb, group)
        res = nn(turned[d, mat, k], rhs).astype(BF)
        step = PANELS[mat]
        for i, p in enumerate(group):
            at = base + k + (p % step) * count
            out[p // step, d // 2, at : at + n, :] = res[:, i * LANES : (i + 1) * LANES]


LOAD_ORDER = (0, 4, 1, 5, 2, 6, 3, 7)


class Loader:
    def __init__(self, sources, targets, sems):
        self.copies = [pltpu.make_async_copy(a, b, sems.at[i]) for i, (a, b) in enumerate(zip(sources, targets))]
        self.targets, self.pending = targets, []
        for i in LOAD_ORDER:
            self.copies[i].start()
            self.copies[i + 8].start()

    def begin(self):
        self.pending = list(range(8))

    def arrive(self, ref):
        for i in list(self.pending):
            if self.targets[i] is ref:
                self.finish((i,))

    def finish(self, which=None):
        for i in list(self.pending) if which is None else which:
            self.copies[i].wait()
            self.copies[i + 8].wait()
            self.pending.remove(i)


def weight_kernel(pieces, thirds, me, *refs):
    held, (out, grads, sems, leave) = refs[17:33], (refs[16], *refs[33:])
    loader = Loader(refs[:16], held, sems)
    flushes = []
    groups = grads.shape[2] // thirds
    for group in range(groups):
        for core in range(2):

            @pl.when(me[0] % 2 == core)
            def _(core=core):
                if group == 0:
                    loader.begin()
                items = [item for item in weight_items(pieces, core) if item[0] // thirds == group]
                weight_part(items, held[:8], held[8:], grads, loader.arrive)
                loader.finish()

        rows = pl.ds(group * thirds, thirds)
        flushes.append(pltpu.make_async_copy(grads.at[:, :, rows], out.at[:, :, rows], leave.at[group]))
        flushes[-1].start()
    for copy in flushes:
        copy.wait()


def weight_call(plan, me, own, other):
    dims = (4, plan.n_dp // 2, plan.size, LANES)
    thirds = plan.size // 3
    return pl.pallas_call(
        functools.partial(weight_kernel, plan.pieces, thirds),
        out_shape=shape(dims, BF),
        in_specs=[SM] + [ANY] * 16,
        out_specs=ANY,
        scratch_shapes=[pltpu.VMEM(x.shape, BF) for x in (*own, *other)]
        + [pltpu.VMEM(dims, BF), pltpu.SemaphoreType.DMA((16,)), pltpu.SemaphoreType.DMA((3,))],
        compiler_params=params_of(),
        name="weight_grads",
    )(me, *own, *other)


def adam_parts(grad, moment, square, master, weight_decay):
    moment_next = beta_one * moment + (1.0 - beta_one) * grad
    square_next = beta_two * square + (1.0 - beta_two) * grad * grad
    corrected = moment_next / (1.0 - beta_one**STEP)
    scaled = square_next / (1.0 - beta_two**STEP)
    update = -rate * (corrected / (jnp.sqrt(scaled) + adam_eps) + weight_decay * master)
    return moment_next, square_next, update


def adam_kernel(plan, me, *refs):
    owned, (master, moment, square, grad, moment_next, square_next, update) = refs[:LAYERS], refs[LAYERS:]
    for layer in range(LAYERS):
        for d, held in enumerate(plan.pieces):

            @pl.when((pl.program_id(0) == layer) & (me[0] == d))
            def _(layer=layer, held=held):
                for mat, k0, k1, base in held:
                    size, step = k1 - k0, PANELS[mat]
                    for j in range(step):
                        rows = owned[layer][pl.ds(base + j * size, size), :]
                        grad[0, 0, pl.ds(base + j, size, stride=step), :] = rows

    new = adam_parts(grad[0, 0], moment[0, 0], square[0, 0], master[0, 0], decay)
    moment_next[0, 0], square_next[0, 0], update[0, 0] = new


def adam_call(plan, me, owned, master, moment, square):
    block = pl.BlockSpec((1, 1) + master.shape[2:], lambda layer: (layer, 0, 0, 0))
    whole = pl.BlockSpec(owned[0].shape, lambda layer: (0, 0))
    return pl.pallas_call(
        functools.partial(adam_kernel, plan),
        grid=(LAYERS,),
        out_shape=[shape(master.shape, F32)] * 4,
        in_specs=[SM] + [whole] * LAYERS + [block] * 3,
        out_specs=[block] * 4,
        compiler_params=params_of(),
        name="adam",
    )(me, *owned, master, moment, square)


class Wire:
    def __init__(self, send, recv):
        self.d, self.z = lax.axis_index("dp"), lax.axis_index("ctx")
        self.place = place_of(self.d)
        self.send, self.recv, self.next = send, recv, 0

    def copy(self, src, dst, d, z, at=None):
        slot = self.next
        self.next += 1
        return pltpu.make_async_remote_copy(
            src_ref=src, dst_ref=dst, send_sem=self.send.at[slot], recv_sem=self.recv.at[slot],
            device_id=(d, z), device_id_type=MESH,
        )

    def push(self, src, dst, flip_dp, flip_ctx):
        copy = self.copy(src, dst, self.d ^ flip_dp, self.z ^ flip_ctx)
        copy.start()
        return copy

    def greet(self, flips, swaps=False):
        barrier = pltpu.get_barrier_semaphore()
        for fd, fz in flips:
            pl.semaphore_signal(barrier, inc=1, device_id=(self.d ^ fd, self.z ^ fz), device_id_type=MESH)
        if not swaps:
            pl.semaphore_wait(barrier, len(flips))
            return

        @pl.when(self.place != self.z)
        def _():
            pl.semaphore_signal(barrier, inc=1, device_id=self.opposite(), device_id_type=MESH)
            pl.semaphore_wait(barrier, len(flips) + 1)

        @pl.when(self.place == self.z)
        def _():
            pl.semaphore_wait(barrier, len(flips))

    def opposite(self):
        return (self.d - self.d % GROUP + place_of(self.z), self.place)

    def swap(self, src, dst):
        copy = self.copy(src, dst, *self.opposite())

        @pl.when(self.place != self.z)
        def _():
            copy.start()

        @pl.when(self.place == self.z)
        def _():
            dst[...] = src[...]

        def finish():
            @pl.when(self.place != self.z)
            def _():
                copy.wait()

        return finish

    def post(self, blocks, into):
        base = self.next
        self.next += GROUP
        first = self.d - self.d % GROUP

        def copy(g, sender):
            return pltpu.make_async_remote_copy(
                src_ref=blocks.at[g], dst_ref=into.at[self.place],
                send_sem=self.send.at[base + g], recv_sem=self.recv.at[base + sender],
                device_id=(first + place_of(g), self.z), device_id_type=MESH,
            )

        def send(g):
            @pl.when(self.place != g)
            def _():
                copy(g, self.place).start()

            @pl.when(self.place == g)
            def _():
                into[g] = blocks[g]

        def finish():
            for r in range(1, GROUP):
                copy(0, self.place ^ r).wait_recv()
            for g in range(GROUP):

                @pl.when(self.place != g)
                def _(g=g):
                    copy(g, self.place).wait_send()

        return send, finish

    def trade(self, blocks, into):
        copies = []
        for r in (2, 3, 1):
            copies.append(self.push(blocks.at[self.place ^ TURN[r]], into.at[self.place], r, 0))
        into[self.place] = blocks[self.place]
        return copies


def drive(jobs, late):
    live = list(zip(jobs, late))
    step = 0
    while live:
        rest = []
        for job, wait in live:
            if step >= wait:
                try:
                    next(job)
                except StopIteration:
                    continue
                yield
            rest.append((job, wait))
        live = rest
        step += 1


def take(steps, count=1):
    for _ in range(count):
        next(steps, None)


def paced(steps, pace):
    owed = [0.0]

    def advance():
        owed[0] += pace
        while owed[0] >= 1.0:
            owed[0] -= 1.0
            next(steps, None)

    return advance


def unpack_vectors(raw, vec, n_dp, size):
    share = 12 * D // (4 * n_dp) // LANES
    per_row = D // LANES
    for d in range(n_dp):
        for z in range(4):
            lines = raw[z, d].astype(F32)
            for r in range(share):
                at = (d * 4 + z) * share + r
                col = at % per_row * LANES
                vec[at // per_row : at // per_row + 1, col : col + LANES] = lines[r : r + 1, :]


def share_normed(wire, normed, everyone):
    mine = everyone.at[wire.place]
    everyone[wire.place] = normed[...]
    return wire.push(mine, mine, 2, 0), wire.push(mine, mine, 1, 0)


def qkv_part(wire, shared, everyone, weight, vec, q, k, v):
    far, near = shared
    rows = everyone.shape[1]
    cols = pl.ds(pl.multiple_of(wire.place * WIDE, WIDE), WIDE)

    def block(g):
        at = pl.ds(pl.multiple_of(g * rows, rows), rows)
        for kind, target in enumerate((q, k, v)):
            acc = nn(everyone[g], side(weight, 2 * (kind * GROUP + wire.place)))
            if kind != 1:
                row = 2 if kind == 0 else 3
                acc = acc + vec[row : row + 1, cols]
            low = acc.astype(BF)
            target[at, :] = (low.astype(F32) * 0.125).astype(BF) if kind == 0 else low
            yield

    yield from block(wire.place)
    near.wait_recv()
    yield from block(wire.place ^ TURN[1])
    far.wait_recv()
    other = everyone.at[wire.place ^ TURN[2]]
    relay = wire.push(other, other, 1, 0)
    yield from block(wire.place ^ TURN[2])
    relay.wait_recv()
    yield from block(wire.place ^ TURN[3])
    for copy in (far, near, relay):
        copy.wait_send()


def attend_part(q, k, v, o, lse, send):
    rows = o.shape[1]
    seen = diagonal(rows)
    for i in reversed(range(GROUP)):
        for h in range(WIDE // HEAD):
            cols = slice(h * HEAD, (h + 1) * HEAD)
            here = slice(i * rows, (i + 1) * rows)
            qi = q[here, cols]
            near = jnp.where(seen, nt(qi, k[here, cols]), -1000000000.0)
            top = jnp.max(near, axis=1, keepdims=True)
            if i:
                far = nt(qi, k[0 : i * rows, cols])
                top = jnp.maximum(top, jnp.max(far, axis=1, keepdims=True))
                far = jnp.exp(far - top)
            near = jnp.exp(near - top)
            total = jnp.sum(near, axis=1, keepdims=True)
            if i:
                total = total + jnp.sum(far, axis=1, keepdims=True)
            res = nn(near.astype(BF), v[here, cols])
            if i:
                res = res + nn(far.astype(BF), v[0 : i * rows, cols])
            o[i, :, cols] = (res * (1.0 / total)).astype(BF)
            lse[here, h : h + 1] = top + jnp.log(total)
            yield
        send(i)


def ff_part(x, parts, vec, weights, wr_rows, sems, attended, hidden, normed, upper, active, out, made):
    wo, we, wr = weights
    for g in range(GROUP):
        attended[:, g * WIDE : (g + 1) * WIDE] = parts[g]
    wait_all(wo, sems[0])
    for g in range(GROUP):
        cols = slice(g * WIDE, (g + 1) * WIDE)
        hidden[:, cols] = x[:, cols].astype(F32) + nn(attended[...], side(wo, 2 * g)) + vec[4:5, cols]
        yield
    hat, _ = norm_parts(hidden[...])
    normed[...] = (hat * vec[5:6, :] + vec[6:7, :]).astype(BF)
    out[...] = hidden[...] + vec[11:12, :]
    wait_all(we, sems[1])
    wait_all(wr, sems[2])
    yield
    for n in range(CHUNKS):
        row, col = 7 + n // GROUP, n % GROUP * WIDE
        u = nn(normed[...], side(we, 2 * n)) + vec[row : row + 1, col : col + WIDE]
        upper[n] = u
        act = (0.5 * u * (1.0 + jnp.tanh(gelu_c * (u + gelu_a * u * u * u)))).astype(BF)
        active[n] = act
        yield
        if n % GROUP == GROUP - 1:
            quarter = jnp.concatenate([active[n - i] for i in reversed(range(GROUP))], axis=1)
            out[...] += nn(quarter, wr_rows(n // GROUP))
            made(n)
            yield


def ring_reader(upper, ring, sems):
    def fetch(n):
        return pltpu.make_async_copy(upper.at[n], ring.at[n % 2], sems[n % 2])

    fetch(0).start()

    def read(n):
        if n + 1 < CHUNKS:
            fetch(n + 1).start()
        fetch(n).wait()
        return ring[n % 2]

    return read


def ff_back_part(dy, read_upper, hidden, vec, weights, sems, dyb, dub, dh, dhb, blocks, acc, bias_grad, vec_grad):
    wo, we, wr = weights
    dyb[...] = dy[...].astype(BF)
    vec_grad[0:1, :] = jnp.sum(dy[...].astype(F32), axis=0, keepdims=True)
    if sems:
        wait_all(wr, sems[2])
        wait_all(we, sems[1])
    for n in range(CHUNKS):
        at = n * WIDE % D
        dg = nt(dyb[...], side_rows(wr, n * WIDE // D, slice(at, at + WIDE)))
        u = read_upper(n)
        t = jnp.tanh(gelu_c * (u + gelu_a * u * u * u))
        slope = 0.5 * (1.0 + t) + 0.5 * u * (1.0 - t * t) * (gelu_c * (1.0 + 3.0 * gelu_a * u * u))
        du = dg * slope
        row, col = n // GROUP, n % GROUP * WIDE
        bias_grad[row : row + 1, col : col + WIDE] = jnp.sum(du, axis=0, keepdims=True)
        low = du.astype(BF)
        dub[n] = low
        yield
        if n % GROUP == GROUP - 1:
            quarter = jnp.concatenate([dub[n - i] for i in reversed(range(GROUP))], axis=1)
            more = nt(quarter, side(we, 2 * (n - GROUP + 1), 2 * GROUP))
            acc[...] = more if n < GROUP else acc[...] + more
            yield
    back, gain, shift = norm_back(hidden[...], vec[5:6, :], acc[...])
    total = dy[...].astype(F32) + back
    vec_grad[1:2, :] = gain
    vec_grad[2:3, :] = shift
    vec_grad[3:4, :] = jnp.sum(total, axis=0, keepdims=True)
    dh[...] = total
    dhb[...] = total.astype(BF)
    if sems:
        wait_all(wo, sems[0])
    yield
    for g in range(GROUP):
        blocks[g] = nt(dhb[...], rows_of(wo, slice(g * WIDE, (g + 1) * WIDE))).astype(BF)
    yield


def side_rows(ref, at, rows):
    return jnp.concatenate([ref[p * 4 + at, rows, :] for p in range(D // LANES)], axis=1)


def attend_back_part(q, k, v, do, lse, dm, dk, dv, sums, send):
    rows = dm.shape[1]
    seen = diagonal(rows)
    sums[...] = jnp.zeros_like(sums)
    for i in reversed(range(GROUP)):
        here = slice(i * rows, (i + 1) * rows)
        past = slice(0, i * rows)
        last = i == GROUP - 1
        for h in range(WIDE // HEAD):
            cols = slice(h * HEAD, (h + 1) * HEAD)
            qi, doi, ls = q[here, cols], do[i, :, cols], lse[here, h : h + 1]
            near = jnp.exp(jnp.where(seen, nt(qi, k[here, cols]), -1000000000.0) - ls)
            dnear = nt(doi, v[here, cols])
            inner = jnp.sum(near * dnear, axis=1, keepdims=True)
            if i:
                far = jnp.exp(nt(qi, k[past, cols]) - ls)
                dfar = nt(doi, v[past, cols])
                inner = inner + jnp.sum(far * dfar, axis=1, keepdims=True)
            snear = (near * (dnear - inner)).astype(BF)
            res = nn(snear, k[here, cols])
            dkn = tn(snear, qi)
            dvn = tn(near.astype(BF), doi)
            dk[here, cols] = dkn if last else dk[here, cols] + dkn
            dv[here, cols] = dvn if last else dv[here, cols] + dvn
            if i:
                sfar = (far * (dfar - inner)).astype(BF)
                res = res + nn(sfar, k[past, cols])
                dkf = tn(sfar, qi)
                dvf = tn(far.astype(BF), doi)
                dk[past, cols] = dkf if last else dk[past, cols] + dkf
                dv[past, cols] = dvf if last else dv[past, cols] + dvf
            res = res * 0.125
            sums[0:1, cols] += jnp.sum(res, axis=0, keepdims=True)
            dm[i, :, cols] = res.astype(BF)
            yield
        dm[i, :, WIDE : 2 * WIDE] = dk[here, :].astype(BF)
        dm[i, :, 2 * WIDE : 3 * WIDE] = dv[here, :].astype(BF)
        sums[1:2, :] += jnp.sum(dv[here, :], axis=0, keepdims=True)
        send(i)


def qkv_back_part(mixed, weight, acc):
    for kind in range(3):
        part = jnp.concatenate([mixed[g, :, kind * WIDE : (kind + 1) * WIDE] for g in range(GROUP)], axis=1)
        more = nt(part, side(weight, 2 * GROUP * kind, 2 * GROUP))
        acc[...] = acc[...] + more if kind else more
        for _ in range(3):
            yield


class Mover:
    def __init__(self, n_dp):
        self.n_dp = n_dp
        self.size, self.pieces = pieces_of(n_dp)
        self.line = 12 * D // (4 * n_dp)
        self.span = self.size + 16

    def gather_all(self, helds):
        wholes = [lax.all_gather(held, ("ctx", "dp"), axis=0, tiled=True) for held in helds]
        return [whole.reshape(4, self.n_dp, self.span, LANES) for whole in wholes]

    def vectors(self, whole):
        rows = -(-self.line // LANES)
        lines = whole[:, :, self.size : self.size + rows].reshape(4, self.n_dp, -1)[:, :, : self.line]
        return lines.transpose(1, 0, 2).reshape(12, D).astype(F32)

    def scatter(self, buffer):
        none = jnp.zeros_like(buffer)
        core = lax.axis_index("dp") % 2
        pair = jnp.stack([jnp.where(core == 0, buffer, none), jnp.where(core == 1, buffer, none)], axis=2)
        flat = pair.reshape(-1, LANES)
        return lax.psum_scatter(flat, ("ctx", "dp"), scatter_dimension=0, tiled=True).astype(F32)

    def scatter_vectors(self, grads):
        return lax.psum_scatter(grads.reshape(-1), ("dp", "ctx"), scatter_dimension=0, tiled=True)


CORE = 1
FLIPS = ((1, 0), (2, 0), (3, 0), (4, 0), (0, 1), (0, 2), (0, 3))


class BitMover(Mover):
    def __init__(self, n_dp):
        super().__init__(n_dp)
        self.gap, self.pace, self.pace_back = 8, (1.3, 4, 2), (1.0, 4, 2, 2, 2.0)
        self.even = self.cut(((4, 4), (2, 2), (4, 4), (2, 2), (4, 4), (2, 2), (4, 4), (2, 2)))
        self.skew = self.cut(((5, 3), (3, 2), (4, 3), (3, 1), (5, 3), (3, 2), (4, 3), (2, 2)))

    def cut(self, plan):
        unit, row, chunks = self.size // 48, 0, []
        for i, pair in enumerate(plan):
            for units, (a, b) in zip(pair, ((2, 4), (4, 2))):
                chunks.append((row, units * unit, (i % 2 == 0, a, b), i // 2 * 2))
                row += units * unit
        return chunks

    def gather_jobs(self, wire, local, helds, wholes, plans, done):
        d, z = wire.d, wire.z

        def job(layer, part):
            low, size, (z_first, a, b), _ = plans[layer][part]
            if part == len(plans[layer]) - 1:
                size = self.span - low
            rows = pl.ds(low, size)
            held, whole = helds[layer].at[rows], wholes[layer]
            started = []

            def push(src, dst, fd, fz):
                started.append(wire.push(src, dst, fd, fz))
                return started[-1]

            def line(dd, fd):
                ref = whole.at[:, dd, rows]
                return push(ref, ref, fd, 0)

            own = pltpu.make_async_copy(held, whole.at[z, d, rows], local.at[layer * len(plans[0]) + part])
            own.start()
            mine = [push(held, whole.at[z, d, rows], 0, k) for k in (3, 2, 1)]
            if z_first:
                yield
                own.wait()
                for copy in mine:
                    copy.wait_recv()
                first = line(d, a)
                second = line(d, b)
                cores = [line(d, CORE)]
                yield
                first.wait_recv()
                third = line(d ^ a, b)
                cores.append(line(d ^ a, CORE))
                yield
                second.wait_recv()
                cores.append(line(d ^ b, CORE))
                yield
                third.wait_recv()
                cores.append(line(d ^ a ^ b, CORE))
            else:
                first = push(held, whole.at[z, d, rows], a, 0)
                yield
                first.wait_recv()
                other = whole.at[z, d ^ a, rows]
                theirs = [push(other, other, 0, k) for k in (3, 2, 1)]
                yield
                own.wait()
                for copy in mine:
                    copy.wait_recv()
                second = line(d, b)
                cores = [line(d, CORE)]
                yield
                for copy in theirs:
                    copy.wait_recv()
                third = line(d ^ a, b)
                cores.append(line(d ^ a, CORE))
                yield
                second.wait_recv()
                cores.append(line(d ^ b, CORE))
                yield
                third.wait_recv()
                cores.append(line(d ^ a ^ b, CORE))
            yield
            for copy in cores:
                copy.wait_recv()
            for copy in started:
                copy.wait_send()
            done[layer] += 1

        jobs = [job(layer, part) for layer, plan in enumerate(plans) for part in range(len(plan))]
        return drive(jobs, [chunk[3] + self.gap * layer for layer, plan in enumerate(plans) for chunk in plan])

    def forward_first(self, helds, tokens):
        rows = tokens.shape[0]
        span = GROUP * rows
        plans = (self.even, self.skew)
        pieces, count, pace = self.pieces, len(self.even), self.pace
        slots = 2 * count * 14 + 16

        def kernel(
            held0, held1, tokens,
            whole0, whole1, value, vec, normed1, heads_out, lse, attended, hidden, normed2, upper_out, active_out, out,
            upper, active, swapped, everyone, q, k, v, o, parts, raw, wa, wo, we, wr, local, sems, send, recv,
        ):
            wire = Wire(send, recv)
            leaving = []

            def leave(src, dst):
                leaving.append(pltpu.make_async_copy(src, dst, sems.at[5 + len(leaving)]))
                leaving[-1].start()

            def made(n):
                if n % 4 == 3:
                    for src, dst in ((upper, upper_out), (active, active_out)):
                        leave(src.at[pl.ds(n - 3, 4)], dst.at[pl.ds(n - 3, 4)])

            wire.greet(FLIPS, swaps=True)
            done = [0, 0]
            comm = self.gather_jobs(wire, local, (held0, held1), (whole0, whole1), plans, done)
            take(comm, 6)
            swap_in = wire.swap(tokens, swapped)
            while done[0] < count:
                next(comm)
            load_vec = pltpu.make_async_copy(whole0.at[:, :, pl.ds(self.size, 16)], raw, sems.at[4])
            load_vec.start()
            load_matrix(whole0, wa, 0, pieces, sems.at[3])
            load_matrix(whole0, wo, 1, pieces, sems.at[0])
            swap_in()
            value[...] = swapped[...]
            load_vec.wait()
            unpack_vectors(raw, vec, self.n_dp, self.size)
            hat, _ = norm_parts(swapped[...].astype(F32))
            normed1[...] = (hat * vec[0:1, :] + vec[1:2, :]).astype(BF)
            shared = share_normed(wire, normed1, everyone)
            wait_all(wa, sems.at[3])
            advance = paced(comm, pace[0])
            for _ in qkv_part(wire, shared, everyone, wa, vec, q, k, v):
                advance()
            load_matrix(whole0, we, 2, pieces, sems.at[1])
            load_matrix(whole0, wr, 3, pieces, sems.at[2])
            take(comm, pace[1])
            for i, ref in enumerate((q, k, v)):
                leave(ref, heads_out.at[i])
            send_o, finish = wire.post(o, parts)
            for _ in attend_part(q, k, v, o, lse, send_o):
                advance()
            take(comm, pace[2])
            finish()
            for _ in ff_part(
                swapped, parts, vec, (wo, we, wr), lambda n: rows_of(wr, slice(n * D, (n + 1) * D)), [sems.at[i] for i in range(3)],
                attended, hidden, normed2, upper, active, out, made,
            ):
                advance()
            for _ in comm:
                pass
            for copy in leaving:
                copy.wait()

        return pl.pallas_call(
            kernel,
            out_shape=[shape((4, self.n_dp, self.span, LANES), BF)] * 2
            + [
                shape((rows, D), BF),
                shape((12, D), F32),
                shape((rows, D), BF),
                shape((3, span, WIDE), BF),
                shape((span, LANES), F32),
                shape((rows, D), BF),
                shape((rows, D), F32),
                shape((rows, D), BF),
                shape((CHUNKS, rows, WIDE), F32),
                shape((CHUNKS, rows, WIDE), BF),
                shape((rows, D), F32),
            ],
            in_specs=[VM] * 3,
            out_specs=[ANY] * 2 + [VM] * 3 + [ANY] + [VM] * 4 + [ANY] * 2 + [VM],
            scratch_shapes=[
                pltpu.VMEM((CHUNKS, rows, WIDE), F32),
                pltpu.VMEM((CHUNKS, rows, WIDE), BF),
                pltpu.VMEM((rows, D), BF),
            ]
            + [pltpu.VMEM((GROUP, rows, D), BF)]
            + [pltpu.VMEM((span, WIDE), BF)] * 3
            + [pltpu.VMEM((GROUP, rows, WIDE), BF)] * 2
            + [
                pltpu.VMEM((4, self.n_dp, 16, LANES), BF),
                pltpu.VMEM((3 * D // LANES, D, LANES), BF),
                pltpu.VMEM((D // LANES, D, LANES), BF),
                pltpu.VMEM((FF // LANES, D, LANES), BF),
                pltpu.VMEM((D // LANES, FF, LANES), BF),
                pltpu.SemaphoreType.DMA((2 * count,)),
                pltpu.SemaphoreType.DMA((16,)),
                pltpu.SemaphoreType.DMA((slots,)),
                pltpu.SemaphoreType.DMA((slots,)),
            ],
            compiler_params=params_of(collective_id=1, has_side_effects=True),
            name="forward_first",
        )(*helds, tokens)

    def scatter_jobs(self, wire, parts):
        d, z = wire.d, wire.z

        def job(grads, acc, from_b, from_a, from_z, order, size, put, local):
            z_first, a, b = order
            started = []

            def push(src, dst, fd, fz):
                started.append(wire.push(src, dst, fd, fz))
                return started[-1]

            places = [(d ^ (ja * a)) // 2 for ja in (1, 0)]
            if acc is None:
                piece = [lambda k, p=p: grads.at[k, p] for p in places]
                pieces = [grads.at[:, p] for p in places]
            else:
                piece = [lambda k, i=i: acc.at[i, k] for i in range(2)]
                pieces = [acc.at[i] for i in range(2)]
            block = min(64, size)

            def add(into, more):
                def body(i, _):
                    at = pl.ds(pl.multiple_of(i * block, block), block)
                    for x, y in zip(into, more):
                        x[at, :] = x[at, :] + y[at, :]
                    return 0

                lax.fori_loop(0, size // block, body, 0)

            def every(i, more):
                add([piece[i](k) for k in range(4)], [more(k) for k in range(4)])

            to_b = [push(grads.at[:, p ^ (b // 2)], from_b.at[i], b, 0) for i, p in enumerate(places)]
            loads = []
            if acc is not None:
                for i in range(2):
                    loads.append(pltpu.make_async_copy(grads.at[:, places[i]], acc.at[i], local[i]))
                    loads[-1].start()
            yield
            for load in loads:
                load.wait()
            to_b[0].wait_recv()
            every(0, lambda k: from_b.at[0, k])
            if z_first:
                to_a = push(pieces[0], from_a, a, 0)
                yield
                to_b[1].wait_recv()
                every(1, lambda k: from_b.at[1, k])
                yield
                to_a.wait_recv()
                every(1, lambda k: from_a.at[k])
                to_z = [push(piece[1](z ^ k), from_z.at[k - 1, 0], 0, k) for k in (3, 2, 1)]
                yield
                more = [from_z.at[k, 0] for k in range(3)]
                last = to_z
            else:
                to_z = [push(piece[0](z ^ k), from_z.at[k - 1, 0], 0, k) for k in (3, 2, 1)]
                yield
                to_b[1].wait_recv()
                every(1, lambda k: from_b.at[1, k])
                to_z1 = [push(piece[1](z ^ k), from_z.at[k - 1, 1], 0, k) for k in (3, 2, 1)]
                yield
                for copy in to_z:
                    copy.wait_recv()
                for k in range(3):
                    add([piece[0](z)], [from_z.at[k, 0]])
                to_a = push(piece[0](z), from_a.at[0], a, 0)
                yield
                more = [from_z.at[k, 1] for k in range(3)] + [from_a.at[0]]
                last = to_z1 + [to_a]
            for copy in last:
                copy.wait_recv()

            def body(i, _):
                at = pl.multiple_of(i * block, block)
                here = pl.ds(at, block)
                value = piece[1](z)[here, :].astype(F32)
                for ref in more:
                    value = value + ref[here, :].astype(F32)
                put(at, block, value)
                return 0

            lax.fori_loop(0, size // block, body, 0)
            for copy in started:
                copy.wait_send()

        return [job(*part) for part in parts]

    def scatter_scratch(self, plan, with_acc):
        result = []
        for _, n, order, _ in plan:
            if with_acc:
                result.append(pltpu.VMEM((2, 4, n, LANES), BF))
            result.append(pltpu.VMEM((2, 4, n, LANES), BF))
            result.append(pltpu.VMEM((4 if order[0] else 1, n, LANES), BF))
            result.append(pltpu.VMEM((3, 1 if order[0] else 2, n, LANES), BF))
        return result

    def scatter_parts(self, plan, grads, scratch, owned, local):
        each = len(scratch) // len(plan)
        parts = []
        for i, (low, n, order, _) in enumerate(plan):
            refs = scratch[i * each : (i + 1) * each]
            acc, (from_b, from_a, from_z) = (refs[0] if each == 4 else None), refs[-3:]

            def put(at, block, value, low=low):
                owned[pl.ds(low + at, block), :] = value

            waits = [local.at[2 * i], local.at[2 * i + 1]] if each == 4 else None
            parts.append((grads.at[:, :, pl.ds(low, n)], acc, from_b, from_a, from_z, order, n, put, waits))
        return parts

    def backward_first(self, me, grads, saved, dy, vec, whole):
        x, normed1, heads, lse, attended, hidden, normed2, upper, active = saved
        rows = x.shape[0]
        span = GROUP * rows
        plan, pieces, pace = self.skew, self.pieces, self.pace_back
        count = len(plan)
        slots = count * 12 + 24
        scratch_count = 4 * count

        def kernel(
            grads, x, normed1, heads, lse, attended, hidden, normed2, upper, active, dy, vec, whole,
            owned, dx, dyb, dub_out, dhb, mixed_out, bias_grad, vec_grad, sums,
            o_normed1, o_attended, o_normed2, o_active, o_mixed, o_dhb, o_dub, o_dyb,
            *scratch,
        ):
            bufs = scratch[:scratch_count]
            dub, mixed, q, k, v, do, blocks, dk, dv, dm, acc, dh, ring, wo, we, wr, local, sems, send, recv = scratch[scratch_count:]
            sems = [sems.at[i] for i in range(10)]
            load_matrix(whole, wr, 3, pieces, sems[2], split=True)
            load_matrix(whole, we, 2, pieces, sems[1])
            load_matrix(whole, wo, 1, pieces, sems[0])
            for i, ref in enumerate((q, k, v)):
                pltpu.make_async_copy(heads.at[i], ref, sems[5]).start()
            wire = Wire(send, recv)
            wire.greet(FLIPS)
            comm = drive(
                self.scatter_jobs(wire, self.scatter_parts(plan, grads, bufs, owned, local)), [chunk[3] for chunk in plan]
            )
            advance = paced(comm, pace[0])
            take(comm, pace[1])
            core = [wire.push(a, b, CORE, 0) for a, b in (
                (normed1, o_normed1), (attended, o_attended), (normed2, o_normed2), (active, o_active))]
            vec_grad[...] = jnp.zeros_like(vec_grad)
            read_upper = ring_reader(upper, ring, sems[3:5])
            for _ in ff_back_part(
                dy, read_upper, hidden, vec, (wo, we, wr), sems, dyb, dub, dh, dhb, blocks, acc, bias_grad, vec_grad
            ):
                advance()
            load_matrix(whole, wr, 0, pieces, sems[6])
            leaving = [pltpu.make_async_copy(dub, dub_out, sems[8]), pltpu.make_async_copy(mixed, mixed_out, sems[9])]
            leaving[0].start()
            core += [wire.push(a, b, CORE, 0) for a, b in ((dyb, o_dyb), (dub, o_dub), (dhb, o_dhb))]
            copies = wire.trade(blocks, do)
            take(comm, pace[2])
            for ref in (q, k, v):
                wait_all(ref, sems[5])
            for copy in copies:
                copy.wait()
            advance = paced(comm, pace[4])
            send_m, finish = wire.post(dm, mixed)
            for _ in attend_back_part(q, k, v, do, lse, dm, dk, dv, sums, send_m):
                advance()
            take(comm, pace[3])
            finish()
            core.append(wire.push(mixed, o_mixed, CORE, 0))
            leaving[1].start()
            wait_all(wr.at[pl.ds(0, 3 * D // LANES)], sems[6])
            for _ in qkv_back_part(mixed, wr, acc):
                advance()
            back, gain, shift = norm_back(x[...].astype(F32), vec[0:1, :], acc[...])
            dx[...] = dh[...] + back
            vec_grad[4:5, :] = gain
            vec_grad[5:6, :] = shift
            for _ in comm:
                pass
            for copy in core + leaving:
                copy.wait()

        token = shape((rows, D), BF)
        wide = shape((CHUNKS, rows, WIDE), BF)
        triple = shape((GROUP, rows, 3 * WIDE), BF)
        return pl.pallas_call(
            kernel,
            out_shape=[
                shape((self.size, LANES), F32),
                shape((rows, D), F32),
                token,
                wide,
                token,
                triple,
                shape((4, D), F32),
                shape((8, D), F32),
                shape((8, WIDE), F32),
            ]
            + [token, token, token, wide, triple, token, wide, token],
            in_specs=[ANY, VM, ANY, ANY, VM, ANY, VM, ANY, ANY, ANY, VM, VM, ANY],
            out_specs=[VM] * 3 + [ANY, VM, ANY] + [VM] * 3 + [ANY] * 8,
            scratch_shapes=self.scatter_scratch(plan, True)
            + [pltpu.VMEM((CHUNKS, rows, WIDE), BF), pltpu.VMEM((GROUP, rows, 3 * WIDE), BF)]
            + [pltpu.VMEM((span, WIDE), BF)] * 3
            + [pltpu.VMEM((GROUP, rows, WIDE), BF)] * 2
            + [pltpu.VMEM((span, WIDE), F32)] * 2
            + [
                pltpu.VMEM((GROUP, rows, 3 * WIDE), BF),
                pltpu.VMEM((rows, D), F32),
                pltpu.VMEM((rows, D), F32),
                pltpu.VMEM((2, rows, WIDE), F32),
                pltpu.VMEM((D // LANES, D, LANES), BF),
                pltpu.VMEM((FF // LANES, D, LANES), BF),
                pltpu.VMEM((4 * D // LANES, D, LANES), BF),
                pltpu.SemaphoreType.DMA((2 * count,)),
                pltpu.SemaphoreType.DMA((10,)),
                pltpu.SemaphoreType.DMA((slots,)),
                pltpu.SemaphoreType.DMA((slots,)),
            ],
            compiler_params=params_of(collective_id=2, has_side_effects=True),
            name="backward_first",
        )(grads, x, normed1, heads, lse, attended, hidden, normed2, upper, active, dy, vec, whole)

    def middle(self, x, cotangent, vec, whole):
        rows = x.shape[0]
        span = GROUP * rows
        pieces = self.pieces
        slots = 40

        def kernel(
            x, cotangent, vec, whole,
            output, dx, normed1, attended, normed2, active_out, mixed_out, dhb, dub_out, dyb,
            o_normed1, o_attended, o_normed2, o_active, o_mixed, o_dhb, o_dub, o_dyb, bias_grad, vec_grad, sums,
            active, mixed, dub, dy, result, returned, everyone, blocks, q, k, v, o, parts, do, lse, hidden, upper, acc, dh, dk, dv, wa, wo, we, wr,
            sems, send, recv,
        ):
            sems = [sems.at[i] for i in range(7)]
            leaving = []

            def leave(src, dst):
                leaving.append(pltpu.make_async_copy(src, dst, sems[4 + len(leaving)]))
                leaving[-1].start()

            load_matrix(whole, wa, 0, pieces, sems[3])
            wire = Wire(send, recv)
            hat, _ = norm_parts(x[...])
            normed1[...] = (hat * vec[0:1, :] + vec[1:2, :]).astype(BF)
            wire.greet(FLIPS, swaps=True)
            shared = share_normed(wire, normed1, everyone)
            core = [wire.push(normed1, o_normed1, CORE, 0)]
            load_matrix(whole, wo, 1, pieces, sems[0])
            wait_all(wa, sems[3])
            for _ in qkv_part(wire, shared, everyone, wa, vec, q, k, v):
                pass
            load_matrix(whole, we, 2, pieces, sems[1])
            load_matrix(whole, wr, 3, pieces, sems[2], split=True)
            swap_in = wire.swap(cotangent, dy)
            send_o, finish = wire.post(o, parts)
            for _ in attend_part(q, k, v, o, lse, send_o):
                pass
            finish()
            for _ in ff_part(
                x, parts, vec, (wo, we, wr), lambda n: side_rows(wr, n, slice(0, D)),
                sems, attended, hidden, normed2, upper, active, dx, lambda n: None,
            ):
                pass
            core += [wire.push(a, b, CORE, 0) for a, b in (
                (attended, o_attended), (normed2, o_normed2), (active, o_active))]
            leave(active, active_out)
            result[...] = dx[...].astype(BF)
            swap_out = wire.swap(result, returned)
            swap_in()
            vec_grad[...] = jnp.zeros_like(vec_grad)
            for _ in ff_back_part(
                dy, lambda n: upper[n], hidden, vec, (wo, we, wr), None, dyb, dub, dh, dhb, o, acc, bias_grad, vec_grad
            ):
                pass
            leave(dub, dub_out)
            copies = wire.trade(o, do)
            core += [wire.push(a, b, CORE, 0) for a, b in ((dyb, o_dyb), (dub, o_dub), (dhb, o_dhb))]
            for copy in copies:
                copy.wait()
            send_m, finish = wire.post(blocks, mixed)
            for _ in attend_back_part(q, k, v, do, lse, blocks, dk, dv, sums, send_m):
                pass
            finish()
            core.append(wire.push(mixed, o_mixed, CORE, 0))
            leave(mixed, mixed_out)
            for _ in qkv_back_part(mixed, wa, acc):
                pass
            back, gain, shift = norm_back(x[...], vec[0:1, :], acc[...])
            dx[...] = dh[...] + back
            vec_grad[4:5, :] = gain
            vec_grad[5:6, :] = shift
            swap_out()
            output[...] = returned[...]
            for copy in core + leaving:
                copy.wait()

        token = shape((rows, D), BF)
        wide = shape((CHUNKS, rows, WIDE), BF)
        triple = shape((GROUP, rows, 3 * WIDE), BF)
        kept = [token, token, token, wide, triple, token, wide, token]
        return pl.pallas_call(
            kernel,
            out_shape=[token, shape((rows, D), F32)] + kept * 2
            + [shape((4, D), F32), shape((8, D), F32), shape((8, WIDE), F32)],
            in_specs=[VM, VM, VM, ANY],
            out_specs=[VM] * 5 + [ANY, ANY, VM, ANY, VM] + [ANY] * 8 + [VM] * 3,
            scratch_shapes=[
                pltpu.VMEM((CHUNKS, rows, WIDE), BF),
                pltpu.VMEM((GROUP, rows, 3 * WIDE), BF),
                pltpu.VMEM((CHUNKS, rows, WIDE), BF),
            ]
            + [pltpu.VMEM((rows, D), BF)] * 3
            + [pltpu.VMEM((GROUP, rows, D), BF), pltpu.VMEM((GROUP, rows, 3 * WIDE), BF)]
            + [pltpu.VMEM((span, WIDE), BF)] * 3
            + [pltpu.VMEM((GROUP, rows, WIDE), BF)] * 3
            + [
                pltpu.VMEM((span, LANES), F32),
                pltpu.VMEM((rows, D), F32),
                pltpu.VMEM((CHUNKS, rows, WIDE), F32),
                pltpu.VMEM((rows, D), F32),
                pltpu.VMEM((rows, D), F32),
                pltpu.VMEM((span, WIDE), F32),
                pltpu.VMEM((span, WIDE), F32),
                pltpu.VMEM((3 * D // LANES, D, LANES), BF),
                pltpu.VMEM((D // LANES, D, LANES), BF),
                pltpu.VMEM((FF // LANES, D, LANES), BF),
                pltpu.VMEM((4 * D // LANES, D, LANES), BF),
                pltpu.SemaphoreType.DMA((7,)),
                pltpu.SemaphoreType.DMA((slots,)),
                pltpu.SemaphoreType.DMA((slots,)),
            ],
            compiler_params=params_of(collective_id=4, has_side_effects=True),
            name="middle",
        )(x, cotangent, vec, whole)

    def scatter_first(self, own, other, vectors0, vectors1):
        plan, pieces, thirds = self.even, self.pieces, self.size // 3
        count = len(plan)
        slots = count * 12 + 24
        scratch_count = 3 * count

        def kernel(*refs):
            vectors, (owned, vec_owned) = (refs[16:19], refs[19:22]), refs[22:24]
            scratch = refs[24:]
            bufs, scratch = scratch[:scratch_count], scratch[scratch_count:]
            held, scratch = scratch[:16], scratch[16:]
            loader = Loader(refs[:16], held, scratch[0])
            grads, lines, got, small, from_b, from_a, from_z, send, recv = scratch[1:]
            wire = Wire(send, recv)
            wire.greet([flip for flip in FLIPS if flip[0] != 3])
            mine = pl.ds(pl.multiple_of(wire.place * WIDE, WIDE), WIDE)
            for i, (bias_grad, vec_grad, sums) in enumerate(vectors):
                lines[i, 0:2, :] = vec_grad[4:6, :]
                lines[i, 2:4, :] = jnp.zeros((2, D), F32)
                lines[i, 2:4, mine] = sums[0:2, :]
                lines[i, 4:5, :] = vec_grad[3:4, :]
                lines[i, 5:7, :] = vec_grad[1:3, :]
                lines[i, 7:11, :] = bias_grad[...]
                lines[i, 11:12, :] = vec_grad[0:1, :]
            trade = wire.push(lines, got, CORE, 0)

            def make(group):
                for core in range(2):
                    items = [item for item in weight_items(pieces, core) if item[0] // thirds == group]

                    @pl.when(wire.d % 2 == core)
                    def _(items=items):
                        if group == 0:
                            loader.begin()
                        weight_part(items, held[:8], held[8:], grads, loader.arrive)
                        loader.finish()

            def put(at, block, value):
                vec_owned[pl.ds(at, block), :] = value

            parts = self.scatter_parts(plan, grads, bufs, owned, None)
            jobs = self.scatter_jobs(wire, parts)
            made = [0]

            def after(job, rows):
                while made[0] * thirds < rows:
                    make(made[0])
                    made[0] += 1
                yield from job

            jobs = [after(job, low + n) for job, (low, n, _, _) in zip(jobs, plan)]

            def vector_job():
                trade.wait()
                lines[...] = lines[...] + got[...]
                share, per_row = self.line // LANES, D // LANES
                small[...] = jnp.zeros_like(small)
                for core in range(2):

                    @pl.when(wire.d % 2 == core)
                    def _(core=core):
                        for d in range(core, self.n_dp, 2):
                            for z in range(4):
                                for r in range(share):
                                    at = (d * 4 + z) * share + r
                                    row, col = at // per_row, at % per_row * LANES
                                    for i in range(2):
                                        here = slice(i * 4 + r, i * 4 + r + 1)
                                        small[z, d // 2, here, :] = lines[i, row : row + 1, col : col + LANES]

                yield from self.scatter_jobs(wire, [(small, None, from_b, from_a, from_z, (True, 2, 4), 8, put, None)])[0]

            jobs.append(vector_job())
            for _ in drive(jobs, [chunk[3] for chunk in plan] + [1]):
                pass

        return pl.pallas_call(
            kernel,
            out_shape=[shape((self.size, LANES), F32), shape((8, LANES), F32)],
            in_specs=[ANY] * 16 + [VM] * 6,
            out_specs=[VM] * 2,
            scratch_shapes=self.scatter_scratch(plan, False)
            + [pltpu.VMEM(x.shape, BF) for x in (*own, *other)]
            + [
                pltpu.SemaphoreType.DMA((16,)),
                pltpu.VMEM((4, self.n_dp // 2, self.size, LANES), BF),
                pltpu.VMEM((2, 12, D), F32),
                pltpu.VMEM((2, 12, D), F32),
                pltpu.VMEM((4, self.n_dp // 2, 8, LANES), F32),
                pltpu.VMEM((2, 4, 8, LANES), F32),
                pltpu.VMEM((4, 8, LANES), F32),
                pltpu.VMEM((3, 1, 8, LANES), F32),
                pltpu.SemaphoreType.DMA((slots,)),
                pltpu.SemaphoreType.DMA((slots,)),
            ],
            compiler_params=params_of(collective_id=3, has_side_effects=True),
            name="scatter_first",
        )(*own, *other, *vectors0, *vectors1)


def swap(values, n_dp):
    pairs = [
        (d * GROUP + z, ((d // GROUP) * GROUP + place_of(z)) * GROUP + place_of(d % GROUP))
        for d in range(n_dp)
        for z in range(GROUP)
    ]
    return lax.ppermute(values, ("dp", "ctx"), pairs)


def send_core(values, n_dp):
    pairs = [(d * GROUP + z, (d ^ 1) * GROUP + z) for d in range(n_dp) for z in range(GROUP)]
    return lax.ppermute(values, ("dp", "ctx"), pairs)


def trade(arrays, n_dp):
    result = [arrays[0]]
    for r in range(1, GROUP):
        pairs = [(d * GROUP + z, (d ^ r) * GROUP + z) for d in range(n_dp) for z in range(GROUP)]
        result.append(lax.ppermute(arrays[r], ("dp", "ctx"), pairs))
    return result


def per_device(
    n_dp,
    layer_input,
    out_cotangent,
    params,
    vectors,
    param_moment,
    vector_moment,
    param_square,
    vector_square,
):
    plan = BitMover(n_dp) if n_dp == 8 else Mover(n_dp)
    me = jnp.stack([lax.axis_index("dp"), lax.axis_index("ctx")]).astype(jnp.int32)
    place = place_of(me[0])

    helds = prepare(plan, me, params, vectors)
    fused = n_dp == 8
    if fused:
        whole0, whole1, value0, vec0, normed1, heads, *rest, value = plan.forward_first(helds, layer_input)
        wholes, vecs = [whole0, whole1], [vec0, plan.vectors(whole1)]
        first = (value0, normed1, heads, *rest)
    else:
        wholes = plan.gather_all(helds)
        vecs = [plan.vectors(whole) for whole in wholes]
        value = swap(layer_input, n_dp).astype(F32)
        grad = swap(out_cotangent, n_dp).astype(F32)

    saved = [None] * LAYERS
    for layer in range(LAYERS if fused else 0, LAYERS):
        vec, whole = vecs[layer], wholes[layer]
        bias = vec[7:11].reshape(CHUNKS, 1, WIDE)
        normed1, *sent = qkv_call(plan, me, value, vec, whole)
        heads = trade(sent, n_dp)
        *sent, lse = attend_call(me, heads)
        attended, hidden, normed2, upper, active, result = ff_call(
            plan, me, trade(sent, n_dp), value, vec, bias, whole
        )
        saved[layer] = (value, normed1, heads, lse, attended, hidden, normed2, upper, active)
        value = result
    if not fused:
        layer_output = swap(value.astype(BF), n_dp)

    def lines_of(gain_one, shift_one, sums, bias_output, gain_two, shift_two, bias_expand, bias_reduce):
        spread = lax.dynamic_update_slice(jnp.zeros((2, D), F32), sums[0:2], (0, place * WIDE))
        rows = [gain_one, shift_one, spread, bias_output, gain_two, shift_two, bias_expand, bias_reduce]
        return jnp.concatenate([row.reshape(-1, D) for row in rows])

    owned, lines = [None] * LAYERS, [None] * LAYERS
    for layer in reversed(range(LAYERS if fused else 0, LAYERS)):
        vec, whole = vecs[layer], wholes[layer]
        x, normed1, heads, lse, attended, hidden, normed2, upper, active = saved[layer]
        dyb, dub, dh, dhb, *rest = ff_back_call(plan, me, grad, upper, hidden, vec, whole)
        sent, bias_grad, vec2 = rest[:GROUP], rest[GROUP], rest[GROUP + 1]
        *sent, sums = attend_back_call(me, heads, trade(sent, n_dp), lse)
        mixed, grad, vec1 = qkv_back_call(plan, me, trade(sent, n_dp), dh, x, vec, whole)
        own = (normed1, attended, normed2, active, mixed, dhb, dub, dyb)
        buffer = weight_call(plan, me, own, [send_core(x, n_dp) for x in own])
        lines[layer] = lines_of(vec1[0], vec1[1], sums, vec2[3], vec2[1], vec2[2], bias_grad, vec2[0])
        owned[layer] = plan.scatter(buffer)
    if fused:
        layer_output, grad, *kept, bias_grad, vec2, sums = plan.middle(value, out_cotangent, vecs[1], whole1)
        buffer = weight_call(plan, me, kept[:8], kept[8:])
        vectors1 = (bias_grad, vec2, sums)
        owned[1], grad, dyb, dub, dhb, mixed, bias_grad, vec2, sums, *other = plan.backward_first(
            me, buffer, first, grad, vec0, whole0
        )
        _, normed1, _, _, attended, _, normed2, _, active = first
        own = (normed1, attended, normed2, active, mixed, dhb, dub, dyb)
        owned[0], vec_sums = plan.scatter_first(own, other, (bias_grad, vec2, sums), vectors1)
        share = plan.line // LANES
        vec_owned = [vec_sums[4 * layer : 4 * layer + share].reshape(-1) for layer in range(LAYERS)]
    else:
        vec_owned = [plan.scatter_vectors(line) for line in lines]
    input_grad = swap(grad.astype(BF), n_dp).astype(F32)

    done = adam_call(plan, me, owned, params, param_moment, param_square)
    vector_grad = jnp.stack(vec_owned)
    vector_step = adam_parts(vector_grad, vector_moment, vector_square, vectors, 0.0)
    return (
        layer_output,
        input_grad,
        done[0],
        vector_grad,
        done[1],
        vector_step[0],
        done[2],
        vector_step[1],
        done[3],
        vector_step[2],
    )


def solution(mesh):
    tokens = P(("dp", "ctx"), None)
    slabs = P(None, "ctx", "dp", None)
    lines = P(None, ("dp", "ctx"))
    return jax.shard_map(
        functools.partial(per_device, mesh.shape["dp"]),
        mesh=mesh,
        in_specs=(tokens, tokens, slabs, lines, slabs, lines, slabs, lines),
        out_specs=(tokens, tokens, slabs, lines, slabs, lines, slabs, lines, slabs, lines),
        check_vma=False,
    )
```
